32 devices in a mesh: dp: 8 (over y, x, core), mp: 4 (over z).
Axes of the slice: x: 2, y: 2, z: 4, core: 2. Of those that a mesh axis runs over, the one named last changes fastest.
Arguments:
- tokens: bfloat16 [32, 577, 768], P(('dp', 'mp')), may hold values from -6 to 6
- lengths: int32 [32], P('dp'), may hold values from 257 to 577, as said below
- attention_norm_gain: float32 [768], replicated, may hold values from 0.5 to 1.5
- feedforward_norm_gain: float32 [768], replicated, may hold values from 0.5 to 1.5
- w_query: bfloat16 [768, 768], P(None, 'mp'), may hold values from -0.21875 to 0.21875
- w_key: bfloat16 [768, 768], P(None, 'mp'), may hold values from -0.21875 to 0.21875
- w_value: bfloat16 [768, 768], P(None, 'mp'), may hold values from -0.21875 to 0.21875
- w_out: bfloat16 [768, 768], P('mp'), may hold values from -1.75 to 1.75
- w_gate: bfloat16 [768, 2048], P(None, 'mp'), may hold values from -0.21875 to 0.21875
- w_up: bfloat16 [768, 2048], P(None, 'mp'), may hold values from -0.21875 to 0.21875
- w_down: bfloat16 [2048, 768], P('mp'), may hold values from -0.125 to 0.125
- cotangent: bfloat16 [32, 577, 768], P(('dp', 'mp')), may hold values from -6 to 6
Outputs:
- block_out: float32 [32, 577, 768], P(('dp', 'mp'))
- input_grad: float32 [32, 577, 768], P(('dp', 'mp'))
- grad_gain_attn: float32 [768], replicated
- grad_gain_mlp: float32 [768], replicated
- grad_query: float32 [768, 768], P(None, 'mp')
- grad_key: float32 [768, 768], P(None, 'mp')
- grad_value: float32 [768, 768], P(None, 'mp')
- grad_out: float32 [768, 768], P('mp')
- grad_gate: float32 [768, 2048], P(None, 'mp')
- grad_up: float32 [768, 2048], P(None, 'mp')
- grad_down: float32 [2048, 768], P('mp')
The draws below stay inside these ranges and needn't reach their ends.
Inputs may be any that keep to these rules, and one draw needn't show every extreme that they name: `lengths`: each item's length is 257 or 577; both occur in every draw.
All inputs are finite; a program needn't handle non-finite values.
Results may differ from the reference program's by a relative error of at most 0.015.
Values may be sent and summed in bfloat16 or wider, within the bound.
A program may use at most 128 MiB of HBM per device.

```python
import jax
import jax.numpy as jnp
from jax import lax

D = 768
HEADS = 12
HEAD = 64
FF = 2048
SEQ = 577
SHORT = 257
ITEMS = 32


def draw_lengths(key, part):
    key = jax.random.fold_in(key, 7)
    picked = jax.random.randint(key, (ITEMS,), 0, 2)
    picked = picked.at[0].set(1).at[1].set(0)
    return (SHORT + (SEQ - SHORT) * picked).astype(jnp.int32)


def level_of(key, shape, cuts, least, largest):
    factor_of, own = 1.0, jax.random.fold_in(key, 6)
    for axis_at, parts in cuts:
        steps = jnp.exp(jax.random.uniform(jax.random.fold_in(own, axis_at), (parts,), jnp.float32, least / len(cuts), largest / len(cuts)))
        factor_of = factor_of * jnp.repeat(steps, shape[axis_at] // parts).reshape([-1 if axis == axis_at else 1 for axis in range(len(shape))])
    return factor_of


def gaussian(rng, shape, spread, most, shards=(), dtype=jnp.bfloat16):
    result = jax.random.normal(rng, shape, jnp.float32) * spread
    if len(shards) > 0:
        result = level_of(rng, shape, shards, -0.22, 0.18) * result
    return jnp.clip(result, min=-most, max=most).astype(dtype)


def setup_inputs(seed: int = 0) -> dict:
    arg_keys = jax.random.split(jax.random.key(seed), 13)
    return {
        "tokens": gaussian(arg_keys[0], (ITEMS, SEQ, D), 1.0, 6.0, ((0, 32),)),
        "lengths": draw_lengths(jax.random.fold_in(arg_keys[12], 71), 0),
        "attention_norm_gain": jnp.clip(1.0 + 0.1 * jax.random.normal(arg_keys[2], (D,), jnp.float32), 0.5, 1.5),
        "feedforward_norm_gain": jnp.clip(1.0 + 0.1 * jax.random.normal(arg_keys[3], (D,), jnp.float32), 0.5, 1.5),
        "w_query": gaussian(arg_keys[4], (D, D), D ** -0.5, 0.21875, ((1, 4),)),
        "w_key": gaussian(arg_keys[5], (D, D), D ** -0.5, 0.21875, ((1, 4),)),
        "w_value": gaussian(arg_keys[6], (D, D), D ** -0.5, 0.21875, ((1, 4),)),
        "w_out": gaussian(arg_keys[7], (D, D), (max(D // 64, 1)) ** -0.5, 1.75, ((0, 4),)),
        "w_gate": gaussian(arg_keys[8], (D, FF), D ** -0.5, 0.21875, ((1, 4),)),
        "w_up": gaussian(arg_keys[9], (D, FF), D ** -0.5, 0.21875, ((1, 4),)),
        "w_down": gaussian(arg_keys[10], (FF, D), FF ** -0.5, 0.125, ((0, 4),)),
        "cotangent": gaussian(arg_keys[11], (ITEMS, SEQ, D), 1.0, 6.0, ((0, 32),)),
    }


@jax.custom_vjp
def low(v):
    return lax.optimization_barrier(v.astype(jnp.bfloat16)).astype(jnp.float32)

@jax.custom_vjp
def low_back(v):
    return v

def low_keep(v):
    return (low(v), None)

def low_pass(kept, grad):
    return (grad,)

def back_keep(v):
    return (v, None)

def back_low(kept, grad):
    return (low(grad),)
low.defvjp(low_keep, low_pass)
low_back.defvjp(back_keep, back_low)
EPS = 1e-05
NEG = -1e+30

def matmul(left, right):
    return jnp.dot(left, right, precision=lax.Precision.HIGHEST)

def normalize(values, gain):
    scale = lax.rsqrt(lax.optimization_barrier(jnp.mean(values * values, axis=-1, keepdims=True)) + EPS)
    return values * scale * gain

def tables():
    position = jnp.arange(SEQ).astype(jnp.float32)
    index = jnp.arange(HEAD // 2).astype(jnp.float32)
    freq = 10000.0 ** (-2.0 * index / HEAD)
    angle = position[:, None] * freq[None, :]
    angle = jnp.concatenate([angle, angle], axis=-1)
    return (jnp.cos(angle), jnp.sin(angle))

def rotate(values, cosine, sine):
    half = values.shape[-1] // 2
    turned = jnp.concatenate([-values[..., half:], values[..., :half]], axis=-1)
    return values * cosine[:, None, :] + turned * sine[:, None, :]

def layer(full_input_rows, gain_a, gain_m, wq, wk, wv, wo, wg, wu, wd, length):
    cosine, sine = tables()
    normed1 = low(normalize(full_input_rows, gain_a))
    query = low(rotate(low_back(matmul(normed1, wq)).reshape(SEQ, HEADS, HEAD), cosine, sine))
    keys = low(rotate(low_back(matmul(normed1, wk)).reshape(SEQ, HEADS, HEAD), cosine, sine))
    values = low(low_back(matmul(normed1, wv))).reshape(SEQ, HEADS, HEAD)
    position = jnp.arange(SEQ)
    allowed = (position[None, :] <= position[:, None]) & (position[None, :] < length)
    scores = jnp.einsum('qhd,khd->hqk', query, keys, precision=lax.Precision.HIGHEST)
    scores = low_back(scores * (1.0 / jnp.sqrt(jnp.float32(HEAD))))
    scores = jnp.where(allowed[None], scores, NEG)
    probs = jax.nn.softmax(scores, axis=-1)
    context = jnp.einsum('hqk,khd->qhd', low(probs), values, precision=lax.Precision.HIGHEST)
    context = low(low_back(context)).reshape(SEQ, D)
    first_hidden_state = full_input_rows + low_back(matmul(context, wo))
    normed2 = low(normalize(first_hidden_state, gain_m))
    gate = low_back(matmul(normed2, wg))
    upper = low_back(matmul(normed2, wu))
    hidden = low(jax.nn.silu(gate) * upper)
    return first_hidden_state + low_back(matmul(hidden, wd))

def reference(tokens, lengths, attention_norm_gain, feedforward_norm_gain, w_query, w_key, w_value, w_out, w_gate, w_up, w_down, cotangent):
    weights = tuple((w.astype(jnp.float32) for w in (w_query, w_key, w_value, w_out, w_gate, w_up, w_down)))
    gains = (attention_norm_gain.astype(jnp.float32), feedforward_norm_gain.astype(jnp.float32))
    position = jnp.arange(SEQ)

    def one_item(totals, item):
        xitem, length, grad_item = item

        def forward(full_input_rows, gain_a, gain_m, wq, wk, wv, wo, wg, wu, wd):
            return layer(full_input_rows, gain_a, gain_m, wq, wk, wv, wo, wg, wu, wd, length)
        output, pull = jax.vjp(forward, xitem.astype(jnp.float32), *gains, *weights)
        valid = (position < length).astype(jnp.float32)
        grads = pull(grad_item.astype(jnp.float32) * valid[:, None])
        totals = tuple((a + b for a, b in zip(totals, grads[1:])))
        return (totals, (output, grads[0]))
    start = tuple((jnp.zeros_like(g) for g in gains)) + tuple((jnp.zeros_like(w) for w in weights))
    totals, (block_out, input_grad) = lax.scan(one_item, start, (tokens, lengths, cotangent))
    return (block_out, input_grad, totals[0], totals[1], totals[2], totals[3], totals[4], totals[5], totals[6], totals[7], totals[8])
```

```python
import functools

import jax
import jax.numpy as jnp
import numpy as np
from jax import lax
from jax.experimental import pallas as pl
from jax.experimental.pallas import tpu as pltpu
from jax.sharding import PartitionSpec as P

HEAD = 64
EPS = 1e-05
NEG = -1e30
MESH = pl.DeviceIdType.MESH
f32, bf16 = jnp.float32, jnp.bfloat16
HEADS = ((0, 0), (0, 1), (1, 0))
RING = 4


def nn(left, right):
    return lax.dot_general(left, right, (((1,), (0,)), ((), ())), preferred_element_type=f32)


def nt(left, right):
    return lax.dot_general(left, right, (((1,), (1,)), ((), ())), preferred_element_type=f32)


def iota(shape, axis):
    return lax.broadcasted_iota(jnp.int32, shape, axis)


def turned(w, low):
    return jnp.where(low, -pltpu.roll(w, 96, 1), pltpu.roll(w, 32, 1))


def order_table(count):
    return [sorted(range(count), key=lambda s: (abs(s - z), s)) for z in range(count)]


def pick(table, row, column):
    found = 0
    for r, values in enumerate(table):
        for c, value in enumerate(values):
            found = found + jnp.where((row == r) & (column == c), value, 0)
    return found


def kernel(
    mp,
    rows,
    len_ref,
    x_ref,
    dy_ref,
    g1_ref,
    g2_ref,
    cos_ref,
    sin_ref,
    own_ref,
    out_ref,
    dx_ref,
    gains_ref,
    fin_ref,
    w,
    n1,
    n1t,
    n2,
    n2t,
    dyb,
    dyt,
    q,
    k,
    v,
    kt,
    vt,
    ctx,
    ctxt,
    lse,
    mask,
    hb,
    dgu,
    dn,
    dk_sum,
    dv_sum,
    dqt,
    dpack,
    gbuf,
    r1,
    r2,
    r3,
    zb,
    r4,
    total,
    gain_in,
    own_sem,
    z_send,
    z_recv,
    g_send,
    g_recv,
    s_send,
    s_recv,
    z4_send,
    z4_recv,
    fin_sem,
    f_send,
    f_recv,
    gain_send,
    gain_recv,
    credit,
):
    T = rows
    seq, width = x_ref.shape[1], x_ref.shape[2]
    half, quarter, eighth = width // 2, width // 4, width // 8
    blocks = [(a, min(a + 256, T)) for a in range(0, T, 256)]
    dp_at, z = lax.axis_index("dp"), lax.axis_index("mp")
    core, bit1, bit2 = dp_at % 2, (dp_at // 2) % 2, (dp_at // 4) % 2
    partner = dp_at + 1 - 2 * core
    flip1, flip2 = dp_at + 2 - 4 * bit1, dp_at + 4 - 8 * bit2
    near = jnp.where(core == 0, flip1, flip2)
    far = jnp.where(core == 0, flip2, flip1)
    near_bit = jnp.where(core == 0, bit1, bit2)
    far_bit = jnp.where(core == 0, bit2, bit1)
    hops = (near, far, partner)
    table = order_table(mp)

    def at(start, size):
        return pl.ds(pl.multiple_of(start, 16), size)

    half_at = core * half
    quarter_at = half_at + far_bit * quarter
    eighth_at = quarter_at + near_bit * eighth
    gather_rows = (at(eighth_at, eighth), at(quarter_at, quarter), at(half_at, half))
    give_rows = (
        at((1 - core) * half, half),
        at(half_at + (1 - far_bit) * quarter, quarter),
        at(quarter_at + (1 - near_bit) * eighth, eighth),
    )
    keep_rows = (at(half_at, half), at(quarter_at, quarter), at(eighth_at, eighth))

    def remote(src, dst, send, recv, dp_to, z_to):
        return pltpu.make_async_remote_copy(
            src_ref=src,
            dst_ref=dst,
            send_sem=send,
            recv_sem=recv,
            device_id={"dp": dp_to, "mp": z_to},
            device_id_type=MESH,
        )


    def along(kind, shard, side):
        part = w.at[kind, shard, gather_rows[0]]
        return remote(part, part, z_send.at[kind, shard, side], z_recv.at[kind, shard], dp_at, z + 1 - 2 * side)

    def across(kind, shard, stage):
        part = w.at[kind, shard, gather_rows[stage]]
        return remote(part, part, g_send.at[kind, shard, stage], g_recv.at[kind, shard, stage], hops[stage], z)

    def send_own(kind):
        for side, there in ((0, z + 1 < mp), (1, z > 0)):
            pl.when(there)(lambda side=side: along(kind, z, side).start())

    def each_side(distance, act):
        for side, shard, there, onward in (
            (0, z - distance, z - distance >= 0, z + 1 < mp),
            (1, z + distance, z + distance < mp, z > 0),
        ):
            pl.when(there)(functools.partial(act, shard, side, onward))

    def arrive(kind, distance, stage):
        def act(shard, side, onward):
            if stage == 0:
                along(kind, shard, side).wait_recv()
                pl.when(onward)(lambda: along(kind, shard, side).start())
            else:
                across(kind, shard, stage - 1).wait_recv()
            if stage < 3:
                across(kind, shard, stage).start()

        each_side(distance, act)

    def unit_of(n):
        later = n - (mp - 1)
        first = n < mp - 1
        return jnp.where(first, 0, 1 + later % 2), jnp.where(first, n + 1, 1 + later // 2)

    units_in = 3 * (mp - 1)

    def tick(n):
        for stage in range(4):
            m = n - stage

            @pl.when((m >= 0) & (m < units_in))
            def _(m=m, stage=stage):
                kind, distance = unit_of(jnp.maximum(m, 0))
                arrive(kind, distance, stage)

    def gather_drain():
        def each(i, carry):
            kind, shard = i // mp, i % mp
            for side, there in ((0, (shard <= z) & (z + 1 < mp)), (1, (shard >= z) & (z > 0))):
                pl.when(there)(lambda side=side: along(kind, shard, side).wait_send())

            @pl.when(shard != z)
            def _():
                for stage in range(3):
                    across(kind, shard, stage).wait_send()

            return carry

        lax.fori_loop(0, 3 * mp, each, 0)


    units_f = 2 * mp
    units = 3 * mp
    landing = (r1, r2, r3)
    hops_back = (partner, far, near)

    def shard_of(u):
        late = u - units_f
        return jnp.where(u < units_f, pick(table, z, u // 2), (z + 1 + late) % mp)

    def kind_of(u):
        return jnp.where(u < units_f, 1 + u % 2, 0)

    def give(u, stage):
        slot = u % RING
        return remote(
            gbuf.at[slot, give_rows[stage]],
            landing[stage].at[slot],
            s_send.at[slot, stage],
            s_recv.at[slot, stage],
            hops_back[stage],
            z,
        )

    def start_give(u, stage):
        pl.when(u >= RING)(lambda: pl.semaphore_wait(credit.at[stage], 1))
        give(u, stage).start()

    def take(u, stage):
        slot = u % RING
        copy = give(u, stage)
        copy.wait_recv()
        copy.wait_send()
        sums = gbuf[slot, keep_rows[stage], :].astype(f32) + landing[stage][slot].astype(f32)
        sums = sums.astype(bf16)

        @pl.when(u + RING < units)
        def _():
            pl.semaphore_signal(
                credit.at[stage], inc=1, device_id={"dp": hops_back[stage], "mp": z}, device_id_type=MESH
            )

        if stage < 2:
            gbuf[slot, keep_rows[stage], :] = sums
            start_give(u, stage + 1)
            return
        shard, kind = shard_of(u), kind_of(u)

        @pl.when(shard == z)
        def _():
            r4[kind, z] = sums

        @pl.when(shard != z)
        def _():
            zb[u] = sums
            home(u).start()

    def home(u):
        kind = kind_of(u)
        return remote(zb.at[u], r4.at[kind, z], z4_send.at[u], z4_recv.at[kind, z], dp_at, shard_of(u))

    def home_drain():
        def each(u, carry):
            pl.when(shard_of(u) != z)(lambda: home(u).wait_send())
            return carry

        lax.fori_loop(0, units, each, 0)


    def fin_own(kind):
        return pltpu.make_async_copy(total.at[kind], fin_ref.at[kind, gather_rows[0]], fin_sem.at[kind])

    def fin_across(kind, stage):
        src = total.at[kind] if stage == 0 else fin_ref.at[kind, gather_rows[stage]]
        return remote(
            src,
            fin_ref.at[kind, gather_rows[stage]],
            f_send.at[kind, stage],
            f_recv.at[kind, stage],
            hops[stage],
            z,
        )

    def finish(kind, stage):
        if stage == 0:
            for src in range(mp):

                @pl.when(z != src)
                def _(src=src):
                    remote(
                        zb.at[0], r4.at[kind, src], z4_send.at[0], z4_recv.at[kind, src], dp_at, src
                    ).wait_recv()

            sums = r4[kind, 0].astype(f32)
            for src in range(1, mp):
                sums = sums + r4[kind, src].astype(f32)
            total[kind] = sums.astype(bf16)
            fin_own(kind).start()
        else:
            if stage == 1:
                fin_own(kind).wait()
            fin_across(kind, stage - 1).wait_recv()
        if stage < 3:
            fin_across(kind, stage).start()

    def finish_drain(kind):
        for stage in range(3):
            fin_across(kind, stage).wait_send()


    gain_hops = ((partner, z), (far, z), (near, z))

    def gain_copy(stage):
        to = gain_hops[stage]
        return remote(
            gain_in.at[0], gain_in.at[1 + stage], gain_send.at[stage], gain_recv.at[stage], *to
        )

    def gain_along(i, to):
        return remote(
            gain_in.at[0], gain_in.at[3 + i], gain_send.at[2 + i], gain_recv.at[2 + i], dp_at, to
        )

    def gain_step(stage):
        if stage > 0:
            copy = gain_copy(stage - 1)
            copy.wait()
            gain_in[0] = gain_in[0] + gain_in[stage]
        if stage < 3:
            gain_copy(stage).start()
        else:
            for i in range(1, mp):
                gain_along(i, (z + i) % mp).start()

    def gain_end():
        for i in range(1, mp):
            gain_along(i, (z + i) % mp).wait()
        sums = gain_in[0]
        for i in range(1, mp):
            sums = sums + gain_in[3 + i]
        gains_ref[...] = sums


    barrier = pltpu.get_barrier_semaphore()
    for to in (partner, near, far):
        pl.semaphore_signal(barrier, inc=1, device_id={"dp": to, "mp": z}, device_id_type=MESH)
    for i in range(1, mp):
        pl.semaphore_signal(
            barrier, inc=1, device_id={"dp": dp_at, "mp": (z + i) % mp}, device_id_type=MESH
        )
    own = [pltpu.make_async_copy(own_ref.at[kind], w.at[kind, z], own_sem.at[kind]) for kind in range(3)]
    for copy in own:
        copy.start()

    lane = iota((T, 128), 1)
    lower = lane < 64
    low = (lane % 64) < 32
    length = len_ref[z]
    full = seq // 16 * 16

    def padded(ref):
        tail = jnp.broadcast_to(ref[0, full:seq, :].astype(f32), (T - full, width))
        tail = jnp.where(iota((T - full, width), 0) < seq - full, tail, 0.0).astype(bf16)
        return jnp.concatenate([ref[0, 0:full, :], tail], axis=0)

    def scale_of(rows_in):
        return lax.rsqrt(jnp.mean(rows_in * rows_in, axis=-1, keepdims=True) + EPS)

    for copy in own:
        copy.wait()
    pl.semaphore_wait(barrier, 3 + mp - 1)
    send_own(0)

    x = padded(x_ref).astype(f32)
    normed = (x * scale_of(x) * g1_ref[...]).astype(bf16)
    n1[...] = normed
    n1t[...] = normed.T
    out_ref[...] = x
    live = jnp.where(iota((T, width), 0) < length, padded(dy_ref).astype(f32), 0.0).astype(bf16)
    dyb[...] = live
    dyt[...] = live.T
    key_at, query_at = iota((T, T), 0), iota((T, T), 1)
    mask[...] = jnp.where((key_at <= query_at) & (key_at < length), 0.0, NEG)
    ctxt[...] = jnp.zeros_like(ctxt)
    dqt[...] = jnp.zeros_like(dqt)


    def attention(step, carry):
        def point(i):
            tick(jnp.where(step == 0, i, 3 + step if i == 0 else -1))

        cos, sin = cos_ref[...], sin_ref[...]
        s = pick(table, z, step)
        wa = w.at[0, s]
        qkv = nn(n1[...], wa[:, 0:640])
        point(0)

        @pl.when(step == 0)
        def _():
            send_own(1)

        first = qkv[:, 0:128]
        mixed = qkv[:, 128:256]
        keys = qkv[:, 256:384]
        first = (first * cos + turned(first, low) * sin) * 0.125
        mixed = mixed * cos + turned(mixed, low) * sin
        keys = keys * cos + turned(keys, low) * sin
        q[s, 0] = first.astype(bf16)
        q[s, 1] = jnp.where(lower, mixed * 0.125, 0.0).astype(bf16)
        k[s, 0] = keys.astype(bf16)
        k[s, 1] = jnp.where(lower, pltpu.roll(mixed, 64, 1), 0.0).astype(bf16)
        v[s, 0] = qkv[:, 384:512].astype(bf16)
        v[s, 1] = jnp.where(lower, qkv[:, 512:640], 0.0).astype(bf16)
        for tile in range(2):
            kt[s, tile] = k[s, tile].T
            vt[tile] = v[s, tile].T
        for h, (tile, side) in enumerate(HEADS):
            qh = q[s, tile]
            if tile == 0:
                qh = jnp.where(lower if side == 0 else ~lower, qh, jnp.zeros_like(qh))
            for a, b in blocks:
                scores = nt(k[s, tile, 0:b, :], qh[a:b]) + mask[0:b, a:b]
                peak = jnp.max(scores, axis=0, keepdims=True)
                e = jnp.exp(scores - peak)
                norm = jnp.sum(e, axis=0, keepdims=True)
                c = nn(vt[tile, 64 * side : 64 * side + 64, 0:b], e.astype(bf16))
                ctxt[64 * h : 64 * h + 64, a:b] = c * (1.0 / norm)
                lse[s, h : h + 1, a:b] = peak + jnp.log(norm)
            point(1 + h)
        last = ctxt[128:256, :].T
        ctx[s, :, 0:128] = jnp.where(lower, 0.0, pltpu.roll(last, 64, 1)).astype(bf16)
        ctx[s, :, 128:256] = ctxt[0:128, :].T.astype(bf16)
        out_ref[...] += nt(ctx[s], wa[:, 512:768])

        @pl.when(step == 0)
        def _():
            send_own(2)

        return carry

    lax.fori_loop(0, mp, attention, 0)

    x1 = out_ref[...]
    dx_ref[...] = x1
    normed = (x1 * scale_of(x1) * g2_ref[...]).astype(bf16)
    n2[...] = normed
    n2t[...] = normed.T
    dn[...] = jnp.zeros_like(dn)


    def feed(step, carry):
        s = pick(table, z, step)
        w0, w1 = w.at[1, s], w.at[2, s]
        u0, u1 = 2 * step, 2 * step + 1
        gu = nn(n2[...], w0[...])
        rest = nn(n2[...], w1[:, 0:256])
        dh = nn(dyb[...], w1[:, 256:768])
        for i in range(2):
            cols = slice(256 * i, 256 * i + 256)
            gate = gu[:, cols]
            up = gu[:, 512:768] if i == 0 else rest
            dhid = dh[:, cols]
            sigma = 1.0 / (1.0 + jnp.exp(-gate))
            active = gate * sigma
            hb[:, cols] = (active * up).astype(bf16)
            dgu[:, cols] = (dhid * up * sigma * (1.0 + gate * (1.0 - sigma))).astype(bf16)
            dgu[:, 512 + 256 * i : 768 + 256 * i] = (dhid * active).astype(bf16)
        tick(7 + 2 * step)
        gbuf[u0 % RING] = nn(n2t[...], dgu[:, 0:768]).astype(bf16)
        start_give(u0, 0)

        @pl.when(step >= 1)
        def _():
            take(u0 - 1, 0)
            take(u0 - 2, 1)

        pl.when(step >= 2)(lambda: take(u0 - 3, 2))
        out_ref[...] += nt(hb[...], w1[:, 256:768])
        tick(jnp.where(step < 2, 8 + 2 * step, -1))
        gbuf[u1 % RING, :, 0:256] = nn(n2t[...], dgu[:, 768:1024]).astype(bf16)
        gbuf[u1 % RING, :, 256:768] = nn(dyt[...], hb[...]).astype(bf16)
        start_give(u1, 0)
        take(u0, 0)

        @pl.when(step >= 1)
        def _():
            take(u0 - 1, 1)
            take(u0 - 2, 2)

        dn[...] += nt(dgu[:, 0:768], w0[...]) + nt(dgu[:, 768:1024], w1[:, 0:256])
        return carry

    lax.fori_loop(0, mp, feed, 0)

    x1 = dx_ref[...]
    scale = scale_of(x1)
    hat = x1 * scale
    d2 = dn[...]
    gain_in[0] = jnp.zeros_like(gain_in[0])
    gain_in[0, 1:2, :] = jnp.sum(d2 * hat, axis=0, keepdims=True)
    e = d2 * g2_ref[...]
    dx1 = dyb[...].astype(f32) + scale * (e - hat * jnp.mean(e * hat, axis=-1, keepdims=True))
    dx_ref[...] = dx1
    lowered = dx1.astype(bf16)
    n2[...] = lowered
    n2t[...] = lowered.T
    dn[...] = jnp.zeros_like(dn)


    def back(step, carry):
        u = units_f + step
        slot = u % RING
        cos, sin = cos_ref[...], sin_ref[...]
        s = shard_of(u)
        wa = w.at[0, s]
        dc = nn(n2[...], wa[:, 512:768])
        dc2 = jnp.where(lower, pltpu.roll(dc[:, 0:128], 64, 1), 0.0).astype(bf16)
        dc01 = dc[:, 128:256].astype(bf16)
        for tile in range(2):
            dk_sum[tile] = jnp.zeros((T, 128), f32)
            dv_sum[tile] = jnp.zeros((T, 128), f32)
        for h, (tile, side) in enumerate(HEADS):
            qh = q[s, tile]
            dch = dc01 if tile == 0 else dc2
            if tile == 0:
                here = lower if side == 0 else ~lower
                qh = jnp.where(here, qh, jnp.zeros_like(qh))
                dch = jnp.where(here, dch, jnp.zeros_like(dch))
            for a, b in blocks:
                scores = nt(k[s, tile, 0:b, :], qh[a:b]) + mask[0:b, a:b]
                p = jnp.exp(scores - lse[s, h : h + 1, a:b])
                dprob = nt(v[s, tile, 0:b, :], dch[a:b])
                delta = jnp.sum(p * dprob, axis=0, keepdims=True)
                ds = (p * (dprob - delta)).astype(bf16)
                dv_sum[tile, 0:b, :] += nn(p.astype(bf16), dch[a:b])
                dk_sum[tile, 0:b, :] += nn(ds, qh[a:b])
                dqt[64 * h : 64 * h + 64, a:b] = nn(kt[s, tile, 64 * side : 64 * side + 64, 0:b], ds)
            take(u - 1, h)
            if h < 2:

                @pl.when(step == 0)
                def _(h=h):
                    take(u - 2, h + 1)
                    if h == 0:
                        take(u - 3, 2)

        dq01 = dqt[0:128, :].T * 0.125
        dq2 = dqt[128:256, :].T * 0.125
        dq01 = dq01 * cos - turned(dq01, low) * sin
        dq2 = dq2 * cos - turned(dq2, low) * sin
        dk01 = dk_sum[0] * cos - turned(dk_sum[0], low) * sin
        dk2 = dk_sum[1] * cos - turned(dk_sum[1], low) * sin
        dpack[:, 0:128] = dq01.astype(bf16)
        dpack[:, 128:256] = jnp.where(lower, dq2, pltpu.roll(dk2, 64, 1)).astype(bf16)
        dpack[:, 256:384] = dk01.astype(bf16)
        dpack[:, 384:512] = dv_sum[0].astype(bf16)
        dpack[:, 512:640] = jnp.where(lower, dv_sum[1], 0.0).astype(bf16)
        gbuf[slot, :, 0:512] = nn(n1t[...], dpack[:, 0:512]).astype(bf16)
        gbuf[slot, :, 512:640] = (
            nn(n1t[...], dpack[:, 512:640]) + nn(n2t[...], ctx[s, :, 0:128])
        ).astype(bf16)
        gbuf[slot, :, 640:768] = nn(n2t[...], ctx[s, :, 128:256]).astype(bf16)
        start_give(u, 0)
        for stage in range(3):

            @pl.when(step == 1 + stage)
            def _(stage=stage):
                finish(1, stage)
                finish(2, stage)

        dn[...] += nt(dpack[...], wa[:, 0:640])
        return carry

    lax.fori_loop(0, mp, back, 0)

    take(units - 1, 0)
    x = padded(x_ref).astype(f32)
    scale = scale_of(x)
    hat = x * scale
    d1 = dn[...]
    gain_in[0, 0:1, :] = jnp.sum(d1 * hat, axis=0, keepdims=True)
    gain_step(0)
    e = d1 * g1_ref[...]
    dx_ref[...] += scale * (e - hat * jnp.mean(e * hat, axis=-1, keepdims=True))
    take(units - 1, 1)
    gain_step(1)
    take(units - 1, 2)
    finish(0, 0)
    gain_step(2)
    finish(0, 1)
    gain_step(3)
    finish(0, 2)
    gain_end()
    finish(1, 3)
    finish(2, 3)
    gather_drain()
    home_drain()
    finish(0, 3)
    for kind in range(3):
        finish_drain(kind)


def rotary(rows):
    position = np.arange(rows).astype(np.float32)
    index = np.arange(HEAD // 2).astype(np.float32)
    freq = (np.float32(10000.0) ** (np.float32(-2.0) * index / np.float32(HEAD))).astype(np.float32)
    angle = position[:, None] * freq[None, :]
    angle = np.concatenate([angle] * 4, axis=-1)
    return np.cos(angle).astype(np.float32), np.sin(angle).astype(np.float32)


def layer(mp, lengths, tokens, cotangent, gain1, gain2, own):
    _, seq, width = tokens.shape
    T = (seq + 15) // 16 * 16
    cosine, sine = rotary(T)
    vmem, anywhere = pl.BlockSpec(memory_space=pltpu.VMEM), pl.BlockSpec(memory_space=pl.ANY)
    V, DMA = pltpu.VMEM, pltpu.SemaphoreType.DMA
    half, quarter, eighth = width // 2, width // 4, width // 8
    scratch = [
        V((3, mp, width, width), bf16),
        V((T, width), bf16),
        V((width, T), bf16),
        V((T, width), bf16),
        V((width, T), bf16),
        V((T, width), bf16),
        V((width, T), bf16),
        V((mp, 2, T, 128), bf16),
        V((mp, 2, T, 128), bf16),
        V((mp, 2, T, 128), bf16),
        V((mp, 2, 128, T), bf16),
        V((2, 128, T), bf16),
        V((mp, T, 256), bf16),
        V((256, T), f32),
        V((mp, 8, T), f32),
        V((T, T), f32),
        V((T, 512), bf16),
        V((T, 1024), bf16),
        V((T, width), f32),
        V((2, T, 128), f32),
        V((2, T, 128), f32),
        V((256, T), f32),
        V((T, 640), bf16),
        V((RING, width, width), bf16),
        V((RING, half, width), bf16),
        V((RING, quarter, width), bf16),
        V((RING, eighth, width), bf16),
        V((3 * mp, eighth, width), bf16),
        V((3, mp, eighth, width), bf16),
        V((3, eighth, width), bf16),
        V((3 + mp, 8, width), f32),
        DMA((3,)),
        DMA((3, mp, 2)),
        DMA((3, mp)),
        DMA((3, mp, 3)),
        DMA((3, mp, 3)),
        DMA((RING, 3)),
        DMA((RING, 3)),
        DMA((3 * mp,)),
        DMA((3, mp)),
        DMA((3,)),
        DMA((3, 3)),
        DMA((3, 3)),
        DMA((2 + mp,)),
        DMA((2 + mp,)),
        pltpu.SemaphoreType.REGULAR((3,)),
    ]
    return pl.pallas_call(
        functools.partial(kernel, mp, T),
        out_shape=(
            jax.ShapeDtypeStruct((T, width), f32),
            jax.ShapeDtypeStruct((T, width), f32),
            jax.ShapeDtypeStruct((8, width), f32),
            jax.ShapeDtypeStruct((3, width, width), bf16),
        ),
        in_specs=[pl.BlockSpec(memory_space=pltpu.SMEM)] + [vmem] * 6 + [anywhere],
        out_specs=[vmem, vmem, vmem, anywhere],
        scratch_shapes=scratch,
        compiler_params=pltpu.CompilerParams(
            collective_id=0, has_side_effects=True, vmem_limit_bytes=63 * 2**20
        ),
    )(lengths, tokens, cotangent, gain1[None], gain2[None], jnp.asarray(cosine), jnp.asarray(sine), own)


def per_device(mp, dp, tokens, lengths, gain1, gain2, wq, wk, wv, wo, wg, wu, wd, cotangent):
    seq = tokens.shape[1]
    wot, wdt = wo.T, wd.T
    own = jnp.stack(
        [
            jnp.concatenate(
                [wq, wk[:, 128:], wk[:, :128], wv, wot[:, 128:], wot[:, :128]], axis=1
            ),
            jnp.concatenate([wg, wu[:, :256]], axis=1),
            jnp.concatenate([wu[:, 256:], wdt], axis=1),
        ]
    )
    out, dx, gains, fin = layer(mp, lengths, tokens, cotangent, gain1, gain2, own)
    fin, gains = fin.astype(f32), gains[0:2]
    if dp > 8:
        groups = [[8 * i + j for i in range(dp // 8)] for j in range(8)]
        fin, gains = lax.psum((fin, gains), "dp", axis_index_groups=groups)
    a, f0, f1 = fin[0], fin[1], fin[2]
    return (
        out[None, :seq],
        dx[None, :seq],
        gains[0],
        gains[1],
        a[:, 0:192],
        jnp.concatenate([a[:, 256:384], a[:, 192:256]], axis=1),
        a[:, 384:576],
        jnp.concatenate([a[:, 640:768], a[:, 576:640]], axis=1).T,
        f0[:, 0:512],
        jnp.concatenate([f0[:, 512:], f1[:, :256]], axis=1),
        f1[:, 256:].T,
    )


def solution(mesh):
    rows, cols, items = P("mp", None), P(None, "mp"), P(("dp", "mp"), None, None)
    return jax.shard_map(
        functools.partial(per_device, mesh.shape["mp"], mesh.shape["dp"]),
        mesh=mesh,
        in_specs=(items, P("dp"), P(), P(), cols, cols, cols, rows, cols, cols, rows, items),
        out_specs=(items, items, P(), P(), cols, cols, cols, rows, cols, cols, rows),
        check_vma=False,
    )
```

```python
import functools

import jax
import jax.numpy as jnp
import numpy as np
from jax import lax
from jax.experimental import pallas as pl
from jax.experimental.pallas import tpu as pltpu
from jax.sharding import PartitionSpec as P

HEAD = 64
EPS = 1e-05
NEG = -1e30
MESH = pl.DeviceIdType.MESH
f32, bf16 = jnp.float32, jnp.bfloat16
HEADS = ((0, 1), (1, 0), (1, 1))
SLOTS = (3, 6, 8, 12)
STEPS = (3, 3, 2)

PLAN = {
    ("P", 0, 0): (("s", 0),),
    ("A", 0, 4): (("s", 1),),
    ("A", 1, 0): (("z", 0, 1), ("g", 0, 1, 0), ("z", 1, 1), ("g", 1, 1, 0), ("g", 0, 1, 1), ("z", 0, 2), ("g", 0, 2, 0), ("g", 1, 1, 1), ("z", 1, 2), ("g", 1, 2, 0), ("g", 0, 1, 2), ("g", 0, 2, 1), ("z", 0, 3), ("g", 0, 3, 0), ("g", 0, 1, 3), ("s", 2),),
    ("A", 1, 3): (("g", 1, 1, 2), ("z", 1, 3), ("g", 1, 3, 0),),
    ("A", 1, 4): (("g", 1, 2, 1),),
    ("A", 2, 0): (("g", 1, 1, 3), ("g", 0, 2, 2), ("g", 0, 3, 1), ("z", 2, 1), ("g", 0, 2, 3), ("g", 2, 1, 0),),
    ("A", 2, 1): (("g", 1, 3, 1),),
    ("A", 3, 0): (("g", 1, 2, 2), ("g", 0, 3, 2), ("g", 1, 2, 3), ("z", 2, 2), ("g", 2, 2, 0), ("g", 0, 3, 3),),
    ("A", 3, 1): (("g", 2, 1, 1),),
    ("A", 3, 4): (("g", 2, 1, 2),),
    ("F", 0, 0): (("g", 1, 3, 2),),
    ("F", 0, 1): (("g", 2, 2, 1), ("g", 1, 3, 3),),
    ("F", 0, 2): (("z", 2, 3), ("g", 2, 3, 0),),
    ("F", 0, 3): (("g", 2, 2, 2),),
    ("F", 0, 4): (("t", 0, 0),),
    ("F", 1, 1): (("t", 1, 0),),
    ("F", 1, 2): (("g", 2, 3, 1),),
    ("F", 1, 4): (("t", 2, 0),),
    ("F", 2, 0): (("g", 2, 3, 2), ("t", 0, 1),),
    ("F", 2, 1): (("t", 3, 0),),
    ("F", 2, 2): (("t", 1, 1),),
    ("F", 2, 4): (("t", 4, 0), ("t", 2, 1),),
    ("F", 3, 1): (("t", 0, 2), ("t", 5, 0),),
    ("F", 3, 3): (("t", 3, 1),),
    ("F", 3, 4): (("t", 1, 2), ("t", 6, 0),),
    ("B", 0, 0): (("t", 7, 0), ("t", 4, 1),),
    ("B", 0, 1): (("t", 2, 2),),
    ("B", 0, 3): (("t", 5, 1),),
    ("B", 0, 5): (("t", 3, 2),),
    ("B", 0, 7): (("t", 6, 1),),
    ("B", 1, 1): (("t", 8, 0), ("t", 7, 1),),
    ("B", 1, 2): (("t", 4, 2),),
    ("B", 1, 3): (("t", 5, 2),),
    ("B", 1, 4): (("t", 6, 2),),
    ("B", 1, 7): (("t", 8, 1),),
    ("B", 1, 8): (("t", 7, 2),),
    ("B", 2, 1): (("t", 9, 0),),
    ("B", 2, 2): (("t", 8, 2),),
    ("B", 2, 6): (("t", 9, 1),),
    ("B", 3, 1): (("t", 10, 0),),
    ("B", 3, 2): (("t", 9, 2),),
    ("B", 3, 3): (("f", 1, 0),),
    ("B", 3, 6): (("t", 10, 1),),
    ("B", 3, 8): (("f", 1, 1), ("f", 2, 0),),
    ("E", 0, 1): (("n", 0),),
    ("E", 0, 2): (("t", 11, 0), ("t", 10, 2), ("n", 1),),
    ("E", 0, 6): (("f", 1, 2),),
    ("E", 0, 7): (("f", 2, 1), ("f", 1, 3), ("t", 11, 1), ("n", 2), ("f", 2, 2), ("t", 11, 2), ("f", 0, 0), ("n", 3), ("f", 2, 3), ("n", 4), ("f", 0, 1), ("f", 0, 2), ("f", 0, 3),),
}


def nn(left, right):
    return lax.dot_general(left, right, (((1,), (0,)), ((), ())), preferred_element_type=f32)


def nt(left, right):
    return lax.dot_general(left, right, (((1,), (1,)), ((), ())), preferred_element_type=f32)


def iota(shape, axis):
    return lax.broadcasted_iota(jnp.int32, shape, axis)


def turned(w, low):
    return jnp.where(low, -pltpu.roll(w, 96, 1), pltpu.roll(w, 32, 1))


def swap(w):
    return pltpu.roll(w, 64, 1)


def order_table(count):
    def key(z):
        return lambda s: (abs(s - z), s if z < count / 2 else -s)

    return [sorted(range(count), key=key(z)) for z in range(count)]


def pick(table, row, column):
    found = 0
    for r, values in enumerate(table):
        for c, value in enumerate(values):
            found = found + jnp.where((row == r) & (column == c), value, 0)
    return found


def kernel(
    mp,
    T,
    len_ref,
    x_ref,
    dy_ref,
    g1_ref,
    g2_ref,
    cos_ref,
    sin_ref,
    wq_ref,
    wk_ref,
    wv_ref,
    wo_ref,
    wg_ref,
    wu_ref,
    wd_ref,
    out_ref,
    dx_ref,
    ga_ref,
    gm_ref,
    fin_ref,
    w,
    n1,
    n2,
    n2t,
    dyb,
    q,
    k,
    v,
    kt,
    vt,
    ctx,
    heads_t,
    lse,
    mask,
    hb,
    turned_rows,
    made,
    acc,
    res,
    dn,
    dk_sum,
    dv_sum,
    gbuf,
    r1,
    r2,
    r3,
    r4,
    total,
    gain_in,
    staged,
    own_sem,
    z_send,
    z_recv,
    g_send,
    g_recv,
    s_send,
    s_recv,
    h_send,
    h_recv,
    fin_sem,
    f_send,
    f_recv,
    gain_send,
    gain_recv,
    out_sem,
    credit,
):
    seq, width = x_ref.shape[1], x_ref.shape[2]
    half, quarter, eighth = width // 2, width // 4, width // 8
    blocks = [(a, min(a + 256, T)) for a in range(0, T, 256)]
    dp_at, z = lax.axis_index("dp"), lax.axis_index("mp")
    core, bit1, bit2 = dp_at % 2, (dp_at // 2) % 2, (dp_at // 4) % 2
    partner = dp_at + 1 - 2 * core
    flip1, flip2 = dp_at + 2 - 4 * bit1, dp_at + 4 - 8 * bit2
    near = jnp.where(core == 0, flip1, flip2)
    far = jnp.where(core == 0, flip2, flip1)
    near_bit = jnp.where(core == 0, bit1, bit2)
    far_bit = jnp.where(core == 0, bit2, bit1)
    table = order_table(mp)
    units_f, units = 2 * mp, 3 * mp

    def at(start, size):
        return pl.ds(pl.multiple_of(start, 16), size)

    half_at = core * half
    quarter_at = half_at + far_bit * quarter
    eighth_at = quarter_at + near_bit * eighth
    half_rows, quarter_rows, eighth_rows = at(half_at, half), at(quarter_at, quarter), at(eighth_at, eighth)
    colour_rows = at(half_at + (bit1 + bit2) % 2 * quarter, quarter)
    widening = ((near, eighth_rows), (far, quarter_rows), (partner, half_rows))
    brief = ((near, colour_rows), (partner, half_rows))

    def remote(src, dst, send, recv, dp_to, z_to):
        return pltpu.make_async_remote_copy(
            src_ref=src,
            dst_ref=dst,
            send_sem=send,
            recv_sem=recv,
            device_id={"dp": dp_to, "mp": z_to},
            device_id_type=MESH,
        )


    def hops(kind):
        return widening if STEPS[kind] == 3 else brief

    def along(kind, shard, side):
        part = w.at[kind, shard, hops(kind)[0][1]]
        return remote(part, part, z_send.at[kind, shard, side], z_recv.at[kind, shard], dp_at, z + 1 - 2 * side)

    def across(kind, shard, stage):
        to, rows = hops(kind)[stage]
        part = w.at[kind, shard, rows]
        return remote(part, part, g_send.at[kind, shard, stage], g_recv.at[kind, shard, stage], to, z)

    def send_own(kind):
        for side, there in ((0, z + 1 < mp), (1, z > 0)):
            pl.when(there)(lambda side=side: along(kind, z, side).start())

    def pass_on(kind, distance):
        for side, shard, there, onward in (
            (0, z - distance, z - distance >= 0, z + 1 < mp),
            (1, z + distance, z + distance < mp, z > 0),
        ):

            @pl.when(there)
            def _(shard=shard, side=side, onward=onward):
                along(kind, shard, side).wait_recv()
                pl.when(onward)(lambda: along(kind, shard, side).start())

    def gather(kind, j, stage):
        shard = pick(table, z, j)
        if stage > 0:
            across(kind, shard, stage - 1).wait_recv()
        if stage < STEPS[kind]:
            across(kind, shard, stage).start()

    def gather_drain():
        for kind in range(3):

            def each(shard, carry, kind=kind):
                for side, there in ((0, (shard <= z) & (z + 1 < mp)), (1, (shard >= z) & (z > 0))):
                    pl.when(there)(lambda side=side: along(kind, shard, side).wait_send())

                @pl.when(shard != z)
                def _():
                    for stage in range(STEPS[kind]):
                        across(kind, shard, stage).wait_send()

                return carry

            lax.fori_loop(0, mp, each, 0)


    def shard_of(u):
        if isinstance(u, int) and u >= units_f or not isinstance(u, int):
            return (z + 1 + (u - units_f)) % mp
        return pick(table, z, u // 2)

    def kind_of(u):
        return 1 + u % 2 if u < units_f else 0

    narrowing = ((partner, 1 - core, half), (far, 1 - far_bit, quarter), (near, 1 - near_bit, eighth))
    kept = (half_at, far_bit * quarter, near_bit * eighth)
    stores = (gbuf, r1, r2, r3)

    def give(u, stage):
        to, which, size = narrowing[stage]
        return remote(
            stores[stage].at[u % SLOTS[stage], at(which * size, size)],
            stores[stage + 1].at[u % SLOTS[stage + 1]],
            s_send.at[u, stage],
            s_recv.at[u, stage],
            to,
            z,
        )

    def start_give(u, stage):
        late = u >= SLOTS[stage + 1]
        if isinstance(late, bool):
            if late:
                pl.semaphore_wait(credit.at[stage], 1)
        else:
            pl.when(late)(lambda: pl.semaphore_wait(credit.at[stage], 1))
        give(u, stage).start()

    def release(u, stage):
        if u + SLOTS[stage + 1] < units:
            pl.semaphore_signal(
                credit.at[stage], inc=1, device_id={"dp": narrowing[stage][0], "mp": z}, device_id_type=MESH
            )

    def take(u, stage):
        copy = give(u, stage)
        copy.wait_recv()
        copy.wait_send()
        mine, came = stores[stage], stores[stage + 1]
        here, there = u % SLOTS[stage], u % SLOTS[stage + 1]

        def add(i, carry):
            to = at(i * eighth, eighth)
            sums = mine[here, at(kept[stage] + i * eighth, eighth), :].astype(f32) + came[there, to, :].astype(f32)
            came[there, to, :] = sums.astype(bf16)
            return carry

        lax.fori_loop(0, (4, 2, 1)[stage], add, 0)
        if stage > 0:
            release(u, stage - 1)
        if stage < 2:
            start_give(u, stage + 1)
            return
        shard = shard_of(u)

        @pl.when(shard == z)
        def _():
            r4[kind_of(u), z] = r3[there]

        pl.when(shard != z)(lambda: home(u).start())

    def home(u):
        kind = kind_of(u)
        return remote(r3.at[u], r4.at[kind, z], h_send.at[u], h_recv.at[kind, z], dp_at, shard_of(u))

    def home_drain():
        for u in range(units):
            pl.when(shard_of(u) != z)(lambda u=u: home(u).wait_send())


    def fin_own(kind):
        return pltpu.make_async_copy(total.at[kind], fin_ref.at[kind, eighth_rows], fin_sem.at[kind])

    def fin_across(kind, stage):
        to, rows = widening[stage]
        src = total.at[kind] if stage == 0 else fin_ref.at[kind, rows]
        return remote(src, fin_ref.at[kind, rows], f_send.at[kind, stage], f_recv.at[kind, stage], to, z)

    def finish(kind, stage):
        if stage == 0:
            for src in range(mp):

                @pl.when(z != src)
                def _(src=src):
                    remote(r3.at[0], r4.at[kind, src], h_send.at[0], h_recv.at[kind, src], dp_at, src).wait_recv()

            sums = r4[kind, 0].astype(f32)
            for src in range(1, mp):
                sums = sums + r4[kind, src].astype(f32)
            total[kind] = sums.astype(bf16)
            fin_own(kind).start()
        else:
            if stage == 1:
                fin_own(kind).wait()
            fin_across(kind, stage - 1).wait_recv()
        if stage < 3:
            fin_across(kind, stage).start()

    def finish_drain(kind):
        for stage in range(3):
            fin_across(kind, stage).wait_send()


    def gain_copy(stage):
        to = (partner, far, near)[stage]
        return remote(gain_in.at[0], gain_in.at[1 + stage], gain_send.at[stage], gain_recv.at[stage], to, z)

    def gain_along(i):
        return remote(
            gain_in.at[0], gain_in.at[3 + i], gain_send.at[2 + i], gain_recv.at[2 + i], dp_at, (z + i) % mp
        )

    def gain_step(stage):
        if stage in (1, 2, 3):
            gain_copy(stage - 1).wait()
            gain_in[0] = gain_in[0] + gain_in[stage]
        if stage < 3:
            gain_copy(stage).start()
        elif stage == 3:
            for i in range(1, mp):
                gain_along(i).start()
        else:
            for i in range(1, mp):
                gain_along(i).wait()
            sums = gain_in[0]
            for i in range(1, mp):
                sums = sums + gain_in[3 + i]
            ga_ref[...] = sums[0]
            gm_ref[...] = sums[1]

    move = {"s": send_own, "z": pass_on, "g": gather, "t": take, "f": finish, "n": gain_step}

    def place(part, step, i):
        for at_step in range(mp):
            acts = PLAN.get((part, at_step, i))
            if acts is None:
                continue

            def run(acts=acts):
                for name, *what in acts:
                    move[name](*what)

            if isinstance(step, int):
                if step == at_step:
                    run()
            else:
                pl.when(step == at_step)(run)


    barrier = pltpu.get_barrier_semaphore()
    for to in (partner, near, far):
        pl.semaphore_signal(barrier, inc=1, device_id={"dp": to, "mp": z}, device_id_type=MESH)
    for i in range(1, mp):
        pl.semaphore_signal(
            barrier, inc=1, device_id={"dp": dp_at, "mp": (z + i) % mp}, device_id_type=MESH
        )
    cols = wq_ref.shape[0]
    hidden = wg_ref.shape[1]
    first = width - hidden
    rest = hidden - first
    pieces = [(ref, w.at[0, z, pl.ds(i * cols, cols)]) for i, ref in enumerate((wq_ref, wk_ref, wv_ref, wo_ref))]
    pieces += [
        (wg_ref, w.at[1, z, :, pl.ds(0, hidden)]),
        (wu_ref.at[:, pl.ds(0, first)], w.at[1, z, :, pl.ds(hidden, first)]),
        (wd_ref, w.at[2, z, pl.ds(0, hidden)]),
    ]
    stripes = width // rest
    tall = width // stripes
    pieces += [
        (wu_ref.at[pl.ds(j * tall, tall), pl.ds(first, rest)], w.at[2, z, pl.ds(hidden, tall), pl.ds(j * rest, rest)])
        for j in range(stripes)
    ]
    own = [pltpu.make_async_copy(src, dst, own_sem.at[i]) for i, (src, dst) in enumerate(pieces)]
    for copy in own:
        copy.start()

    lane = iota((T, 128), 1)
    lower = lane < 64
    low = (lane % 64) < 32
    length = len_ref[z]
    full = seq // 16 * 16

    def padded(ref):
        tail = jnp.broadcast_to(ref[0, full:seq, :].astype(f32), (T - full, width))
        tail = jnp.where(iota((T - full, width), 0) < seq - full, tail, 0.0).astype(bf16)
        return jnp.concatenate([ref[0, 0:full, :], tail], axis=0)

    def scale_of(rows_in):
        return lax.rsqrt(jnp.mean(rows_in * rows_in, axis=-1, keepdims=True) + EPS)

    def gain(ref):
        return ref[...].reshape(1, width)

    x = padded(x_ref).astype(f32)
    n1[...] = (x * scale_of(x) * gain(g1_ref)).astype(bf16)
    for copy in own:
        copy.wait()
    pl.semaphore_wait(barrier, 3 + mp - 1)
    place("P", 0, 0)

    acc[...] = x
    dyb[...] = jnp.where(iota((T, width), 0) < length, padded(dy_ref).astype(f32), 0.0).astype(bf16)
    key_at, query_at = iota((T, T), 0), iota((T, T), 1)
    mask[...] = jnp.where((key_at <= query_at) & (key_at < length), 0.0, NEG)
    heads_t[...] = jnp.zeros_like(heads_t)


    def attention(step, carry):
        place("A", step, 0)
        cos, sin = cos_ref[...], sin_ref[...]
        s = pick(table, z, step)
        wa = w.at[0, s]
        qkv = nt(n1[...], wa[0:640, :])
        tiles = [qkv[:, 128 * i : 128 * i + 128] for i in range(5)]
        t0, t1, t2 = (t * cos + turned(t, low) * sin for t in tiles[0:3])
        t0, t1s = swap(t0), swap(t1)
        q[s, 0] = jnp.where(lower, 0.0, t0 * 0.125).astype(bf16)
        q[s, 1] = (jnp.where(lower, t0, t1s) * 0.125).astype(bf16)
        k[s, 0] = jnp.where(lower, 0.0, t1).astype(bf16)
        k[s, 1] = t2.astype(bf16)
        t3, t4 = swap(tiles[3]), swap(tiles[4])
        v[s, 0] = jnp.where(lower, 0.0, t3).astype(bf16)
        v[s, 1] = jnp.where(lower, t3, t4).astype(bf16)
        place("A", step, 1)
        for tile in range(2):
            kt[s, tile] = k[s, tile].T
            vt[tile] = v[s, tile].T
        for h, (tile, side) in enumerate(HEADS):
            qh = q[s, tile]
            if tile == 1:
                qh = jnp.where(lower if side == 0 else ~lower, qh, jnp.zeros_like(qh))
            at_row = 128 * tile + 64 * side
            for a, b in blocks:
                scores = nt(k[s, tile, 0:b, :], qh[a:b]) + mask[0:b, a:b]
                peak = jnp.max(scores, axis=0, keepdims=True)
                e = jnp.exp(scores - peak)
                norm = jnp.sum(e, axis=0, keepdims=True)
                c = nn(vt[tile, 64 * side : 64 * side + 64, 0:b], e.astype(bf16))
                heads_t[at_row : at_row + 64, a:b] = c * (1.0 / norm)
                lse[s, h : h + 1, a:b] = peak + jnp.log(norm)
            place("A", step, 2 + h)
        c = heads_t[...].astype(bf16)
        ctx[s] = c
        acc[...] += nn(c.T, wa[512:768, :])
        return carry

    lax.fori_loop(0, mp, attention, 0)

    x1 = acc[...]
    res[...] = x1
    normed = (x1 * scale_of(x1) * gain(g2_ref)).astype(bf16)
    n2[...] = normed
    n2t[...] = normed.T
    dn[...] = jnp.zeros_like(dn)


    def feed(step, carry):
        place("F", step, 0)
        s = pick(table, z, step)
        w1, w2 = w.at[1, s], w.at[2, s]
        u0, u1 = 2 * step, 2 * step + 1
        gu = nn(n2[...], w1[...])
        late = nn(n2[:, 0:256], w2[512:768, 0:256])
        for j in range(1, 3):
            late = late + nn(n2[:, 256 * j : 256 * j + 256], w2[512:768, 256 * j : 256 * j + 256])
        dh = nt(dyb[...], w2[0:512, :])
        for i in range(2):
            part = slice(256 * i, 256 * i + 256)
            gate = gu[:, part]
            up = gu[:, 512:768] if i == 0 else late
            dhid = dh[:, part]
            sigma = 1.0 / (1.0 + jnp.exp(-gate))
            active = gate * sigma
            hb[step, :, part] = (active * up).astype(bf16)
            made[:, part] = (dhid * up * sigma * (1.0 + gate * (1.0 - sigma))).astype(bf16)
            made[:, 512 + 256 * i : 768 + 256 * i] = (dhid * active).astype(bf16)
        place("F", step, 1)
        gbuf[u0 % SLOTS[0]] = nn(n2t[...], made[:, 0:768]).astype(bf16)
        start_give(u0, 0)
        place("F", step, 2)
        turned_rows[0:512, :] = hb[step].T
        dn[...] += nt(made[:, 0:768], w1[...])
        place("F", step, 3)
        gbuf[u1 % SLOTS[0], 0:512, :] = nn(turned_rows[0:512, :], dyb[...]).astype(bf16)
        for j in range(3):
            part = slice(256 * j, 256 * j + 256)
            gbuf[u1 % SLOTS[0], 512:768, part] = nn(n2t[part, :], made[:, 768:1024]).astype(bf16)
        start_give(u1, 0)
        place("F", step, 4)
        for j in range(3):
            part = slice(256 * j, 256 * j + 256)
            dn[:, part] += nt(made[:, 768:1024], w2[512:768, part])
        return carry

    lax.fori_loop(0, mp, feed, 0)

    place("M", 0, 0)
    x1 = res[...]
    scale = scale_of(x1)
    hat = x1 * scale
    d2 = dn[...]
    gain_in[0] = jnp.zeros_like(gain_in[0])
    gain_in[0, 1:2, :] = jnp.sum(d2 * hat, axis=0, keepdims=True)
    e = d2 * gain(g2_ref)
    dx1 = dyb[...].astype(f32) + scale * (e - hat * jnp.mean(e * hat, axis=-1, keepdims=True))
    res[...] = dx1
    n2[...] = dx1.astype(bf16)
    dn[...] = jnp.zeros_like(dn)
    heads_t[192:256, :] = jnp.zeros((64, T), f32)


    def back(step, carry):
        u = units_f + step
        slot = u % SLOTS[0]
        place("B", step, 0)
        cos, sin = cos_ref[...], sin_ref[...]
        s = shard_of(u)
        wa = w.at[0, s]
        dc = nt(n2[...], wa[512:768, :])
        dc = [jnp.where(lower, 0.0, dc[:, 0:128]).astype(bf16), dc[:, 128:256].astype(bf16)]
        for tile in range(2):
            dk_sum[tile] = jnp.zeros((T, 128), f32)
            dv_sum[tile] = jnp.zeros((T, 128), f32)
        for h, (tile, side) in enumerate(HEADS):
            qh, dch = q[s, tile], dc[tile]
            if tile == 1:
                here = lower if side == 0 else ~lower
                qh = jnp.where(here, qh, jnp.zeros_like(qh))
                dch = jnp.where(here, dch, jnp.zeros_like(dch))
            for i, (a, b) in enumerate(blocks):
                scores = nt(k[s, tile, 0:b, :], qh[a:b]) + mask[0:b, a:b]
                p = jnp.exp(scores - lse[s, h : h + 1, a:b])
                dprob = nt(v[s, tile, 0:b, :], dch[a:b])
                delta = jnp.sum(p * dprob, axis=0, keepdims=True)
                ds = (p * (dprob - delta)).astype(bf16)
                dv_sum[tile, 0:b, :] += nn(p.astype(bf16), dch[a:b])
                dk_sum[tile, 0:b, :] += nn(ds, qh[a:b])
                heads_t[64 * h : 64 * h + 64, a:b] = nn(kt[s, tile, 64 * side : 64 * side + 64, 0:b], ds)
                if i == 1:
                    place("B", step, 1 + 2 * h)
            place("B", step, 2 + 2 * h)

        def unturned(t):
            return t * cos - turned(t, low) * sin

        dq01 = unturned(heads_t[0:128, :].T * 0.125)
        dq2 = unturned(heads_t[128:256, :].T * 0.125)
        made[:, 0:128] = dq01.astype(bf16)
        made[:, 128:256] = jnp.where(lower, dq2, unturned(dk_sum[0])).astype(bf16)
        made[:, 256:384] = unturned(dk_sum[1]).astype(bf16)
        dv0, dv1 = swap(dv_sum[0]), swap(dv_sum[1])
        made[:, 384:512] = jnp.where(lower, dv0, dv1).astype(bf16)
        made[:, 512:640] = jnp.where(lower, dv1, 0.0).astype(bf16)
        turned_rows[...] = made[:, 0:640].T
        place("B", step, 7)
        gbuf[slot, 0:576, :] = nn(turned_rows[0:576, :], n1[...]).astype(bf16)
        gbuf[slot, 576:768, :] = nn(ctx[s, 64:256, :], n2[...]).astype(bf16)
        start_give(u, 0)
        place("B", step, 8)
        dn[...] += nn(made[:, 0:640], wa[0:640, :])
        return carry

    lax.fori_loop(0, mp, back, 0)


    place("E", 0, 0)
    x = padded(x_ref).astype(f32)
    scale = scale_of(x)
    hat = x * scale
    d1 = dn[...]
    gain_in[0, 0:1, :] = jnp.sum(d1 * hat, axis=0, keepdims=True)
    place("E", 0, 1)
    e = d1 * gain(g1_ref)
    dx = res[...] + scale * (e - hat * jnp.mean(e * hat, axis=-1, keepdims=True))
    staged[:, 0, :] = dx[0:seq]
    out_dx = pltpu.make_async_copy(staged, dx_ref, out_sem.at[0])
    out_dx.start()
    place("E", 0, 2)
    for j in range(mp):
        acc[...] += nn(hb[j], w[2, pick(table, z, j), 0:512, :])
        place("E", 0, 3 + j)
    out_dx.wait()
    staged[:, 0, :] = acc[0:seq, :]
    out_y = pltpu.make_async_copy(staged, out_ref, out_sem.at[1])
    out_y.start()
    place("E", 0, 3 + mp)
    gather_drain()
    home_drain()
    for kind in range(3):
        finish_drain(kind)
    out_y.wait()


def rotary(rows):
    position = np.arange(rows).astype(np.float32)
    index = np.arange(HEAD // 2).astype(np.float32)
    freq = (np.float32(10000.0) ** (np.float32(-2.0) * index / np.float32(HEAD))).astype(np.float32)
    angle = position[:, None] * freq[None, :]
    angle = np.concatenate([angle] * 4, axis=-1)
    return np.cos(angle).astype(np.float32), np.sin(angle).astype(np.float32)


def layer(mp, lengths, tokens, cotangent, gain1, gain2, weights):
    _, seq, width = tokens.shape
    T = (seq + 15) // 16 * 16
    cosine, sine = rotary(T)
    vmem, anywhere = pl.BlockSpec(memory_space=pltpu.VMEM), pl.BlockSpec(memory_space=pl.ANY)
    V, DMA = pltpu.VMEM, pltpu.SemaphoreType.DMA
    half, quarter, eighth = width // 2, width // 4, width // 8
    scratch = [
        V((3, mp, width, width), bf16),
        V((T, width), bf16),
        V((T, width), bf16),
        V((width, T), bf16),
        V((T, width), bf16),
        V((mp, 2, T, 128), bf16),
        V((mp, 2, T, 128), bf16),
        V((mp, 2, T, 128), bf16),
        V((mp, 2, 128, T), bf16),
        V((2, 128, T), bf16),
        V((mp, 256, T), bf16),
        V((256, T), f32),
        V((mp, 8, T), f32),
        V((T, T), f32),
        V((mp, T, 512), bf16),
        V((640, T), bf16),
        V((T, 1024), bf16),
        V((T, width), f32),
        V((T, width), f32),
        V((T, width), f32),
        V((2, T, 128), f32),
        V((2, T, 128), f32),
        V((SLOTS[0], width, width), bf16),
        V((SLOTS[1], half, width), bf16),
        V((SLOTS[2], quarter, width), bf16),
        V((SLOTS[3], eighth, width), bf16),
        V((3, mp, eighth, width), bf16),
        V((3, eighth, width), bf16),
        V((3 + mp, 8, width), f32),
        V((seq, 1, width), f32),
        DMA((10,)),
        DMA((3, mp, 2)),
        DMA((3, mp)),
        DMA((3, mp, 3)),
        DMA((3, mp, 3)),
        DMA((3 * mp, 3)),
        DMA((3 * mp, 3)),
        DMA((3 * mp,)),
        DMA((3, mp)),
        DMA((3,)),
        DMA((3, 3)),
        DMA((3, 3)),
        DMA((2 + mp,)),
        DMA((2 + mp,)),
        DMA((2,)),
        pltpu.SemaphoreType.REGULAR((3,)),
    ]
    return pl.pallas_call(
        functools.partial(kernel, mp, T),
        out_shape=(
            jax.ShapeDtypeStruct((seq, 1, width), f32),
            jax.ShapeDtypeStruct((seq, 1, width), f32),
            jax.ShapeDtypeStruct((width,), f32),
            jax.ShapeDtypeStruct((width,), f32),
            jax.ShapeDtypeStruct((3, width, width), bf16),
        ),
        in_specs=[pl.BlockSpec(memory_space=pltpu.SMEM)] + [vmem] * 6 + [anywhere] * 7,
        out_specs=[anywhere, anywhere, vmem, vmem, anywhere],
        scratch_shapes=scratch,
        compiler_params=pltpu.CompilerParams(
            collective_id=0, has_side_effects=True, vmem_limit_bytes=63 * 2**20
        ),
    )(lengths, tokens, cotangent, gain1, gain2, jnp.asarray(cosine), jnp.asarray(sine), *weights)


def per_device(mp, dp, tokens, lengths, gain1, gain2, wq, wk, wv, wo, wg, wu, wd, cotangent):
    _, seq, width = tokens.shape
    weights = (wq.T, wk.T, wv.T, wo, wg, wu, wd)
    out, dx, gain_a, gain_m, fin = layer(mp, lengths, tokens, cotangent, gain1, gain2, weights)
    if dp > 8:
        groups = [[8 * i + j for i in range(dp // 8)] for j in range(8)]
        fin, gain_a, gain_m = lax.psum((fin.astype(f32), gain_a, gain_m), "dp", axis_index_groups=groups)
    fin = fin.astype(f32)
    cols, hidden = wq.shape[1], wg.shape[1]
    first = width - hidden
    rest = hidden - first
    late = fin[2, hidden:]
    late = jnp.concatenate([late[:, rest * j : rest * j + rest] for j in range(width // rest)], axis=0)
    return (
        out.reshape(1, seq, width),
        dx.reshape(1, seq, width),
        gain_a,
        gain_m,
        fin[0, 0:cols].T,
        fin[0, cols : 2 * cols].T,
        fin[0, 2 * cols : 3 * cols].T,
        fin[0, 3 * cols :],
        fin[1, :, 0:hidden],
        jnp.concatenate([fin[1, :, hidden:], late], axis=1),
        fin[2, 0:hidden],
    )


def solution(mesh):
    rows, cols, items = P("mp", None), P(None, "mp"), P(("dp", "mp"), None, None)
    return jax.shard_map(
        functools.partial(per_device, mesh.shape["mp"], mesh.shape["dp"]),
        mesh=mesh,
        in_specs=(items, P("dp"), P(), P(), cols, cols, cols, rows, cols, cols, rows, items),
        out_specs=(items, items, P(), P(), cols, cols, cols, rows, cols, cols, rows),
        check_vma=False,
    )
```

```python
import functools

import jax
import jax.numpy as jnp
import numpy as np
from jax import lax
from jax.experimental import pallas as pl
from jax.experimental.pallas import tpu as pltpu
from jax.sharding import PartitionSpec as P

HEAD = 64
EPS = 1e-05
NEG = -1e30
MESH = pl.DeviceIdType.MESH
f32, bf16 = jnp.float32, jnp.bfloat16
HEADS = ((0, 1), (1, 0), (1, 1))
SLOTS = (3, 6, 8, 12)
STEPS = (3, 3, 3)

PLAN = {
    ("P", 0, 0): (("s", 0),),
    ("A", 0, 2): (("s", 1),),
    ("A", 1, 0): (("g", 0, 1, 0), ("g", 0, 1, 1), ("g", 0, 2, 0), ("g", 0, 2, 1), ("g", 0, 1, 2), ("g", 0, 3, 0), ("g", 1, 1, 0), ("g", 0, 1, 3),),
    ("A", 1, 3): (("s", 2),),
    ("A", 2, 0): (("g", 1, 2, 0), ("g", 0, 3, 1), ("g", 1, 1, 1), ("g", 0, 2, 2), ("g", 0, 2, 3),),
    ("A", 2, 4): (("g", 1, 2, 1), ("g", 1, 3, 0), ("g", 2, 1, 0),),
    ("A", 3, 0): (("g", 2, 2, 0), ("g", 0, 3, 2), ("g", 1, 1, 2), ("g", 0, 3, 3),),
    ("A", 3, 1): (("g", 1, 1, 3),),
    ("A", 3, 3): (("g", 1, 3, 1), ("g", 2, 1, 1),),
    ("A", 3, 4): (("g", 2, 3, 0),),
    ("F", 0, 0): (("g", 1, 2, 2), ("g", 2, 2, 1),),
    ("F", 0, 2): (("g", 1, 2, 3),),
    ("F", 1, 0): (("t", 0, 0), ("g", 2, 3, 1), ("t", 1, 0), ("g", 1, 3, 2), ("g", 2, 1, 2), ("g", 1, 3, 3), ("g", 2, 1, 3),),
    ("F", 1, 2): (("g", 2, 2, 2),),
    ("F", 2, 0): (("t", 2, 0), ("g", 2, 2, 3),),
    ("F", 2, 1): (("t", 3, 0), ("g", 2, 3, 2), ("t", 0, 1), ("t", 1, 1),),
    ("F", 2, 3): (("g", 2, 3, 3),),
    ("F", 3, 0): (("t", 4, 0),),
    ("F", 3, 1): (("t", 2, 1), ("t", 5, 0),),
    ("F", 3, 4): (("t", 0, 2), ("t", 1, 2), ("t", 6, 0),),
    ("B", 0, 0): (("t", 7, 0),),
    ("B", 0, 1): (("t", 3, 1),),
    ("B", 0, 2): (("t", 2, 2),),
    ("B", 0, 5): (("t", 4, 1),),
    ("B", 1, 1): (("t", 5, 1),),
    ("B", 1, 2): (("t", 3, 2), ("t", 8, 0), ("t", 6, 1),),
    ("B", 1, 3): (("t", 4, 2), ("t", 7, 1),),
    ("B", 1, 4): (("t", 5, 2),),
    ("B", 1, 8): (("t", 6, 2),),
    ("B", 2, 2): (("t", 7, 2), ("t", 8, 1), ("t", 9, 0),),
    ("B", 2, 8): (("t", 8, 2),),
    ("B", 3, 1): (("t", 9, 1), ("t", 10, 0),),
    ("B", 3, 6): (("t", 9, 2),),
    ("B", 3, 7): (("f", 1, 0),),
    ("E", 0, 0): (("t", 10, 1),),
    ("E", 0, 1): (("n", 0),),
    ("E", 0, 2): (("t", 11, 0), ("n", 1),),
    ("E", 0, 3): (("f", 1, 1),),
    ("E", 0, 4): (("f", 2, 0), ("t", 10, 2),),
    ("E", 0, 6): (("n", 2),),
    ("E", 0, 7): (("n", 3), ("f", 2, 1), ("t", 11, 1), ("f", 1, 2), ("n", 4), ("f", 1, 3), ("t", 11, 2), ("f", 0, 0), ("f", 2, 2), ("f", 2, 3), ("f", 0, 1), ("f", 0, 2), ("f", 0, 3),),
}


def nn(left, right):
    return lax.dot_general(left, right, (((1,), (0,)), ((), ())), preferred_element_type=f32)


def nt(left, right):
    return lax.dot_general(left, right, (((1,), (1,)), ((), ())), preferred_element_type=f32)


def iota(shape, axis):
    return lax.broadcasted_iota(jnp.int32, shape, axis)


def turned(w, low):
    return jnp.where(low, -pltpu.roll(w, 96, 1), pltpu.roll(w, 32, 1))


def swap(w):
    return pltpu.roll(w, 64, 1)


def order_table(count):
    return [sorted(range(count), key=lambda s: s ^ z) for z in range(count)]


def pick(table, row, column):
    found = 0
    for r, values in enumerate(table):
        for c, value in enumerate(values):
            found = found + jnp.where((row == r) & (column == c), value, 0)
    return found


def kernel(
    mp,
    T,
    len_ref,
    x_ref,
    dy_ref,
    g1_ref,
    g2_ref,
    cos_ref,
    sin_ref,
    wq_ref,
    wk_ref,
    wv_ref,
    wo_ref,
    wg_ref,
    wu_ref,
    wd_ref,
    out_ref,
    dx_ref,
    ga_ref,
    gm_ref,
    fin_ref,
    w,
    n1,
    n2,
    n2t,
    dyb,
    q,
    k,
    v,
    kt,
    vt,
    ctx,
    heads_t,
    lse,
    mask,
    hb,
    turned_rows,
    made,
    acc,
    res,
    dn,
    dk_sum,
    dv_sum,
    gbuf,
    r1,
    r2,
    r3,
    r4,
    total,
    gain_in,
    staged,
    own_sem,
    z_send,
    z_recv,
    g_send,
    g_recv,
    s_send,
    s_recv,
    h_send,
    h_recv,
    fin_sem,
    f_send,
    f_recv,
    gain_send,
    gain_recv,
    out_sem,
    credit,
):
    seq, width = x_ref.shape[1], x_ref.shape[2]
    half, quarter, eighth = width // 2, width // 4, width // 8
    blocks = [(a, min(a + 256, T)) for a in range(0, T, 256)]
    dp_at, z = lax.axis_index("dp"), lax.axis_index("mp")
    core, bit1, bit2 = dp_at % 2, (dp_at // 2) % 2, (dp_at // 4) % 2
    partner = dp_at + 1 - 2 * core
    flip1, flip2 = dp_at + 2 - 4 * bit1, dp_at + 4 - 8 * bit2
    near = jnp.where(core == 0, flip1, flip2)
    far = jnp.where(core == 0, flip2, flip1)
    near_bit = jnp.where(core == 0, bit1, bit2)
    far_bit = jnp.where(core == 0, bit2, bit1)
    table = order_table(mp)
    units_f, units = 2 * mp, 3 * mp

    def at(start, size):
        return pl.ds(pl.multiple_of(start, 16), size)

    half_at = core * half
    quarter_at = half_at + far_bit * quarter
    eighth_at = quarter_at + near_bit * eighth
    half_rows, quarter_rows, eighth_rows = at(half_at, half), at(quarter_at, quarter), at(eighth_at, eighth)
    colour_rows = at(half_at + (bit1 + bit2) % 2 * quarter, quarter)
    widening = ((near, eighth_rows), (far, quarter_rows), (partner, half_rows))
    brief = ((near, colour_rows), (partner, half_rows))

    def remote(src, dst, send, recv, dp_to, z_to):
        return pltpu.make_async_remote_copy(
            src_ref=src,
            dst_ref=dst,
            send_sem=send,
            recv_sem=recv,
            device_id={"dp": dp_to, "mp": z_to},
            device_id_type=MESH,
        )


    def hops(kind):
        return widening if STEPS[kind] == 3 else brief

    def along(kind, shard, to):
        part = w.at[kind, shard, hops(kind)[0][1]]
        return remote(part, part, z_send.at[kind, to], z_recv.at[kind, shard], dp_at, to)

    def across(kind, shard, stage):
        to, rows = hops(kind)[stage]
        part = w.at[kind, shard, rows]
        return remote(part, part, g_send.at[kind, shard, stage], g_recv.at[kind, shard, stage], to, z)

    def send_own(kind):
        for j in range(1, mp):
            along(kind, z, pick(table, z, j)).start()

    def gather(kind, j, stage):
        shard = pick(table, z, j)
        if stage == 0:
            along(kind, shard, shard).wait_recv()
        else:
            across(kind, shard, stage - 1).wait_recv()
        if stage < STEPS[kind]:
            across(kind, shard, stage).start()

    def gather_drain():
        for kind in range(3):
            for j in range(1, mp):
                shard = pick(table, z, j)
                along(kind, z, shard).wait_send()
                for stage in range(STEPS[kind]):
                    across(kind, shard, stage).wait_send()


    def shard_of(u):
        return pick(table, z, u // 2) if u < units_f else (z + 1 + u - units_f) % mp

    def kind_of(u):
        return 1 + u % 2 if u < units_f else 0

    narrowing = ((partner, 1 - core, half), (far, 1 - far_bit, quarter), (near, 1 - near_bit, eighth))
    kept = (half_at, far_bit * quarter, near_bit * eighth)
    stores = (gbuf, r1, r2, r3)

    def give(u, stage):
        to, which, size = narrowing[stage]
        return remote(
            stores[stage].at[u % SLOTS[stage], at(which * size, size)],
            stores[stage + 1].at[u % SLOTS[stage + 1]],
            s_send.at[u, stage],
            s_recv.at[u, stage],
            to,
            z,
        )

    def start_give(u, stage):
        if u >= SLOTS[stage + 1]:
            pl.semaphore_wait(credit.at[stage], 1)
        give(u, stage).start()

    def release(u, stage):
        if u + SLOTS[stage + 1] < units:
            pl.semaphore_signal(
                credit.at[stage], inc=1, device_id={"dp": narrowing[stage][0], "mp": z}, device_id_type=MESH
            )

    def take(u, stage):
        copy = give(u, stage)
        copy.wait_recv()
        copy.wait_send()
        mine, came = stores[stage], stores[stage + 1]
        here, there = u % SLOTS[stage], u % SLOTS[stage + 1]

        def add(i, carry):
            to = at(i * eighth, eighth)
            sums = mine[here, at(kept[stage] + i * eighth, eighth), :].astype(f32) + came[there, to, :].astype(f32)
            came[there, to, :] = sums.astype(bf16)
            return carry

        lax.fori_loop(0, (4, 2, 1)[stage], add, 0)
        if stage > 0:
            release(u, stage - 1)
        if stage < 2:
            start_give(u, stage + 1)
            return
        if u in (0, 1, units - 1):
            r4[kind_of(u), z] = r3[there]
        else:
            home(u).start()

    def home(u):
        kind = kind_of(u)
        return remote(r3.at[u], r4.at[kind, z], h_send.at[u], h_recv.at[kind, z], dp_at, shard_of(u))

    def home_drain():
        for u in range(2, units - 1):
            home(u).wait_send()


    def fin_own(kind):
        return pltpu.make_async_copy(total.at[kind], fin_ref.at[kind, eighth_rows], fin_sem.at[kind])

    def fin_across(kind, stage):
        to, rows = widening[stage]
        src = total.at[kind] if stage == 0 else fin_ref.at[kind, rows]
        return remote(src, fin_ref.at[kind, rows], f_send.at[kind, stage], f_recv.at[kind, stage], to, z)

    def finish(kind, stage):
        if stage == 0:
            for src in range(mp):

                @pl.when(z != src)
                def _(src=src):
                    remote(r3.at[0], r4.at[kind, src], h_send.at[0], h_recv.at[kind, src], dp_at, src).wait_recv()

            sums = r4[kind, 0].astype(f32)
            for src in range(1, mp):
                sums = sums + r4[kind, src].astype(f32)
            total[kind] = sums.astype(bf16)
            fin_own(kind).start()
        else:
            if stage == 1:
                fin_own(kind).wait()
            fin_across(kind, stage - 1).wait_recv()
        if stage < 3:
            fin_across(kind, stage).start()

    def finish_drain(kind):
        for stage in range(3):
            fin_across(kind, stage).wait_send()


    def gain_copy(stage):
        to = (partner, far, near)[stage]
        return remote(gain_in.at[0], gain_in.at[1 + stage], gain_send.at[stage], gain_recv.at[stage], to, z)

    def gain_along(i):
        return remote(
            gain_in.at[0], gain_in.at[3 + i], gain_send.at[2 + i], gain_recv.at[2 + i], dp_at, (z + i) % mp
        )

    def gain_step(stage):
        if stage in (1, 2, 3):
            gain_copy(stage - 1).wait()
            gain_in[0] = gain_in[0] + gain_in[stage]
        if stage < 3:
            gain_copy(stage).start()
        elif stage == 3:
            for i in range(1, mp):
                gain_along(i).start()
        else:
            for i in range(1, mp):
                gain_along(i).wait()
            sums = gain_in[0]
            for i in range(1, mp):
                sums = sums + gain_in[3 + i]
            ga_ref[...] = sums[0]
            gm_ref[...] = sums[1]

    move = {"s": send_own, "g": gather, "t": take, "f": finish, "n": gain_step}

    def place(part, step, i):
        for name, *what in PLAN.get((part, step, i), ()):
            move[name](*what)


    barrier = pltpu.get_barrier_semaphore()
    for to in (partner, near, far):
        pl.semaphore_signal(barrier, inc=1, device_id={"dp": to, "mp": z}, device_id_type=MESH)
    for i in range(1, mp):
        pl.semaphore_signal(
            barrier, inc=1, device_id={"dp": dp_at, "mp": (z + i) % mp}, device_id_type=MESH
        )
    cols = wq_ref.shape[0]
    hidden = wg_ref.shape[1]
    first = width - hidden
    rest = hidden - first
    pieces = [(ref, w.at[0, z, pl.ds(i * cols, cols)]) for i, ref in enumerate((wq_ref, wk_ref, wv_ref, wo_ref))]
    pieces += [
        (wg_ref, w.at[1, z, :, pl.ds(0, hidden)]),
        (wu_ref.at[:, pl.ds(0, first)], w.at[1, z, :, pl.ds(hidden, first)]),
        (wd_ref, w.at[2, z, pl.ds(0, hidden)]),
    ]
    stripes = width // rest
    tall = width // stripes
    pieces += [
        (wu_ref.at[pl.ds(j * tall, tall), pl.ds(first, rest)], w.at[2, z, pl.ds(hidden, tall), pl.ds(j * rest, rest)])
        for j in range(stripes)
    ]
    own = [pltpu.make_async_copy(src, dst, own_sem.at[i]) for i, (src, dst) in enumerate(pieces)]
    for copy in own:
        copy.start()

    lane = iota((T, 128), 1)
    lower = lane < 64
    low = (lane % 64) < 32
    length = len_ref[z]
    full = seq // 16 * 16

    def padded(ref):
        tail = jnp.broadcast_to(ref[0, full:seq, :].astype(f32), (T - full, width))
        tail = jnp.where(iota((T - full, width), 0) < seq - full, tail, 0.0).astype(bf16)
        return jnp.concatenate([ref[0, 0:full, :], tail], axis=0)

    def scale_of(rows_in):
        return lax.rsqrt(jnp.mean(rows_in * rows_in, axis=-1, keepdims=True) + EPS)

    def gain(ref):
        return ref[...].reshape(1, width)

    x = padded(x_ref).astype(f32)
    n1[...] = (x * scale_of(x) * gain(g1_ref)).astype(bf16)
    for copy in own:
        copy.wait()
    pl.semaphore_wait(barrier, 3 + mp - 1)
    place("P", 0, 0)

    acc[...] = x
    dyb[...] = jnp.where(iota((T, width), 0) < length, padded(dy_ref).astype(f32), 0.0).astype(bf16)
    key_at, query_at = iota((T, T), 0), iota((T, T), 1)
    mask[...] = jnp.where((key_at <= query_at) & (key_at < length), 0.0, NEG)
    heads_t[...] = jnp.zeros_like(heads_t)


    def attention(step):
        place("A", step, 0)
        cos, sin = cos_ref[...], sin_ref[...]
        s = pick(table, z, step)
        wa = w.at[0, s]
        qkv = nt(n1[...], wa[0:640, :])
        tiles = [qkv[:, 128 * i : 128 * i + 128] for i in range(5)]
        t0, t1, t2 = (t * cos + turned(t, low) * sin for t in tiles[0:3])
        t0, t1s = swap(t0), swap(t1)
        q[s, 0] = jnp.where(lower, 0.0, t0 * 0.125).astype(bf16)
        q[s, 1] = (jnp.where(lower, t0, t1s) * 0.125).astype(bf16)
        k[s, 0] = jnp.where(lower, 0.0, t1).astype(bf16)
        k[s, 1] = t2.astype(bf16)
        t3, t4 = swap(tiles[3]), swap(tiles[4])
        v[s, 0] = jnp.where(lower, 0.0, t3).astype(bf16)
        v[s, 1] = jnp.where(lower, t3, t4).astype(bf16)
        place("A", step, 1)
        for tile in range(2):
            kt[s, tile] = k[s, tile].T
            vt[tile] = v[s, tile].T
        for h, (tile, side) in enumerate(HEADS):
            qh = q[s, tile]
            if tile == 1:
                qh = jnp.where(lower if side == 0 else ~lower, qh, jnp.zeros_like(qh))
            at_row = 128 * tile + 64 * side
            for a, b in blocks:
                scores = nt(k[s, tile, 0:b, :], qh[a:b]) + mask[0:b, a:b]
                peak = jnp.max(scores, axis=0, keepdims=True)
                e = jnp.exp(scores - peak)
                norm = jnp.sum(e, axis=0, keepdims=True)
                c = nn(vt[tile, 64 * side : 64 * side + 64, 0:b], e.astype(bf16))
                heads_t[at_row : at_row + 64, a:b] = c * (1.0 / norm)
                lse[s, h : h + 1, a:b] = peak + jnp.log(norm)
            place("A", step, 2 + h)
        c = heads_t[...].astype(bf16)
        ctx[s] = c
        acc[...] += nn(c.T, wa[512:768, :])

    for step in range(mp):
        attention(step)

    x1 = acc[...]
    res[...] = x1
    normed = (x1 * scale_of(x1) * gain(g2_ref)).astype(bf16)
    n2[...] = normed
    n2t[...] = normed.T
    dn[...] = jnp.zeros_like(dn)


    def feed(step):
        place("F", step, 0)
        s = pick(table, z, step)
        w1, w2 = w.at[1, s], w.at[2, s]
        u0, u1 = 2 * step, 2 * step + 1
        gu = nn(n2[...], w1[...])
        late = nn(n2[:, 0:256], w2[512:768, 0:256])
        for j in range(1, 3):
            late = late + nn(n2[:, 256 * j : 256 * j + 256], w2[512:768, 256 * j : 256 * j + 256])
        dh = nt(dyb[...], w2[0:512, :])
        for i in range(2):
            part = slice(256 * i, 256 * i + 256)
            gate = gu[:, part]
            up = gu[:, 512:768] if i == 0 else late
            dhid = dh[:, part]
            sigma = 1.0 / (1.0 + jnp.exp(-gate))
            active = gate * sigma
            hb[step, :, part] = (active * up).astype(bf16)
            made[:, part] = (dhid * up * sigma * (1.0 + gate * (1.0 - sigma))).astype(bf16)
            made[:, 512 + 256 * i : 768 + 256 * i] = (dhid * active).astype(bf16)
        place("F", step, 1)
        gbuf[u0 % SLOTS[0]] = nn(n2t[...], made[:, 0:768]).astype(bf16)
        start_give(u0, 0)
        place("F", step, 2)
        turned_rows[0:512, :] = hb[step].T
        dn[...] += nt(made[:, 0:768], w1[...])
        place("F", step, 3)
        gbuf[u1 % SLOTS[0], 0:512, :] = nn(turned_rows[0:512, :], dyb[...]).astype(bf16)
        for j in range(3):
            part = slice(256 * j, 256 * j + 256)
            gbuf[u1 % SLOTS[0], 512:768, part] = nn(n2t[part, :], made[:, 768:1024]).astype(bf16)
        start_give(u1, 0)
        place("F", step, 4)
        for j in range(3):
            part = slice(256 * j, 256 * j + 256)
            dn[:, part] += nt(made[:, 768:1024], w2[512:768, part])

    for step in range(mp):
        feed(step)

    place("M", 0, 0)
    x1 = res[...]
    scale = scale_of(x1)
    hat = x1 * scale
    d2 = dn[...]
    gain_in[0] = jnp.zeros_like(gain_in[0])
    gain_in[0, 1:2, :] = jnp.sum(d2 * hat, axis=0, keepdims=True)
    e = d2 * gain(g2_ref)
    dx1 = dyb[...].astype(f32) + scale * (e - hat * jnp.mean(e * hat, axis=-1, keepdims=True))
    res[...] = dx1
    n2[...] = dx1.astype(bf16)
    dn[...] = jnp.zeros_like(dn)
    heads_t[192:256, :] = jnp.zeros((64, T), f32)


    def back(step):
        u = units_f + step
        slot = u % SLOTS[0]
        place("B", step, 0)
        cos, sin = cos_ref[...], sin_ref[...]
        s = shard_of(u)
        wa = w.at[0, s]
        dc = nt(n2[...], wa[512:768, :])
        dc = [jnp.where(lower, 0.0, dc[:, 0:128]).astype(bf16), dc[:, 128:256].astype(bf16)]
        for tile in range(2):
            dk_sum[tile] = jnp.zeros((T, 128), f32)
            dv_sum[tile] = jnp.zeros((T, 128), f32)
        for h, (tile, side) in enumerate(HEADS):
            qh, dch = q[s, tile], dc[tile]
            if tile == 1:
                here = lower if side == 0 else ~lower
                qh = jnp.where(here, qh, jnp.zeros_like(qh))
                dch = jnp.where(here, dch, jnp.zeros_like(dch))
            for i, (a, b) in enumerate(blocks):
                scores = nt(k[s, tile, 0:b, :], qh[a:b]) + mask[0:b, a:b]
                p = jnp.exp(scores - lse[s, h : h + 1, a:b])
                dprob = nt(v[s, tile, 0:b, :], dch[a:b])
                delta = jnp.sum(p * dprob, axis=0, keepdims=True)
                ds = (p * (dprob - delta)).astype(bf16)
                dv_sum[tile, 0:b, :] += nn(p.astype(bf16), dch[a:b])
                dk_sum[tile, 0:b, :] += nn(ds, qh[a:b])
                heads_t[64 * h : 64 * h + 64, a:b] = nn(kt[s, tile, 64 * side : 64 * side + 64, 0:b], ds)
                if i == 1:
                    place("B", step, 1 + 2 * h)
            place("B", step, 2 + 2 * h)

        def unturned(t):
            return t * cos - turned(t, low) * sin

        dq01 = unturned(heads_t[0:128, :].T * 0.125)
        dq2 = unturned(heads_t[128:256, :].T * 0.125)
        made[:, 0:128] = dq01.astype(bf16)
        made[:, 128:256] = jnp.where(lower, dq2, unturned(dk_sum[0])).astype(bf16)
        made[:, 256:384] = unturned(dk_sum[1]).astype(bf16)
        dv0, dv1 = swap(dv_sum[0]), swap(dv_sum[1])
        made[:, 384:512] = jnp.where(lower, dv0, dv1).astype(bf16)
        made[:, 512:640] = jnp.where(lower, dv1, 0.0).astype(bf16)
        turned_rows[...] = made[:, 0:640].T
        place("B", step, 7)
        gbuf[slot, 0:576, :] = nn(turned_rows[0:576, :], n1[...]).astype(bf16)
        gbuf[slot, 576:768, :] = nn(ctx[s, 64:256, :], n2[...]).astype(bf16)
        start_give(u, 0)
        place("B", step, 8)
        dn[...] += nn(made[:, 0:640], wa[0:640, :])

    for step in range(mp):
        back(step)


    place("E", 0, 0)
    x = padded(x_ref).astype(f32)
    scale = scale_of(x)
    hat = x * scale
    d1 = dn[...]
    gain_in[0, 0:1, :] = jnp.sum(d1 * hat, axis=0, keepdims=True)
    place("E", 0, 1)
    e = d1 * gain(g1_ref)
    dx = res[...] + scale * (e - hat * jnp.mean(e * hat, axis=-1, keepdims=True))
    staged[:, 0, :] = dx[0:seq]
    out_dx = pltpu.make_async_copy(staged, dx_ref, out_sem.at[0])
    out_dx.start()
    place("E", 0, 2)
    for j in range(mp):
        acc[...] += nn(hb[j], w[2, pick(table, z, j), 0:512, :])
        place("E", 0, 3 + j)
    out_dx.wait()
    staged[:, 0, :] = acc[0:seq, :]
    out_y = pltpu.make_async_copy(staged, out_ref, out_sem.at[1])
    out_y.start()
    place("E", 0, 3 + mp)
    gather_drain()
    home_drain()
    for kind in range(3):
        finish_drain(kind)
    out_y.wait()


def rotary(rows):
    position = np.arange(rows).astype(np.float32)
    index = np.arange(HEAD // 2).astype(np.float32)
    freq = (np.float32(10000.0) ** (np.float32(-2.0) * index / np.float32(HEAD))).astype(np.float32)
    angle = position[:, None] * freq[None, :]
    angle = np.concatenate([angle] * 4, axis=-1)
    return np.cos(angle).astype(np.float32), np.sin(angle).astype(np.float32)


def layer(mp, lengths, tokens, cotangent, gain1, gain2, weights):
    _, seq, width = tokens.shape
    T = (seq + 15) // 16 * 16
    cosine, sine = rotary(T)
    vmem, anywhere = pl.BlockSpec(memory_space=pltpu.VMEM), pl.BlockSpec(memory_space=pl.ANY)
    V, DMA = pltpu.VMEM, pltpu.SemaphoreType.DMA
    half, quarter, eighth = width // 2, width // 4, width // 8
    scratch = [
        V((3, mp, width, width), bf16),
        V((T, width), bf16),
        V((T, width), bf16),
        V((width, T), bf16),
        V((T, width), bf16),
        V((mp, 2, T, 128), bf16),
        V((mp, 2, T, 128), bf16),
        V((mp, 2, T, 128), bf16),
        V((mp, 2, 128, T), bf16),
        V((2, 128, T), bf16),
        V((mp, 256, T), bf16),
        V((256, T), f32),
        V((mp, 8, T), f32),
        V((T, T), f32),
        V((mp, T, 512), bf16),
        V((640, T), bf16),
        V((T, 1024), bf16),
        V((T, width), f32),
        V((T, width), f32),
        V((T, width), f32),
        V((2, T, 128), f32),
        V((2, T, 128), f32),
        V((SLOTS[0], width, width), bf16),
        V((SLOTS[1], half, width), bf16),
        V((SLOTS[2], quarter, width), bf16),
        V((SLOTS[3], eighth, width), bf16),
        V((3, mp, eighth, width), bf16),
        V((3, eighth, width), bf16),
        V((3 + mp, 8, width), f32),
        V((seq, 1, width), f32),
        DMA((10,)),
        DMA((3, mp)),
        DMA((3, mp)),
        DMA((3, mp, 3)),
        DMA((3, mp, 3)),
        DMA((3 * mp, 3)),
        DMA((3 * mp, 3)),
        DMA((3 * mp,)),
        DMA((3, mp)),
        DMA((3,)),
        DMA((3, 3)),
        DMA((3, 3)),
        DMA((2 + mp,)),
        DMA((2 + mp,)),
        DMA((2,)),
        pltpu.SemaphoreType.REGULAR((3,)),
    ]
    return pl.pallas_call(
        functools.partial(kernel, mp, T),
        out_shape=(
            jax.ShapeDtypeStruct((seq, 1, width), f32),
            jax.ShapeDtypeStruct((seq, 1, width), f32),
            jax.ShapeDtypeStruct((width,), f32),
            jax.ShapeDtypeStruct((width,), f32),
            jax.ShapeDtypeStruct((3, width, width), bf16),
        ),
        in_specs=[pl.BlockSpec(memory_space=pltpu.SMEM)] + [vmem] * 6 + [anywhere] * 7,
        out_specs=[anywhere, anywhere, vmem, vmem, anywhere],
        scratch_shapes=scratch,
        compiler_params=pltpu.CompilerParams(
            collective_id=0, has_side_effects=True, vmem_limit_bytes=63 * 2**20
        ),
    )(lengths, tokens, cotangent, gain1, gain2, jnp.asarray(cosine), jnp.asarray(sine), *weights)


def tidy_kernel(
    cols, hidden, out_in, dx_in, ga_in, gm_in, fin, out, dx, ga, gm, gq, gk, gv, go, gg, gu, gd, a, b, c, big, row, sems
):
    seq, width = out.shape[0], out.shape[2]
    first = width - hidden
    rest = hidden - first
    come = [pltpu.make_async_copy(src, row.at[i], sems.at[i]) for i, src in enumerate((out_in, dx_in))]
    go_on = [pltpu.make_async_copy(row.at[i], dst, sems.at[2 + i]) for i, dst in enumerate((out, dx))]
    loads = [pltpu.make_async_copy(fin.at[i], t, sems.at[4 + i]) for i, t in enumerate((a, b, c))]
    for copy in (*loads, *come):
        copy.start()
    ga[...] = ga_in[...]
    gm[...] = gm_in[...]
    stores = []

    def store(src, dst):
        copy = pltpu.make_async_copy(src, dst, sems.at[7 + len(stores)])
        copy.start()
        stores.append(copy)

    loads[0].wait()
    for i, dst in enumerate((gq, gk, gv, go)):
        part = pl.ds(i * cols, cols)
        big[0, part, :] = a[part, :].astype(f32)
        store(big.at[0, part], dst)
    loads[1].wait()
    big[1, :, 0:hidden] = b[:, 0:hidden].astype(f32)
    store(big.at[1, :, pl.ds(0, hidden)], gg)
    loads[2].wait()
    big[2, 0:hidden, :] = c[0:hidden, :].astype(f32)
    store(big.at[2, pl.ds(0, hidden)], gd)
    for first_half, second_half in zip(come, go_on):
        first_half.wait()
        second_half.start()
    big[3, :, 0:first] = b[:, hidden:].astype(f32)
    tall = width - hidden
    for j in range(width // rest):
        big[3, j * tall : j * tall + tall, first:hidden] = c[hidden:, j * rest : j * rest + rest].astype(f32)
    store(big.at[3, :, pl.ds(0, hidden)], gu)
    for copy in (*go_on, *stores):
        copy.wait()


def tidy(cols, hidden, out, dx, ga, gm, fin):
    seq, _, width = out.shape
    vmem, anywhere = pl.BlockSpec(memory_space=pltpu.VMEM), pl.BlockSpec(memory_space=pl.ANY)
    shapes = [(seq, 1, width)] * 2 + [(width,)] * 2 + [(cols, width)] * 4 + [(width, hidden)] * 2 + [(hidden, width)]
    return pl.pallas_call(
        functools.partial(tidy_kernel, cols, hidden),
        out_shape=tuple(jax.ShapeDtypeStruct(shape, f32) for shape in shapes),
        in_specs=[anywhere, anywhere, vmem, vmem, anywhere],
        out_specs=[anywhere, anywhere, vmem, vmem] + [anywhere] * 7,
        scratch_shapes=[pltpu.VMEM((width, width), fin.dtype)] * 3
        + [
            pltpu.VMEM((4, width, width), f32),
            pltpu.VMEM((2, seq, 1, width), f32),
            pltpu.SemaphoreType.DMA((14,)),
        ],
        compiler_params=pltpu.CompilerParams(vmem_limit_bytes=60 * 2**20),
    )(out, dx, ga, gm, fin)


def per_device(mp, dp, tokens, lengths, gain1, gain2, wq, wk, wv, wo, wg, wu, wd, cotangent):
    _, seq, width = tokens.shape
    weights = (wq.T, wk.T, wv.T, wo, wg, wu, wd)
    out, dx, gain_a, gain_m, fin = layer(mp, lengths, tokens, cotangent, gain1, gain2, weights)
    if dp > 8:
        groups = [[8 * i + j for i in range(dp // 8)] for j in range(8)]
        fin, gain_a, gain_m = lax.psum((fin.astype(f32), gain_a, gain_m), "dp", axis_index_groups=groups)
    cols, hidden = wq.shape[1], wg.shape[1]
    out, dx, gain_a, gain_m, gq, gk, gv, go, gg, gu, gd = tidy(cols, hidden, out, dx, gain_a, gain_m, fin)
    items = (1, seq, width)
    return out.reshape(items), dx.reshape(items), gain_a, gain_m, gq.T, gk.T, gv.T, go, gg, gu, gd


def solution(mesh):
    rows, cols, items = P("mp", None), P(None, "mp"), P(("dp", "mp"), None, None)
    return jax.shard_map(
        functools.partial(per_device, mesh.shape["mp"], mesh.shape["dp"]),
        mesh=mesh,
        in_specs=(items, P("dp"), P(), P(), cols, cols, cols, rows, cols, cols, rows, items),
        out_specs=(items, items, P(), P(), cols, cols, cols, rows, cols, cols, rows),
        check_vma=False,
    )
```

```python
import functools

import jax
import jax.numpy as jnp
import numpy as np
from jax import lax
from jax.experimental import pallas as pl
from jax.experimental.pallas import tpu as pltpu
from jax.sharding import PartitionSpec as P

HEAD = 64
EPS = 1e-05
NEG = -1e30
MESH = pl.DeviceIdType.MESH
f32, bf16 = jnp.float32, jnp.bfloat16
LOOPED = ("A", "F", "B")
SLOTS = (3, 6, 8, 12)
STEPS = ((3, 3, 3), (2, 3, 3), (2, 3, 3))

PLAN = {
    ("P", 0, 0): (("s", 0),),
    ("A", 0, 0): (("s", 1),),
    ("A", 0, 2): (("a", 1, 0, 0),),
    ("A", 1, 0): (("a", 1, 1, 0), ("a", 1, 2, 0), ("a", 1, 0, 1), ("a", 2, 0, 0), ("a", 2, 1, 0), ("a", 1, 1, 1), ("a", 1, 2, 1), ("a", 2, 0, 1), ("a", 2, 2, 0), ("a", 1, 0, 2), ("a", 1, 0, 3), ("a", 3, 0, 0),),
    ("A", 1, 1): (("a", 2, 1, 1), ("a", 3, 1, 0), ("a", 1, 1, 2), ("a", 1, 2, 2), ("a", 2, 2, 1), ("a", 2, 0, 2), ("a", 1, 1, 3), ("a", 3, 0, 1), ("a", 1, 2, 3), ("a", 3, 2, 0),),
    ("A", 1, 2): (("a", 2, 0, 3), ("s", 2),),
    ("A", 2, 0): (("a", 2, 1, 2), ("a", 3, 1, 1),),
    ("A", 2, 1): (("a", 2, 1, 3), ("a", 2, 2, 2), ("a", 3, 0, 2), ("a", 3, 2, 1), ("g", 1, 1, 0),),
    ("A", 2, 2): (("a", 2, 2, 3), ("a", 3, 0, 3),),
    ("A", 3, 0): (("a", 3, 1, 2), ("g", 1, 2, 0),),
    ("A", 3, 1): (("a", 3, 1, 3), ("a", 3, 2, 2),),
    ("A", 3, 2): (("a", 3, 2, 3), ("g", 1, 1, 1), ("g", 1, 3, 0),),
    ("F", 0, 0): (("g", 1, 1, 2), ("g", 1, 2, 1),),
    ("F", 0, 2): (("p", 0), ("g", 1, 3, 1), ("g", 2, 1, 0),),
    ("F", 0, 3): (("g", 2, 2, 0),),
    ("F", 0, 4): (("p", 1), ("t", 0, 0),),
    ("F", 1, 0): (("g", 1, 2, 2), ("t", 1, 0), ("g", 2, 3, 0), ("g", 1, 2, 3), ("g", 2, 2, 1), ("g", 1, 3, 2), ("g", 2, 3, 1), ("g", 2, 1, 1), ("g", 1, 3, 3), ("g", 2, 1, 2),),
    ("F", 1, 2): (("p", 2), ("t", 0, 1), ("t", 1, 1),),
    ("F", 1, 3): (("g", 2, 2, 2),),
    ("F", 1, 4): (("p", 3), ("g", 2, 3, 2), ("t", 2, 0),),
    ("F", 2, 0): (("g", 2, 2, 3),),
    ("F", 2, 1): (("g", 2, 3, 3), ("t", 3, 0), ("t", 0, 2), ("t", 1, 2),),
    ("F", 2, 2): (("p", 4),),
    ("F", 2, 4): (("p", 5), ("t", 2, 1), ("t", 4, 0),),
    ("F", 3, 1): (("t", 3, 1), ("t", 5, 0),),
    ("F", 3, 2): (("p", 6),),
    ("F", 3, 4): (("p", 7), ("t", 2, 2), ("t", 6, 0),),
    ("B", 0, 0): (("t", 7, 0),),
    ("B", 0, 7): (("p", 8), ("t", 3, 2), ("t", 4, 1),),
    ("B", 0, 8): (("p", 9), ("t", 5, 1), ("t", 8, 0),),
    ("B", 0, 9): (("p", 10), ("t", 6, 1), ("t", 9, 0),),
    ("B", 1, 7): (("p", 11), ("t", 4, 2), ("t", 5, 2), ("t", 7, 1), ("t", 8, 1), ("t", 10, 0), ("t", 11, 0), ("t", 9, 1), ("t", 6, 2),),
    ("B", 1, 8): (("p", 12),),
    ("B", 1, 9): (("p", 13), ("t", 8, 2), ("t", 9, 2), ("t", 12, 0), ("t", 10, 1), ("t", 11, 1), ("t", 7, 2), ("t", 13, 0),),
    ("B", 2, 7): (("p", 14),),
    ("B", 2, 8): (("p", 15), ("t", 10, 2), ("t", 11, 2), ("t", 12, 1), ("t", 13, 1), ("t", 14, 0),),
    ("B", 2, 9): (("p", 16), ("t", 15, 0),),
    ("B", 3, 7): (("p", 17), ("t", 12, 2), ("t", 13, 2), ("t", 14, 1), ("t", 15, 1), ("t", 16, 0), ("f", 1, 0), ("t", 17, 0),),
    ("B", 3, 8): (("p", 18),),
    ("B", 3, 9): (("p", 19), ("t", 14, 2), ("t", 15, 2), ("t", 18, 0),),
    ("E", 0, 0): (("t", 16, 1), ("t", 17, 1), ("t", 19, 0), ("f", 1, 1), ("f", 2, 0),),
    ("E", 0, 1): (("n", 0),),
    ("E", 0, 2): (("n", 1),),
    ("E", 0, 3): (("t", 18, 1), ("t", 16, 2),),
    ("E", 0, 4): (("t", 17, 2),),
    ("E", 0, 5): (("n", 2), ("t", 19, 1),),
    ("E", 0, 6): (("f", 3, 0),),
    ("E", 0, 7): (("t", 18, 2), ("f", 2, 1), ("f", 4, 0), ("n", 3), ("f", 1, 2), ("t", 19, 2), ("f", 5, 0), ("f", 3, 1), ("f", 1, 3), ("f", 4, 1), ("n", 4), ("f", 5, 1), ("f", 3, 2), ("f", 2, 2), ("f", 3, 3), ("f", 4, 2), ("f", 5, 2), ("f", 2, 3), ("f", 4, 3), ("f", 5, 3),),
}


def nn(left, right):
    return lax.dot_general(left, right, (((1,), (0,)), ((), ())), preferred_element_type=f32)


def nt(left, right):
    return lax.dot_general(left, right, (((1,), (1,)), ((), ())), preferred_element_type=f32)


def iota(shape, axis):
    return lax.broadcasted_iota(jnp.int32, shape, axis)


def turned(w, low):
    return jnp.where(low, -pltpu.roll(w, 96, 1), pltpu.roll(w, 32, 1))


def swap(w):
    return pltpu.roll(w, 64, 1)


def order_table(count):
    return [sorted(range(count), key=lambda s: s ^ z) for z in range(count)]


def pick(table, row, column):
    found = 0
    for r, values in enumerate(table):
        for c, value in enumerate(values):
            found = found + jnp.where((row == r) & (column == c), value, 0)
    return found


def kernel(
    mp,
    T,
    len_ref,
    x_ref,
    dy_ref,
    g1_ref,
    g2_ref,
    cos_ref,
    sin_ref,
    wq_ref,
    wk_ref,
    wv_ref,
    wo_ref,
    wg_ref,
    wu_ref,
    wd_ref,
    out_ref,
    dx_ref,
    ga_ref,
    gm_ref,
    fin_ref,
    w,
    n1,
    n2,
    n2t,
    dyb,
    q,
    k,
    v,
    kt,
    ctx,
    outs,
    heads_t,
    lse,
    mask,
    hb,
    turned_rows,
    made,
    acc,
    res,
    dn,
    dk_sum,
    dv_sum,
    gbuf,
    r1,
    r2,
    r3,
    r4,
    total,
    gain_in,
    staged,
    own_sem,
    az_send,
    az_recv,
    ag_send,
    ag_recv,
    z_send,
    z_recv,
    g_send,
    g_recv,
    s_send,
    s_recv,
    h_send,
    h_recv,
    fin_sem,
    f_send,
    f_recv,
    gain_send,
    gain_recv,
    out_sem,
    credit,
):
    seq, width = x_ref.shape[1], x_ref.shape[2]
    half, quarter, eighth = width // 2, width // 4, width // 8
    heads = wq_ref.shape[0] // HEAD
    tall = width // heads
    blocks = [(a, min(a + 256, T)) for a in range(0, T, 256)]
    dp_at, z = lax.axis_index("dp"), lax.axis_index("mp")
    core, bit1, bit2 = dp_at % 2, (dp_at // 2) % 2, (dp_at // 4) % 2
    partner = dp_at + 1 - 2 * core
    flip1, flip2 = dp_at + 2 - 4 * bit1, dp_at + 4 - 8 * bit2
    near = jnp.where(core == 0, flip1, flip2)
    far = jnp.where(core == 0, flip2, flip1)
    near_bit = jnp.where(core == 0, bit1, bit2)
    far_bit = jnp.where(core == 0, bit2, bit1)
    table = order_table(mp)
    units_f, units = 2 * mp, 3 * mp

    def at(start, size):
        return pl.ds(pl.multiple_of(start, 16), size)

    def spans(start, size):
        half_at = start + core * (size // 2)
        quarter_at = half_at + far_bit * (size // 4)
        eighth_at = quarter_at + near_bit * (size // 8)
        return (near, at(eighth_at, size // 8)), (far, at(quarter_at, size // 4)), (partner, at(half_at, size // 2))

    widening = spans(0, width)
    by_head = [spans(h * tall, tall) for h in range(heads)]
    brief = ((near, at(core * half + (bit1 + bit2) % 2 * quarter, quarter)), widening[2])
    direct = (widening[2],)

    def remote(src, dst, send, recv, dp_to, z_to):
        return pltpu.make_async_remote_copy(
            src_ref=src,
            dst_ref=dst,
            send_sem=send,
            recv_sem=recv,
            device_id={"dp": dp_to, "mp": z_to},
            device_id_type=MESH,
        )


    def hops(kind, j):
        return (None, direct, brief, widening)[STEPS[kind][j - 1]]

    def along(kind, j, shard, to):
        part = w.at[kind, shard, hops(kind, j)[0][1]]
        return remote(part, part, z_send.at[kind, j], z_recv.at[kind, j], dp_at, to)

    def across(kind, j, shard, stage):
        to, rows = hops(kind, j)[stage]
        part = w.at[kind, shard, rows]
        return remote(part, part, g_send.at[kind, j, stage], g_recv.at[kind, j, stage], to, z)

    def head_along(j, h, shard, to):
        part = w.at[0, shard, by_head[h][0][1]]
        return remote(part, part, az_send.at[j, h], az_recv.at[j, h], dp_at, to)

    def head_across(j, h, shard, stage):
        to, rows = by_head[h][stage]
        part = w.at[0, shard, rows]
        return remote(part, part, ag_send.at[j, h, stage], ag_recv.at[j, h, stage], to, z)

    def send_own(kind):
        for j in range(1, mp):
            if kind == 0:
                for h in range(heads):
                    head_along(j, h, z, pick(table, z, j)).start()
            else:
                along(kind, j, z, pick(table, z, j)).start()

    def gather_head(j, h, stage):
        shard = pick(table, z, j)
        if stage == 0:
            head_along(j, h, shard, shard).wait_recv()
        else:
            head_across(j, h, shard, stage - 1).wait_recv()
        if stage < 3:
            head_across(j, h, shard, stage).start()

    def gather(kind, j, stage):
        shard = pick(table, z, j)
        if stage == 0:
            along(kind, j, shard, shard).wait_recv()
        else:
            across(kind, j, shard, stage - 1).wait_recv()
        if stage < STEPS[kind][j - 1]:
            across(kind, j, shard, stage).start()

    def gather_drain():
        for j in range(1, mp):
            shard = pick(table, z, j)
            for h in range(heads):
                head_along(j, h, z, shard).wait_send()
                for stage in range(3):
                    head_across(j, h, shard, stage).wait_send()
            for kind in (1, 2):
                along(kind, j, z, shard).wait_send()
                for stage in range(STEPS[kind][j - 1]):
                    across(kind, j, shard, stage).wait_send()


    def unit_of(u):
        return u if u < units_f else units_f + (u - units_f) // heads

    def head_of(u):
        return (u - units_f) % heads

    def shard_of(u):
        return pick(table, z, u // 2) if u < units_f else (z + 1 + (u - units_f) // heads) % mp

    def kind_of(u):
        return 1 + u % 2 if u < units_f else 0

    stores = (gbuf, r1, r2, r3)
    hops_back = (partner, far, near)
    given = (1 - core, 1 - far_bit, 1 - near_bit)
    kept = (core, far_bit, near_bit)

    def size_of(u, stage):
        whole = width if u < units_f else tall
        h = 0 if u < units_f else head_of(u)
        return whole >> (stage + 1), h * (whole >> stage), h * (whole >> (stage + 1))

    def give(u, stage):
        size, before, after = size_of(u, stage)
        unit = unit_of(u)
        return remote(
            stores[stage].at[unit % SLOTS[stage], at(before + given[stage] * size, size)],
            stores[stage + 1].at[unit % SLOTS[stage + 1], at(after, size)],
            s_send.at[u, stage],
            s_recv.at[u, stage],
            hops_back[stage],
            z,
        )

    def start_give(u, stage):
        if unit_of(u) >= SLOTS[stage + 1] and (u < units_f or head_of(u) == 0):
            pl.semaphore_wait(credit.at[stage], 1)
        give(u, stage).start()

    def release(u, stage):
        if unit_of(u) + SLOTS[stage + 1] < units and (u < units_f or head_of(u) == heads - 1):
            pl.semaphore_signal(
                credit.at[stage], inc=1, device_id={"dp": hops_back[stage], "mp": z}, device_id_type=MESH
            )

    def take(u, stage):
        copy = give(u, stage)
        copy.wait_recv()
        copy.wait_send()
        mine, came = stores[stage], stores[stage + 1]
        unit = unit_of(u)
        here, there = unit % SLOTS[stage], unit % SLOTS[stage + 1]
        size, before, after = size_of(u, stage)
        step = size >> (2 - stage)

        def add(i, carry):
            to = at(after + i * step, step)
            sums = mine[here, at(before + kept[stage] * size + i * step, step), :].astype(f32)
            came[there, to, :] = (sums + came[there, to, :].astype(f32)).astype(bf16)
            return carry

        lax.fori_loop(0, (4, 2, 1)[stage], add, 0)
        if stage > 0:
            release(u, stage - 1)
        if stage < 2:
            start_give(u, stage + 1)
        elif own_shard(u):
            rows = pl.ds(after, size)
            r4[kind_of(u), z, rows, :] = r3[there, rows, :]
        else:
            home(u).start()

    def own_shard(u):
        return u < 2 or u >= units_f + (mp - 1) * heads

    def home(u):
        size, _, after = size_of(u, 2)
        kind, rows = kind_of(u), pl.ds(after, size)
        arrived = kind if u < units_f else 3 + head_of(u)
        return remote(
            r3.at[unit_of(u) % SLOTS[3], rows],
            r4.at[kind, z, rows],
            h_send.at[u],
            h_recv.at[arrived, z],
            dp_at,
            shard_of(u),
        )

    def home_drain():
        for u in range(units_f + mp * heads):
            if not own_shard(u):
                home(u).wait_send()


    def sum_rows(which):
        if which < 3:
            return which, pl.ds(0, eighth), widening
        return 0, pl.ds((which - 3) * (tall // 8), tall // 8), by_head[which - 3]

    def fin_own(which):
        kind, rows, spans_of = sum_rows(which)
        return pltpu.make_async_copy(total.at[kind, rows], fin_ref.at[kind, spans_of[0][1]], fin_sem.at[which])

    def fin_across(which, stage):
        kind, own_rows, spans_of = sum_rows(which)
        to, rows = spans_of[stage]
        src = total.at[kind, own_rows] if stage == 0 else fin_ref.at[kind, rows]
        return remote(src, fin_ref.at[kind, rows], f_send.at[which, stage], f_recv.at[which, stage], to, z)

    def finish(which, stage):
        kind, rows, _ = sum_rows(which)
        if stage == 0:
            for src in range(mp):

                @pl.when(z != src)
                def _(src=src):
                    remote(
                        r3.at[0, rows], r4.at[kind, src, rows], h_send.at[0], h_recv.at[which, src], dp_at, src
                    ).wait_recv()

            sums = r4[kind, 0, rows, :].astype(f32)
            for src in range(1, mp):
                sums = sums + r4[kind, src, rows, :].astype(f32)
            total[kind, rows, :] = sums.astype(bf16)
            fin_own(which).start()
        else:
            if stage == 1:
                fin_own(which).wait()
            fin_across(which, stage - 1).wait_recv()
        if stage < 3:
            fin_across(which, stage).start()

    def finish_drain(which):
        for stage in range(3):
            fin_across(which, stage).wait_send()


    def gain_copy(stage):
        to = (partner, far, near)[stage]
        return remote(gain_in.at[0], gain_in.at[1 + stage], gain_send.at[stage], gain_recv.at[stage], to, z)

    def gain_along(i):
        return remote(
            gain_in.at[0], gain_in.at[3 + i], gain_send.at[2 + i], gain_recv.at[2 + i], dp_at, (z + i) % mp
        )

    def gain_step(stage):
        if stage in (1, 2, 3):
            gain_copy(stage - 1).wait()
            gain_in[0] = gain_in[0] + gain_in[stage]
        if stage < 3:
            gain_copy(stage).start()
        elif stage == 3:
            for i in range(1, mp):
                gain_along(i).start()
        else:
            for i in range(1, mp):
                gain_along(i).wait()
            sums = gain_in[0]
            for i in range(1, mp):
                sums = sums + gain_in[3 + i]
            ga_ref[...] = sums[0]
            gm_ref[...] = sums[1]

    move = {"p": lambda u: start_give(u, 0), "s": send_own, "a": gather_head, "g": gather, "t": take, "f": finish, "n": gain_step}

    def place(part, step, i):
        def run(acts):
            for name, *what in acts:
                move[name](*what)

        if isinstance(step, int):
            run(PLAN.get((part, step, i), ()))
            return
        for at_step in range(mp):
            acts = PLAN.get((part, at_step, i))
            if acts is not None:
                pl.when(step == at_step)(functools.partial(run, acts))

    def run_steps(part, body):
        if part in LOOPED:

            def again(step, carry):
                body(step)
                return carry

            lax.fori_loop(0, mp, again, 0)
        else:
            for step in range(mp):
                body(step)


    barrier = pltpu.get_barrier_semaphore()
    for to in (partner, near, far):
        pl.semaphore_signal(barrier, inc=1, device_id={"dp": to, "mp": z}, device_id_type=MESH)
    for i in range(1, mp):
        pl.semaphore_signal(
            barrier, inc=1, device_id={"dp": dp_at, "mp": (z + i) % mp}, device_id_type=MESH
        )
    hidden = wg_ref.shape[1]
    first = width - hidden
    rest = hidden - first
    pieces = [
        (ref.at[pl.ds(HEAD * h, HEAD)], w.at[0, z, pl.ds(tall * h + HEAD * i, HEAD)])
        for h in range(heads)
        for i, ref in enumerate((wq_ref, wk_ref, wv_ref, wo_ref))
    ]
    pieces += [
        (wg_ref, w.at[1, z, :, pl.ds(0, hidden)]),
        (wu_ref.at[:, pl.ds(0, first)], w.at[1, z, :, pl.ds(hidden, first)]),
        (wd_ref, w.at[2, z, pl.ds(0, hidden)]),
    ]
    stripes = width // rest
    stripe = width // stripes
    pieces += [
        (wu_ref.at[pl.ds(j * stripe, stripe), pl.ds(first, rest)], w.at[2, z, pl.ds(hidden, stripe), pl.ds(j * rest, rest)])
        for j in range(stripes)
    ]
    own = [pltpu.make_async_copy(src, dst, own_sem.at[i]) for i, (src, dst) in enumerate(pieces)]
    for copy in own:
        copy.start()

    lane = iota((T, 128), 1)
    lower = lane < 64
    low = (lane % 64) < 32
    length = len_ref[z]
    full = seq // 16 * 16

    def padded(ref):
        tail = jnp.broadcast_to(ref[0, full:seq, :].astype(f32), (T - full, width))
        tail = jnp.where(iota((T - full, width), 0) < seq - full, tail, 0.0).astype(bf16)
        return jnp.concatenate([ref[0, 0:full, :], tail], axis=0)

    def scale_of(rows_in):
        return lax.rsqrt(jnp.mean(rows_in * rows_in, axis=-1, keepdims=True) + EPS)

    def gain(ref):
        return ref[...].reshape(1, width)

    x = padded(x_ref).astype(f32)
    n1[...] = (x * scale_of(x) * gain(g1_ref)).astype(bf16)
    for copy in own[: 4 * heads]:
        copy.wait()
    pl.semaphore_wait(barrier, 3 + mp - 1)
    place("P", 0, 0)
    for copy in own[4 * heads :]:
        copy.wait()

    acc[...] = x
    dyb[...] = jnp.where(iota((T, width), 0) < length, padded(dy_ref).astype(f32), 0.0).astype(bf16)
    key_at, query_at = iota((T, T), 0), iota((T, T), 1)
    mask[...] = jnp.where((key_at <= query_at) & (key_at < length), 0.0, NEG)
    heads_t[...] = jnp.zeros_like(heads_t)
    ctx[:, heads * HEAD :, :] = jnp.zeros((mp, 256 - heads * HEAD, T), bf16)
    outs[...] = jnp.zeros_like(outs)


    def out_rows(s):
        for h in range(heads):
            outs[HEAD * h : HEAD * h + HEAD, :] = w[0, s, tall * h + 3 * HEAD : tall * h + 4 * HEAD, :]

    def attention(step):
        s = pick(table, z, step)
        cos, sin = cos_ref[...], sin_ref[...]
        for h in range(heads):
            place("A", step, h)
            qkv = nt(n1[...], w[0, s, tall * h : tall * h + tall, :])
            qk, vo = qkv[:, 0:128], qkv[:, 128:256]
            qk = qk * cos + turned(qk, low) * sin
            qh = jnp.where(lower, qk * 0.125, 0.0).astype(bf16)
            kh = jnp.where(lower, swap(qk), 0.0).astype(bf16)
            vh = jnp.where(lower, vo, 0.0).astype(bf16)
            q[s, h], k[s, h], v[s, h] = qh, kh, vh
            kt[s, h] = kh.T[0:HEAD]
            vt = vh.T[0:HEAD]
            for a, b in blocks:
                scores = nt(kh[0:b], qh[a:b]) + mask[0:b, a:b]
                peak = jnp.max(scores, axis=0, keepdims=True)
                e = jnp.exp(scores - peak)
                norm = jnp.sum(e, axis=0, keepdims=True)
                c = nn(vt[:, 0:b], e.astype(bf16))
                ctx[s, HEAD * h : HEAD * h + HEAD, a:b] = (c * (1.0 / norm)).astype(bf16)
                lse[s, h : h + 1, a:b] = peak + jnp.log(norm)
        place("A", step, heads)
        out_rows(s)
        acc[...] += nn(ctx[s].T, outs[...])

    run_steps("A", attention)

    x1 = acc[...]
    res[...] = x1
    normed = (x1 * scale_of(x1) * gain(g2_ref)).astype(bf16)
    n2[...] = normed
    n2t[...] = normed.T
    dn[...] = jnp.zeros_like(dn)


    def feed(step):
        place("F", step, 0)
        s = pick(table, z, step)
        w1, w2 = w.at[1, s], w.at[2, s]
        u0, u1 = 2 * step, 2 * step + 1
        gu = nn(n2[...], w1[...])
        late = nn(n2[:, 0:256], w2[512:768, 0:256])
        for j in range(1, 3):
            late = late + nn(n2[:, 256 * j : 256 * j + 256], w2[512:768, 256 * j : 256 * j + 256])
        dh = nt(dyb[...], w2[0:512, :])
        for i in range(2):
            part = slice(256 * i, 256 * i + 256)
            gate = gu[:, part]
            up = gu[:, 512:768] if i == 0 else late
            dhid = dh[:, part]
            sigma = 1.0 / (1.0 + jnp.exp(-gate))
            active = gate * sigma
            hb[step, :, part] = (active * up).astype(bf16)
            made[:, part] = (dhid * up * sigma * (1.0 + gate * (1.0 - sigma))).astype(bf16)
            made[:, 512 + 256 * i : 768 + 256 * i] = (dhid * active).astype(bf16)
        place("F", step, 1)
        gbuf[u0 % SLOTS[0]] = nn(n2t[...], made[:, 0:768]).astype(bf16)
        place("F", step, 2)
        turned_rows[0:512, :] = hb[step].T
        dn[...] += nt(made[:, 0:768], w1[...])
        place("F", step, 3)
        gbuf[u1 % SLOTS[0], 0:512, :] = nn(turned_rows[0:512, :], dyb[...]).astype(bf16)
        for j in range(3):
            part = slice(256 * j, 256 * j + 256)
            gbuf[u1 % SLOTS[0], 512:768, part] = nn(n2t[part, :], made[:, 768:1024]).astype(bf16)
        place("F", step, 4)
        for j in range(3):
            part = slice(256 * j, 256 * j + 256)
            dn[:, part] += nt(made[:, 768:1024], w2[512:768, part])

    run_steps("F", feed)

    place("M", 0, 0)
    x1 = res[...]
    scale = scale_of(x1)
    hat = x1 * scale
    d2 = dn[...]
    gain_in[0] = jnp.zeros_like(gain_in[0])
    gain_in[0, 1:2, :] = jnp.sum(d2 * hat, axis=0, keepdims=True)
    e = d2 * gain(g2_ref)
    dx1 = dyb[...].astype(f32) + scale * (e - hat * jnp.mean(e * hat, axis=-1, keepdims=True))
    res[...] = dx1
    n2[...] = dx1.astype(bf16)
    dn[...] = jnp.zeros_like(dn)


    def back(step):
        slot = (units_f + step) % SLOTS[0]
        cos, sin = cos_ref[...], sin_ref[...]
        s = (z + 1 + step) % mp
        out_rows(s)
        place("B", step, 0)
        dc = nt(n2[...], outs[...])
        dc = [jnp.where(lower, t, 0.0).astype(bf16) for t in (dc[:, 0:128], swap(dc[:, 0:128]), dc[:, 128:256])]
        of_out = nn(ctx[s, 0 : heads * HEAD, :], n2[...]).astype(bf16)
        for h in range(heads):
            gbuf[slot, tall * h + 3 * HEAD : tall * h + 4 * HEAD, :] = of_out[HEAD * h : HEAD * h + HEAD]
        for h in range(heads):
            place("B", step, 1 + 2 * h)
            qh, dch = q[s, h], dc[h]
            dk_sum[...] = jnp.zeros_like(dk_sum)
            dv_sum[...] = jnp.zeros_like(dv_sum)
            for a, b in blocks:
                scores = nt(k[s, h, 0:b, :], qh[a:b]) + mask[0:b, a:b]
                p = jnp.exp(scores - lse[s, h : h + 1, a:b])
                dprob = nt(v[s, h, 0:b, :], dch[a:b])
                delta = jnp.sum(p * dprob, axis=0, keepdims=True)
                ds = (p * (dprob - delta)).astype(bf16)
                dv_sum[0:b, :] += nn(p.astype(bf16), dch[a:b])
                dk_sum[0:b, :] += nn(ds, qh[a:b])
                heads_t[0:HEAD, a:b] = nn(kt[s, h, :, 0:b], ds)
            d = heads_t[...].T * 0.125 + swap(dk_sum[...])
            made[:, 0:128] = (d * cos - turned(d, low) * sin).astype(bf16)
            made[:, 128:256] = dv_sum[...].astype(bf16)
            turned_rows[0:256, :] = made[:, 0:256].T
            place("B", step, 2 + 2 * h)
            gbuf[slot, tall * h : tall * h + 3 * HEAD, :] = nn(turned_rows[0 : 3 * HEAD, :], n1[...]).astype(bf16)
            place("B", step, 7 + h)
            dn[...] += nn(made[:, 0:256], w[0, s, tall * h : tall * h + tall, :])

    run_steps("B", back)


    place("E", 0, 0)
    x = padded(x_ref).astype(f32)
    scale = scale_of(x)
    hat = x * scale
    d1 = dn[...]
    gain_in[0, 0:1, :] = jnp.sum(d1 * hat, axis=0, keepdims=True)
    place("E", 0, 1)
    e = d1 * gain(g1_ref)
    dx = res[...] + scale * (e - hat * jnp.mean(e * hat, axis=-1, keepdims=True))
    staged[:, 0, :] = dx[0:seq]
    out_dx = pltpu.make_async_copy(staged, dx_ref, out_sem.at[0])
    out_dx.start()
    place("E", 0, 2)
    for j in range(mp):
        acc[...] += nn(hb[j], w[2, pick(table, z, j), 0:512, :])
        place("E", 0, 3 + j)
    out_dx.wait()
    staged[:, 0, :] = acc[0:seq, :]
    out_y = pltpu.make_async_copy(staged, out_ref, out_sem.at[1])
    out_y.start()
    place("E", 0, 3 + mp)
    gather_drain()
    home_drain()
    for which in range(1, 3 + heads):
        finish_drain(which)
    out_y.wait()


def rotary(rows):
    position = np.arange(rows).astype(np.float32)
    index = np.arange(HEAD // 2).astype(np.float32)
    freq = (np.float32(10000.0) ** (np.float32(-2.0) * index / np.float32(HEAD))).astype(np.float32)
    angle = position[:, None] * freq[None, :]
    angle = np.concatenate([angle] * 4, axis=-1)
    return np.cos(angle).astype(np.float32), np.sin(angle).astype(np.float32)


def layer(mp, lengths, tokens, cotangent, gain1, gain2, weights):
    _, seq, width = tokens.shape
    T = (seq + 15) // 16 * 16
    cosine, sine = rotary(T)
    vmem, anywhere = pl.BlockSpec(memory_space=pltpu.VMEM), pl.BlockSpec(memory_space=pl.ANY)
    V, DMA = pltpu.VMEM, pltpu.SemaphoreType.DMA
    half, quarter, eighth = width // 2, width // 4, width // 8
    heads = weights[0].shape[0] // HEAD
    scratch = [
        V((3, mp, width, width), bf16),
        V((T, width), bf16),
        V((T, width), bf16),
        V((width, T), bf16),
        V((T, width), bf16),
        V((mp, heads, T, 128), bf16),
        V((mp, heads, T, 128), bf16),
        V((mp, heads, T, 128), bf16),
        V((mp, heads, HEAD, T), bf16),
        V((mp, 256, T), bf16),
        V((256, width), bf16),
        V((128, T), f32),
        V((mp, 8, T), f32),
        V((T, T), f32),
        V((mp, T, 512), bf16),
        V((512, T), bf16),
        V((T, 1024), bf16),
        V((T, width), f32),
        V((T, width), f32),
        V((T, width), f32),
        V((T, 128), f32),
        V((T, 128), f32),
        V((SLOTS[0], width, width), bf16),
        V((SLOTS[1], half, width), bf16),
        V((SLOTS[2], quarter, width), bf16),
        V((SLOTS[3], eighth, width), bf16),
        V((3, mp, eighth, width), bf16),
        V((3, eighth, width), bf16),
        V((3 + mp, 8, width), f32),
        V((seq, 1, width), f32),
        DMA((4 * heads + 6,)),
        DMA((mp, heads)),
        DMA((mp, heads)),
        DMA((mp, heads, 3)),
        DMA((mp, heads, 3)),
        DMA((3, mp)),
        DMA((3, mp)),
        DMA((3, mp, 3)),
        DMA((3, mp, 3)),
        DMA((2 * mp + heads * mp, 3)),
        DMA((2 * mp + heads * mp, 3)),
        DMA((2 * mp + heads * mp,)),
        DMA((3 + heads, mp)),
        DMA((3 + heads,)),
        DMA((3 + heads, 3)),
        DMA((3 + heads, 3)),
        DMA((2 + mp,)),
        DMA((2 + mp,)),
        DMA((2,)),
        pltpu.SemaphoreType.REGULAR((3,)),
    ]
    return pl.pallas_call(
        functools.partial(kernel, mp, T),
        out_shape=(
            jax.ShapeDtypeStruct((seq, 1, width), f32),
            jax.ShapeDtypeStruct((seq, 1, width), f32),
            jax.ShapeDtypeStruct((width,), f32),
            jax.ShapeDtypeStruct((width,), f32),
            jax.ShapeDtypeStruct((3, width, width), bf16),
        ),
        in_specs=[pl.BlockSpec(memory_space=pltpu.SMEM)] + [vmem] * 6 + [anywhere] * 7,
        out_specs=[anywhere, anywhere, vmem, vmem, anywhere],
        scratch_shapes=scratch,
        compiler_params=pltpu.CompilerParams(
            collective_id=0, has_side_effects=True, vmem_limit_bytes=63 * 2**20
        ),
    )(lengths, tokens, cotangent, gain1, gain2, jnp.asarray(cosine), jnp.asarray(sine), *weights)


def tidy_kernel(
    cols, hidden, out_in, dx_in, ga_in, gm_in, fin, out, dx, ga, gm, gq, gk, gv, go, gg, gu, gd, a, b, c, big, row, sems
):
    seq, width = out.shape[0], out.shape[2]
    first = width - hidden
    rest = hidden - first
    come = [pltpu.make_async_copy(src, row.at[i], sems.at[i]) for i, src in enumerate((out_in, dx_in))]
    go_on = [pltpu.make_async_copy(row.at[i], dst, sems.at[2 + i]) for i, dst in enumerate((out, dx))]
    loads = [pltpu.make_async_copy(fin.at[i], t, sems.at[4 + i]) for i, t in enumerate((a, b, c))]
    for copy in (*loads, *come):
        copy.start()
    ga[...] = ga_in[...]
    gm[...] = gm_in[...]
    stores = []

    def store(src, dst):
        copy = pltpu.make_async_copy(src, dst, sems.at[7 + len(stores)])
        copy.start()
        stores.append(copy)

    loads[0].wait()
    heads = cols // HEAD
    for i, dst in enumerate((gq, gk, gv, go)):
        for h in range(heads):
            at_row, from_row = i * cols + h * HEAD, h * (width // heads) + i * HEAD
            big[0, at_row : at_row + HEAD, :] = a[from_row : from_row + HEAD, :].astype(f32)
        store(big.at[0, pl.ds(i * cols, cols)], dst)
    loads[1].wait()
    big[1, :, 0:hidden] = b[:, 0:hidden].astype(f32)
    store(big.at[1, :, pl.ds(0, hidden)], gg)
    loads[2].wait()
    big[2, 0:hidden, :] = c[0:hidden, :].astype(f32)
    store(big.at[2, pl.ds(0, hidden)], gd)
    for first_half, second_half in zip(come, go_on):
        first_half.wait()
        second_half.start()
    big[3, :, 0:first] = b[:, hidden:].astype(f32)
    tall = width - hidden
    for j in range(width // rest):
        big[3, j * tall : j * tall + tall, first:hidden] = c[hidden:, j * rest : j * rest + rest].astype(f32)
    store(big.at[3, :, pl.ds(0, hidden)], gu)
    for copy in (*go_on, *stores):
        copy.wait()


def tidy(cols, hidden, out, dx, ga, gm, fin):
    seq, _, width = out.shape
    vmem, anywhere = pl.BlockSpec(memory_space=pltpu.VMEM), pl.BlockSpec(memory_space=pl.ANY)
    shapes = [(seq, 1, width)] * 2 + [(width,)] * 2 + [(cols, width)] * 4 + [(width, hidden)] * 2 + [(hidden, width)]
    return pl.pallas_call(
        functools.partial(tidy_kernel, cols, hidden),
        out_shape=tuple(jax.ShapeDtypeStruct(shape, f32) for shape in shapes),
        in_specs=[anywhere, anywhere, vmem, vmem, anywhere],
        out_specs=[anywhere, anywhere, vmem, vmem] + [anywhere] * 7,
        scratch_shapes=[pltpu.VMEM((width, width), fin.dtype)] * 3
        + [
            pltpu.VMEM((4, width, width), f32),
            pltpu.VMEM((2, seq, 1, width), f32),
            pltpu.SemaphoreType.DMA((14,)),
        ],
        compiler_params=pltpu.CompilerParams(vmem_limit_bytes=60 * 2**20),
    )(out, dx, ga, gm, fin)


def per_device(mp, dp, tokens, lengths, gain1, gain2, wq, wk, wv, wo, wg, wu, wd, cotangent):
    _, seq, width = tokens.shape
    weights = (wq.T, wk.T, wv.T, wo, wg, wu, wd)
    out, dx, gain_a, gain_m, fin = layer(mp, lengths, tokens, cotangent, gain1, gain2, weights)
    if dp > 8:
        groups = [[8 * i + j for i in range(dp // 8)] for j in range(8)]
        fin, gain_a, gain_m = lax.psum((fin.astype(f32), gain_a, gain_m), "dp", axis_index_groups=groups)
    cols, hidden = wq.shape[1], wg.shape[1]
    out, dx, gain_a, gain_m, gq, gk, gv, go, gg, gu, gd = tidy(cols, hidden, out, dx, gain_a, gain_m, fin)
    items = (1, seq, width)
    return out.reshape(items), dx.reshape(items), gain_a, gain_m, gq.T, gk.T, gv.T, go, gg, gu, gd


def solution(mesh):
    rows, cols, items = P("mp", None), P(None, "mp"), P(("dp", "mp"), None, None)
    return jax.shard_map(
        functools.partial(per_device, mesh.shape["mp"], mesh.shape["dp"]),
        mesh=mesh,
        in_specs=(items, P("dp"), P(), P(), cols, cols, cols, rows, cols, cols, rows, items),
        out_specs=(items, items, P(), P(), cols, cols, cols, rows, cols, cols, rows),
        check_vma=False,
    )
```

```python
import functools

import jax
import jax.numpy as jnp
import numpy as np
from jax import lax
from jax.experimental import pallas as pl
from jax.experimental.pallas import tpu as pltpu
from jax.sharding import PartitionSpec as P

HEAD = 64
EPS = 1e-05
NEG = -1e30
MESH = pl.DeviceIdType.MESH
f32, bf16 = jnp.float32, jnp.bfloat16
LOOPED = ("A", "F", "B")
SLOTS = (3, 6, 8, 12)
STEPS = ((3, 3, 3), (2, 3, 3), (3, 3, 2))

PLAN = {
    ("P", 0, 0): (("s", 0),),
    ("A", 0, 1): (("s", 1),),
    ("A", 0, 2): (("a", 1, 0, 0), ("a", 1, 1, 0),),
    ("A", 0, 3): (("a", 1, 2, 0),),
    ("A", 1, 0): (("a", 1, 0, 1), ("a", 1, 1, 1), ("a", 2, 0, 0), ("a", 1, 2, 1), ("a", 2, 1, 0), ("a", 2, 2, 0), ("a", 2, 0, 1), ("a", 1, 0, 2), ("a", 3, 0, 0), ("a", 1, 1, 2), ("a", 1, 0, 3), ("a", 2, 1, 1), ("a", 1, 2, 2), ("a", 1, 1, 3), ("a", 3, 1, 0), ("a", 2, 2, 1), ("a", 1, 2, 3),),
    ("A", 1, 1): (("a", 2, 0, 2), ("a", 3, 0, 1), ("a", 3, 2, 0), ("a", 2, 1, 2),),
    ("A", 1, 2): (("a", 2, 0, 3), ("a", 2, 1, 3), ("a", 2, 2, 2), ("a", 3, 1, 1),),
    ("A", 1, 3): (("a", 2, 2, 3), ("a", 3, 2, 1), ("a", 3, 0, 2), ("g", 1, 1, 0),),
    ("A", 2, 0): (("a", 3, 0, 3), ("a", 3, 1, 2), ("s", 2),),
    ("A", 2, 1): (("a", 3, 1, 3), ("g", 1, 2, 0), ("a", 3, 2, 2),),
    ("A", 2, 2): (("a", 3, 2, 3),),
    ("A", 2, 3): (("g", 1, 1, 1), ("g", 1, 3, 0), ("g", 1, 2, 1),),
    ("A", 3, 0): (("g", 2, 1, 0), ("g", 1, 1, 2),),
    ("A", 3, 3): (("g", 1, 3, 1),),
    ("F", 0, 0): (("g", 2, 1, 1), ("g", 2, 2, 0), ("g", 1, 2, 2),),
    ("F", 0, 1): (("g", 1, 2, 3),),
    ("F", 0, 2): (("p", 0),),
    ("F", 0, 3): (("g", 1, 3, 2), ("t", 0, 0), ("g", 2, 2, 1), ("g", 1, 3, 3), ("g", 2, 1, 2),),
    ("F", 0, 4): (("p", 1), ("g", 2, 1, 3), ("g", 2, 3, 0),),
    ("F", 1, 0): (("t", 1, 0),),
    ("F", 1, 2): (("p", 2),),
    ("F", 1, 3): (("t", 0, 1), ("t", 2, 0), ("g", 2, 2, 2),),
    ("F", 1, 4): (("p", 3), ("g", 2, 2, 3),),
    ("F", 2, 0): (("t", 3, 0),),
    ("F", 2, 1): (("g", 2, 3, 1), ("t", 1, 1), ("t", 0, 2),),
    ("F", 2, 2): (("p", 4), ("g", 2, 3, 2),),
    ("F", 2, 4): (("p", 5), ("t", 4, 0), ("t", 2, 1),),
    ("F", 3, 0): (("t", 5, 0), ("t", 1, 2), ("t", 3, 1),),
    ("F", 3, 2): (("p", 6),),
    ("F", 3, 4): (("p", 7), ("t", 2, 2), ("t", 6, 0),),
    ("M", 0, 0): (("t", 7, 0), ("t", 3, 2), ("t", 4, 1),),
    ("B", 0, 0): (("t", 5, 1),),
    ("B", 0, 8): (("t", 6, 1), ("t", 4, 2),),
    ("B", 0, 9): (("p", 8), ("t", 5, 2), ("t", 7, 1), ("t", 6, 2), ("t", 8, 0),),
    ("B", 1, 7): (("t", 7, 2),),
    ("B", 1, 8): (("t", 8, 1),),
    ("B", 1, 9): (("p", 9),),
    ("B", 2, 7): (("t", 8, 2), ("t", 9, 0),),
    ("B", 2, 9): (("p", 10), ("f", 1, 0),),
    ("B", 3, 0): (("t", 9, 1), ("t", 10, 0),),
    ("B", 3, 7): (("p", 11), ("f", 1, 1), ("f", 2, 0), ("t", 9, 2), ("t", 11, 0),),
    ("B", 3, 8): (("p", 12), ("t", 10, 1),),
    ("B", 3, 9): (("p", 13), ("t", 12, 0), ("f", 2, 1), ("t", 11, 1), ("t", 13, 0),),
    ("E", 0, 0): (("f", 1, 2), ("t", 10, 2),),
    ("E", 0, 1): (("n", 0), ("f", 1, 3), ("t", 11, 2), ("n", 1), ("t", 12, 1),),
    ("E", 0, 2): (("t", 13, 1), ("f", 2, 2), ("n", 2), ("t", 12, 2), ("f", 3, 0), ("f", 4, 0), ("f", 2, 3), ("t", 13, 2), ("f", 5, 0), ("n", 3),),
    ("E", 0, 3): (("f", 3, 1), ("f", 4, 1),),
    ("E", 0, 4): (("f", 5, 1), ("n", 4),),
    ("E", 0, 7): (("f", 3, 2), ("f", 4, 2), ("f", 5, 2), ("f", 3, 3), ("f", 4, 3), ("f", 5, 3),),
}


def nn(left, right):
    return lax.dot_general(left, right, (((1,), (0,)), ((), ())), preferred_element_type=f32)


def nt(left, right):
    return lax.dot_general(left, right, (((1,), (1,)), ((), ())), preferred_element_type=f32)


def iota(shape, axis):
    return lax.broadcasted_iota(jnp.int32, shape, axis)


def turned(w, low):
    return jnp.where(low, -pltpu.roll(w, 96, 1), pltpu.roll(w, 32, 1))


def swap(w):
    return pltpu.roll(w, 64, 1)


def order_table(count):
    return [sorted(range(count), key=lambda s: s ^ z) for z in range(count)]


def pick(table, row, column):
    found = 0
    for r, values in enumerate(table):
        for c, value in enumerate(values):
            found = found + jnp.where((row == r) & (column == c), value, 0)
    return found


def kernel(
    mp,
    T,
    len_ref,
    x_ref,
    dy_ref,
    g1_ref,
    g2_ref,
    cos_ref,
    sin_ref,
    wq_ref,
    wk_ref,
    wv_ref,
    wo_ref,
    wg_ref,
    wu_ref,
    wd_ref,
    out_ref,
    dx_ref,
    ga_ref,
    gm_ref,
    fin_ref,
    w,
    n1,
    n2,
    n2t,
    dyb,
    q,
    k,
    v,
    kt,
    ctx,
    outs,
    heads_t,
    lse,
    mask,
    hb,
    turned_rows,
    made,
    acc,
    res,
    dn,
    dk_sum,
    dv_sum,
    gbuf,
    r1,
    r2,
    r3,
    r4,
    total,
    gain_in,
    staged,
    own_sem,
    az_send,
    az_recv,
    ag_send,
    ag_recv,
    z_send,
    z_recv,
    g_send,
    g_recv,
    s_send,
    s_recv,
    h_send,
    h_recv,
    fin_sem,
    f_send,
    f_recv,
    gain_send,
    gain_recv,
    out_sem,
    credit,
):
    seq, width = x_ref.shape[1], x_ref.shape[2]
    half, quarter = width // 2, width // 4
    heads = wq_ref.shape[0] // HEAD
    tall = width // heads
    blocks = [(a, min(a + 256, T)) for a in range(0, T, 256)]
    dp_at, z = lax.axis_index("dp"), lax.axis_index("mp")
    core, bit1, bit2 = dp_at % 2, (dp_at // 2) % 2, (dp_at // 4) % 2
    partner = dp_at + 1 - 2 * core
    flip1, flip2 = dp_at + 2 - 4 * bit1, dp_at + 4 - 8 * bit2
    near = jnp.where(core == 0, flip1, flip2)
    far = jnp.where(core == 0, flip2, flip1)
    near_bit = jnp.where(core == 0, bit1, bit2)
    far_bit = jnp.where(core == 0, bit2, bit1)
    table = order_table(mp)
    units_f, units = 2 * mp, 3 * mp

    def at(start, size):
        return pl.ds(pl.multiple_of(start, 16), size)

    def spans(start, size):
        half_at = start + core * (size // 2)
        quarter_at = half_at + far_bit * (size // 4)
        eighth_at = quarter_at + near_bit * (size // 8)
        return (near, at(eighth_at, size // 8)), (far, at(quarter_at, size // 4)), (partner, at(half_at, size // 2))

    widening = spans(0, width)
    by_head = [spans(h * tall, tall) for h in range(heads)]
    brief = ((near, at(core * half + (bit1 + bit2) % 2 * quarter, quarter)), widening[2])
    direct = (widening[2],)

    def remote(src, dst, send, recv, dp_to, z_to):
        return pltpu.make_async_remote_copy(
            src_ref=src,
            dst_ref=dst,
            send_sem=send,
            recv_sem=recv,
            device_id={"dp": dp_to, "mp": z_to},
            device_id_type=MESH,
        )


    def hops(kind, j):
        return (None, direct, brief, widening)[STEPS[kind][j - 1]]

    def along(kind, j, shard, to):
        part = w.at[kind, shard, hops(kind, j)[0][1]]
        return remote(part, part, z_send.at[kind, j], z_recv.at[kind, j], dp_at, to)

    def across(kind, j, shard, stage):
        to, rows = hops(kind, j)[stage]
        part = w.at[kind, shard, rows]
        return remote(part, part, g_send.at[kind, j, stage], g_recv.at[kind, j, stage], to, z)

    def head_along(j, h, shard, to):
        part = w.at[0, shard, by_head[h][0][1]]
        return remote(part, part, az_send.at[j, h], az_recv.at[j, h], dp_at, to)

    def head_across(j, h, shard, stage):
        to, rows = by_head[h][stage]
        part = w.at[0, shard, rows]
        return remote(part, part, ag_send.at[j, h, stage], ag_recv.at[j, h, stage], to, z)

    def send_own(kind):
        for j in range(1, mp):
            if kind == 0:
                for h in range(heads):
                    head_along(j, h, z, pick(table, z, j)).start()
            else:
                along(kind, j, z, pick(table, z, j)).start()

    def gather_head(j, h, stage):
        shard = pick(table, z, j)
        if stage == 0:
            head_along(j, h, shard, shard).wait_recv()
        else:
            head_across(j, h, shard, stage - 1).wait_recv()
        if stage < 3:
            head_across(j, h, shard, stage).start()

    def gather(kind, j, stage):
        shard = pick(table, z, j)
        if stage == 0:
            along(kind, j, shard, shard).wait_recv()
        else:
            across(kind, j, shard, stage - 1).wait_recv()
        if stage < STEPS[kind][j - 1]:
            across(kind, j, shard, stage).start()

    def gather_drain():
        for j in range(1, mp):
            shard = pick(table, z, j)
            for h in range(heads):
                head_along(j, h, z, shard).wait_send()
                for stage in range(3):
                    head_across(j, h, shard, stage).wait_send()
            for kind in (1, 2):
                along(kind, j, z, shard).wait_send()
                for stage in range(STEPS[kind][j - 1]):
                    across(kind, j, shard, stage).wait_send()


    whole = units - 1

    def unit_of(u):
        return min(u, whole)

    def block_of(u):
        return pl.ds(0, heads) if u < whole else pl.ds(u - whole, 1)

    def shard_of(u):
        return pick(table, z, u // 2) if u < units_f else (z + 1 + u - units_f) % mp

    def kind_of(u):
        return 1 + u % 2 if u < units_f else 0

    stores = (gbuf, r1, r2, r3)
    hops_back = (partner, far, near)
    given = (1 - core, 1 - far_bit, 1 - near_bit)
    kept = (core, far_bit, near_bit)

    def give(u, stage):
        size = tall >> (stage + 1)
        unit, block = unit_of(u), block_of(u)
        return remote(
            stores[stage].at[unit % SLOTS[stage], block, at(given[stage] * size, size)],
            stores[stage + 1].at[unit % SLOTS[stage + 1], block],
            s_send.at[u, stage],
            s_recv.at[u, stage],
            hops_back[stage],
            z,
        )

    def start_give(u, stage):
        if unit_of(u) >= SLOTS[stage + 1] and u <= whole:
            pl.semaphore_wait(credit.at[stage], 1)
        give(u, stage).start()

    def release(u, stage):
        if unit_of(u) + SLOTS[stage + 1] < units:
            pl.semaphore_signal(
                credit.at[stage], inc=1, device_id={"dp": hops_back[stage], "mp": z}, device_id_type=MESH
            )

    def take(u, stage):
        copy = give(u, stage)
        copy.wait_recv()
        copy.wait_send()
        mine, came = stores[stage], stores[stage + 1]
        here, there = unit_of(u) % SLOTS[stage], unit_of(u) % SLOTS[stage + 1]
        size = tall >> (stage + 1)

        def add(block, carry):
            sums = mine[here, block, at(kept[stage] * size, size), :].astype(f32) + came[there, block].astype(f32)
            came[there, block] = sums.astype(bf16)
            return carry

        if u < whole:
            lax.fori_loop(0, heads, add, 0)
        else:
            add(u - whole, 0)
        if stage > 0:
            release(u, stage - 1)
        if stage < 2:
            start_give(u, stage + 1)
        elif own_shard(u):
            r4[kind_of(u), z, block_of(u)] = r3[there, block_of(u)]
        else:
            home(u).start()

    def own_shard(u):
        return u < 2 or u >= whole

    def home(u):
        kind = kind_of(u)
        return remote(r3.at[u % SLOTS[3]], r4.at[kind, z], h_send.at[u], h_recv.at[kind, z], dp_at, shard_of(u))

    def home_drain():
        for u in range(2, whole):
            home(u).wait_send()


    def sum_block(which):
        return (which, pl.ds(0, heads)) if which < 3 else (0, pl.ds(which - 3, 1))

    tall_spans = spans(0, tall)

    def fin_own(which):
        kind, block = sum_block(which)
        return pltpu.make_async_copy(
            total.at[kind, block], fin_ref.at[kind, block, tall_spans[0][1]], fin_sem.at[which]
        )

    def fin_across(which, stage):
        kind, block = sum_block(which)
        to, rows = tall_spans[stage]
        dst = fin_ref.at[kind, block, rows]
        src = total.at[kind, block] if stage == 0 else dst
        return remote(src, dst, f_send.at[which, stage], f_recv.at[which, stage], to, z)

    def finish(which, stage):
        kind, block = sum_block(which)
        if stage == 0:
            if which <= 3:
                for src in range(mp):

                    @pl.when(z != src)
                    def _(src=src):
                        remote(r3.at[0], r4.at[kind, src], h_send.at[0], h_recv.at[kind, src], dp_at, src).wait_recv()

            sums = r4[kind, 0, block].astype(f32)
            for src in range(1, mp):
                sums = sums + r4[kind, src, block].astype(f32)
            total[kind, block] = sums.astype(bf16)
            fin_own(which).start()
        else:
            if stage == 1:
                fin_own(which).wait()
            fin_across(which, stage - 1).wait_recv()
        if stage < 3:
            fin_across(which, stage).start()

    def finish_drain(which):
        for stage in range(3):
            fin_across(which, stage).wait_send()


    def gain_copy(stage):
        to = (partner, far, near)[stage]
        return remote(gain_in.at[0], gain_in.at[1 + stage], gain_send.at[stage], gain_recv.at[stage], to, z)

    def gain_along(i):
        return remote(
            gain_in.at[0], gain_in.at[3 + i], gain_send.at[2 + i], gain_recv.at[2 + i], dp_at, (z + i) % mp
        )

    def gain_step(stage):
        if stage in (1, 2, 3):
            gain_copy(stage - 1).wait()
            gain_in[0] = gain_in[0] + gain_in[stage]
        if stage < 3:
            gain_copy(stage).start()
        elif stage == 3:
            for i in range(1, mp):
                gain_along(i).start()
        else:
            for i in range(1, mp):
                gain_along(i).wait()
            sums = gain_in[0]
            for i in range(1, mp):
                sums = sums + gain_in[3 + i]
            ga_ref[...] = sums[0]
            gm_ref[...] = sums[1]

    move = {"p": lambda u: start_give(u, 0), "s": send_own, "a": gather_head, "g": gather, "t": take, "f": finish, "n": gain_step}

    def place(part, step, i):
        def run(acts):
            for name, *what in acts:
                move[name](*what)

        if isinstance(step, int):
            run(PLAN.get((part, step, i), ()))
            return
        for at_step in range(mp):
            acts = PLAN.get((part, at_step, i))
            if acts is not None:
                pl.when(step == at_step)(functools.partial(run, acts))

    def run_steps(part, body):
        if part in LOOPED:

            def again(step, carry):
                body(step)
                return carry

            lax.fori_loop(0, mp, again, 0)
        else:
            for step in range(mp):
                body(step)


    barrier = pltpu.get_barrier_semaphore()
    for to in (partner, near, far):
        pl.semaphore_signal(barrier, inc=1, device_id={"dp": to, "mp": z}, device_id_type=MESH)
    for i in range(1, mp):
        pl.semaphore_signal(
            barrier, inc=1, device_id={"dp": dp_at, "mp": (z + i) % mp}, device_id_type=MESH
        )
    hidden = wg_ref.shape[1]
    first = width - hidden
    rest = hidden - first
    pieces = [
        (ref.at[pl.ds(HEAD * h, HEAD)], w.at[0, z, pl.ds(tall * h + HEAD * i, HEAD)])
        for h in range(heads)
        for i, ref in enumerate((wq_ref, wk_ref, wv_ref, wo_ref))
    ]
    pieces += [
        (wg_ref, w.at[1, z, :, pl.ds(0, hidden)]),
        (wu_ref.at[:, pl.ds(0, first)], w.at[1, z, :, pl.ds(hidden, first)]),
        (wd_ref, w.at[2, z, pl.ds(0, hidden)]),
    ]
    stripes = width // rest
    stripe = width // stripes
    pieces += [
        (wu_ref.at[pl.ds(j * stripe, stripe), pl.ds(first, rest)], w.at[2, z, pl.ds(hidden, stripe), pl.ds(j * rest, rest)])
        for j in range(stripes)
    ]
    own = [pltpu.make_async_copy(src, dst, own_sem.at[i]) for i, (src, dst) in enumerate(pieces)]
    for copy in own:
        copy.start()

    lane = iota((T, 128), 1)
    lower = lane < 64
    low = (lane % 64) < 32
    length = len_ref[z]
    full = seq // 16 * 16

    def padded(ref):
        tail = jnp.broadcast_to(ref[0, full:seq, :].astype(f32), (T - full, width))
        tail = jnp.where(iota((T - full, width), 0) < seq - full, tail, 0.0).astype(bf16)
        return jnp.concatenate([ref[0, 0:full, :], tail], axis=0)

    def scale_of(rows_in):
        return lax.rsqrt(jnp.mean(rows_in * rows_in, axis=-1, keepdims=True) + EPS)

    def gain(ref):
        return ref[...].reshape(1, width)

    x = padded(x_ref).astype(f32)
    n1[...] = (x * scale_of(x) * gain(g1_ref)).astype(bf16)
    for copy in own[: 4 * heads]:
        copy.wait()
    pl.semaphore_wait(barrier, 3 + mp - 1)
    place("P", 0, 0)
    for copy in own[4 * heads :]:
        copy.wait()

    acc[...] = x
    dyb[...] = jnp.where(iota((T, width), 0) < length, padded(dy_ref).astype(f32), 0.0).astype(bf16)
    key_at, query_at = iota((T, T), 0), iota((T, T), 1)
    mask[...] = jnp.where((key_at <= query_at) & (key_at < length), 0.0, NEG)
    heads_t[...] = jnp.zeros_like(heads_t)
    ctx[:, heads * HEAD :, :] = jnp.zeros((mp, 256 - heads * HEAD, T), bf16)
    outs[...] = jnp.zeros_like(outs)


    def out_rows(s):
        for h in range(heads):
            outs[HEAD * h : HEAD * h + HEAD, :] = w[0, s, tall * h + 3 * HEAD : tall * h + 4 * HEAD, :]

    def attention(step):
        s = pick(table, z, step)
        cos, sin = cos_ref[...], sin_ref[...]
        for h in range(heads):
            place("A", step, h)
            qkv = nt(n1[...], w[0, s, tall * h : tall * h + tall, :])
            qk, vo = qkv[:, 0:128], qkv[:, 128:256]
            qk = qk * cos + turned(qk, low) * sin
            qh = jnp.where(lower, qk * 0.125, 0.0).astype(bf16)
            kh = jnp.where(lower, swap(qk), 0.0).astype(bf16)
            vh = jnp.where(lower, vo, 0.0).astype(bf16)
            q[s, h], k[s, h], v[s, h] = qh, kh, vh
            kt[s, h] = kh.T[0:HEAD]
            vt = vh.T[0:HEAD]
            for a, b in blocks:
                scores = nt(kh[0:b], qh[a:b]) + mask[0:b, a:b]
                peak = jnp.max(scores, axis=0, keepdims=True)
                e = jnp.exp(scores - peak)
                norm = jnp.sum(e, axis=0, keepdims=True)
                c = nn(vt[:, 0:b], e.astype(bf16))
                ctx[s, HEAD * h : HEAD * h + HEAD, a:b] = (c * (1.0 / norm)).astype(bf16)
                lse[s, h : h + 1, a:b] = peak + jnp.log(norm)
        place("A", step, heads)
        out_rows(s)
        acc[...] += nn(ctx[s].T, outs[...])

    run_steps("A", attention)

    x1 = acc[...]
    res[...] = x1
    normed = (x1 * scale_of(x1) * gain(g2_ref)).astype(bf16)
    n2[...] = normed
    n2t[...] = normed.T
    dn[...] = jnp.zeros_like(dn)


    def feed(step):
        place("F", step, 0)
        s = pick(table, z, step)
        w1, w2 = w.at[1, s], w.at[2, s]
        u0, u1 = 2 * step, 2 * step + 1
        gu = nn(n2[...], w1[...])
        late = nn(n2[:, 0:256], w2[512:768, 0:256])
        for j in range(1, 3):
            late = late + nn(n2[:, 256 * j : 256 * j + 256], w2[512:768, 256 * j : 256 * j + 256])
        dh = nt(dyb[...], w2[0:512, :])
        for i in range(2):
            part = slice(256 * i, 256 * i + 256)
            gate = gu[:, part]
            up = gu[:, 512:768] if i == 0 else late
            dhid = dh[:, part]
            sigma = 1.0 / (1.0 + jnp.exp(-gate))
            active = gate * sigma
            hb[step, :, part] = (active * up).astype(bf16)
            made[:, part] = (dhid * up * sigma * (1.0 + gate * (1.0 - sigma))).astype(bf16)
            made[:, 512 + 256 * i : 768 + 256 * i] = (dhid * active).astype(bf16)
        place("F", step, 1)
        gbuf[u0 % SLOTS[0]] = nn(n2t[...], made[:, 0:768]).astype(bf16).reshape(heads, tall, width)
        place("F", step, 2)
        turned_rows[0:512, :] = hb[step].T
        dn[...] += nt(made[:, 0:768], w1[...])
        place("F", step, 3)
        gbuf[u1 % SLOTS[0], 0:2] = nn(turned_rows[0:512, :], dyb[...]).astype(bf16).reshape(2, tall, width)
        for j in range(3):
            part = slice(256 * j, 256 * j + 256)
            gbuf[u1 % SLOTS[0], 2, :, part] = nn(n2t[part, :], made[:, 768:1024]).astype(bf16)
        place("F", step, 4)
        for j in range(3):
            part = slice(256 * j, 256 * j + 256)
            dn[:, part] += nt(made[:, 768:1024], w2[512:768, part])

    run_steps("F", feed)

    place("M", 0, 0)
    x1 = res[...]
    scale = scale_of(x1)
    hat = x1 * scale
    d2 = dn[...]
    gain_in[0] = jnp.zeros_like(gain_in[0])
    gain_in[0, 1:2, :] = jnp.sum(d2 * hat, axis=0, keepdims=True)
    e = d2 * gain(g2_ref)
    dx1 = dyb[...].astype(f32) + scale * (e - hat * jnp.mean(e * hat, axis=-1, keepdims=True))
    res[...] = dx1
    n2[...] = dx1.astype(bf16)
    dn[...] = jnp.zeros_like(dn)


    def back(step):
        slot = (units_f + step) % SLOTS[0]
        cos, sin = cos_ref[...], sin_ref[...]
        s = (z + 1 + step) % mp
        out_rows(s)
        place("B", step, 0)
        dc = nt(n2[...], outs[...])
        dc = [jnp.where(lower, t, 0.0).astype(bf16) for t in (dc[:, 0:128], swap(dc[:, 0:128]), dc[:, 128:256])]
        of_out = nn(ctx[s, 0 : heads * HEAD, :], n2[...]).astype(bf16)
        for h in range(heads):
            gbuf[slot, h, 3 * HEAD : 4 * HEAD, :] = of_out[HEAD * h : HEAD * h + HEAD]
        for h in range(heads):
            place("B", step, 1 + 2 * h)
            qh, dch = q[s, h], dc[h]
            dk_sum[...] = jnp.zeros_like(dk_sum)
            dv_sum[...] = jnp.zeros_like(dv_sum)
            for a, b in blocks:
                scores = nt(k[s, h, 0:b, :], qh[a:b]) + mask[0:b, a:b]
                p = jnp.exp(scores - lse[s, h : h + 1, a:b])
                dprob = nt(v[s, h, 0:b, :], dch[a:b])
                delta = jnp.sum(p * dprob, axis=0, keepdims=True)
                ds = (p * (dprob - delta)).astype(bf16)
                dv_sum[0:b, :] += nn(p.astype(bf16), dch[a:b])
                dk_sum[0:b, :] += nn(ds, qh[a:b])
                heads_t[0:HEAD, a:b] = nn(kt[s, h, :, 0:b], ds)
            d = heads_t[...].T * 0.125 + swap(dk_sum[...])
            made[:, 0:128] = (d * cos - turned(d, low) * sin).astype(bf16)
            made[:, 128:256] = dv_sum[...].astype(bf16)
            turned_rows[0:256, :] = made[:, 0:256].T
            place("B", step, 2 + 2 * h)
            gbuf[slot, h, 0 : 3 * HEAD, :] = nn(turned_rows[0 : 3 * HEAD, :], n1[...]).astype(bf16)
            place("B", step, 7 + h)
            dn[...] += nn(made[:, 0:256], w[0, s, tall * h : tall * h + tall, :])

    run_steps("B", back)


    place("E", 0, 0)
    x = padded(x_ref).astype(f32)
    scale = scale_of(x)
    hat = x * scale
    d1 = dn[...]
    gain_in[0, 0:1, :] = jnp.sum(d1 * hat, axis=0, keepdims=True)
    place("E", 0, 1)
    e = d1 * gain(g1_ref)
    dx = res[...] + scale * (e - hat * jnp.mean(e * hat, axis=-1, keepdims=True))
    staged[:, 0, :] = dx[0:seq]
    out_dx = pltpu.make_async_copy(staged, dx_ref, out_sem.at[0])
    out_dx.start()
    place("E", 0, 2)
    for j in range(mp):
        acc[...] += nn(hb[j], w[2, pick(table, z, j), 0:512, :])
        place("E", 0, 3 + j)
    out_dx.wait()
    staged[:, 0, :] = acc[0:seq, :]
    out_y = pltpu.make_async_copy(staged, out_ref, out_sem.at[1])
    out_y.start()
    place("E", 0, 3 + mp)
    gather_drain()
    home_drain()
    for which in range(1, 3 + heads):
        finish_drain(which)
    out_y.wait()


def rotary(rows):
    position = np.arange(rows).astype(np.float32)
    index = np.arange(HEAD // 2).astype(np.float32)
    freq = (np.float32(10000.0) ** (np.float32(-2.0) * index / np.float32(HEAD))).astype(np.float32)
    angle = position[:, None] * freq[None, :]
    angle = np.concatenate([angle] * 4, axis=-1)
    return np.cos(angle).astype(np.float32), np.sin(angle).astype(np.float32)


def layer(mp, lengths, tokens, cotangent, gain1, gain2, weights):
    _, seq, width = tokens.shape
    T = (seq + 15) // 16 * 16
    cosine, sine = rotary(T)
    vmem, anywhere = pl.BlockSpec(memory_space=pltpu.VMEM), pl.BlockSpec(memory_space=pl.ANY)
    V, DMA = pltpu.VMEM, pltpu.SemaphoreType.DMA
    heads = weights[0].shape[0] // HEAD
    tall = width // heads
    scratch = [
        V((3, mp, width, width), bf16),
        V((T, width), bf16),
        V((T, width), bf16),
        V((width, T), bf16),
        V((T, width), bf16),
        V((mp, heads, T, 128), bf16),
        V((mp, heads, T, 128), bf16),
        V((mp, heads, T, 128), bf16),
        V((mp, heads, HEAD, T), bf16),
        V((mp, 256, T), bf16),
        V((256, width), bf16),
        V((128, T), f32),
        V((mp, 8, T), f32),
        V((T, T), f32),
        V((mp, T, 512), bf16),
        V((512, T), bf16),
        V((T, 1024), bf16),
        V((T, width), f32),
        V((T, width), f32),
        V((T, width), f32),
        V((T, 128), f32),
        V((T, 128), f32),
        V((SLOTS[0], heads, tall, width), bf16),
        V((SLOTS[1], heads, tall // 2, width), bf16),
        V((SLOTS[2], heads, tall // 4, width), bf16),
        V((SLOTS[3], heads, tall // 8, width), bf16),
        V((3, mp, heads, tall // 8, width), bf16),
        V((3, heads, tall // 8, width), bf16),
        V((3 + mp, 8, width), f32),
        V((seq, 1, width), f32),
        DMA((4 * heads + 6,)),
        DMA((mp, heads)),
        DMA((mp, heads)),
        DMA((mp, heads, 3)),
        DMA((mp, heads, 3)),
        DMA((3, mp)),
        DMA((3, mp)),
        DMA((3, mp, 3)),
        DMA((3, mp, 3)),
        DMA((3 * mp - 1 + heads, 3)),
        DMA((3 * mp - 1 + heads, 3)),
        DMA((3 * mp - 1,)),
        DMA((3, mp)),
        DMA((3 + heads,)),
        DMA((3 + heads, 3)),
        DMA((3 + heads, 3)),
        DMA((2 + mp,)),
        DMA((2 + mp,)),
        DMA((2,)),
        pltpu.SemaphoreType.REGULAR((3,)),
    ]
    return pl.pallas_call(
        functools.partial(kernel, mp, T),
        out_shape=(
            jax.ShapeDtypeStruct((seq, 1, width), f32),
            jax.ShapeDtypeStruct((seq, 1, width), f32),
            jax.ShapeDtypeStruct((width,), f32),
            jax.ShapeDtypeStruct((width,), f32),
            jax.ShapeDtypeStruct((3, heads, tall, width), bf16),
        ),
        in_specs=[pl.BlockSpec(memory_space=pltpu.SMEM)] + [vmem] * 6 + [anywhere] * 7,
        out_specs=[anywhere, anywhere, vmem, vmem, anywhere],
        scratch_shapes=scratch,
        compiler_params=pltpu.CompilerParams(
            collective_id=0, has_side_effects=True, vmem_limit_bytes=63 * 2**20
        ),
    )(lengths, tokens, cotangent, gain1, gain2, jnp.asarray(cosine), jnp.asarray(sine), *weights)


def tidy_kernel(
    cols, hidden, out_in, dx_in, ga_in, gm_in, fin, out, dx, ga, gm, gq, gk, gv, go, gg, gu, gd, a, b, c, big, row, sems
):
    seq, width = out.shape[0], out.shape[2]
    first = width - hidden
    rest = hidden - first
    come = [pltpu.make_async_copy(src, row.at[i], sems.at[i]) for i, src in enumerate((out_in, dx_in))]
    go_on = [pltpu.make_async_copy(row.at[i], dst, sems.at[2 + i]) for i, dst in enumerate((out, dx))]
    loads = [pltpu.make_async_copy(fin.at[i], t, sems.at[4 + i]) for i, t in enumerate((a, b, c))]
    for copy in (*loads, *come):
        copy.start()
    ga[...] = ga_in[...]
    gm[...] = gm_in[...]
    stores = []

    def store(src, dst):
        copy = pltpu.make_async_copy(src, dst, sems.at[7 + len(stores)])
        copy.start()
        stores.append(copy)

    loads[0].wait()
    heads = cols // HEAD
    for i, dst in enumerate((gq, gk, gv, go)):
        for h in range(heads):
            at_row, from_row = i * cols + h * HEAD, h * (width // heads) + i * HEAD
            big[0, at_row : at_row + HEAD, :] = a[from_row : from_row + HEAD, :].astype(f32)
        store(big.at[0, pl.ds(i * cols, cols)], dst)
    loads[1].wait()
    big[1, :, 0:hidden] = b[:, 0:hidden].astype(f32)
    store(big.at[1, :, pl.ds(0, hidden)], gg)
    loads[2].wait()
    big[2, 0:hidden, :] = c[0:hidden, :].astype(f32)
    store(big.at[2, pl.ds(0, hidden)], gd)
    for first_half, second_half in zip(come, go_on):
        first_half.wait()
        second_half.start()
    big[3, :, 0:first] = b[:, hidden:].astype(f32)
    tall = width - hidden
    for j in range(width // rest):
        big[3, j * tall : j * tall + tall, first:hidden] = c[hidden:, j * rest : j * rest + rest].astype(f32)
    store(big.at[3, :, pl.ds(0, hidden)], gu)
    for copy in (*go_on, *stores):
        copy.wait()


def tidy(cols, hidden, out, dx, ga, gm, fin):
    seq, _, width = out.shape
    vmem, anywhere = pl.BlockSpec(memory_space=pltpu.VMEM), pl.BlockSpec(memory_space=pl.ANY)
    shapes = [(seq, 1, width)] * 2 + [(width,)] * 2 + [(cols, width)] * 4 + [(width, hidden)] * 2 + [(hidden, width)]
    return pl.pallas_call(
        functools.partial(tidy_kernel, cols, hidden),
        out_shape=tuple(jax.ShapeDtypeStruct(shape, f32) for shape in shapes),
        in_specs=[anywhere, anywhere, vmem, vmem, anywhere],
        out_specs=[anywhere, anywhere, vmem, vmem] + [anywhere] * 7,
        scratch_shapes=[pltpu.VMEM((width, width), fin.dtype)] * 3
        + [
            pltpu.VMEM((4, width, width), f32),
            pltpu.VMEM((2, seq, 1, width), f32),
            pltpu.SemaphoreType.DMA((14,)),
        ],
        compiler_params=pltpu.CompilerParams(vmem_limit_bytes=60 * 2**20),
    )(out, dx, ga, gm, fin)


def per_device(mp, dp, tokens, lengths, gain1, gain2, wq, wk, wv, wo, wg, wu, wd, cotangent):
    _, seq, width = tokens.shape
    weights = (wq.T, wk.T, wv.T, wo, wg, wu, wd)
    out, dx, gain_a, gain_m, fin = layer(mp, lengths, tokens, cotangent, gain1, gain2, weights)
    if dp > 8:
        groups = [[8 * i + j for i in range(dp // 8)] for j in range(8)]
        fin, gain_a, gain_m = lax.psum((fin.astype(f32), gain_a, gain_m), "dp", axis_index_groups=groups)
    cols, hidden = wq.shape[1], wg.shape[1]
    fin = fin.reshape(3, width, width)
    out, dx, gain_a, gain_m, gq, gk, gv, go, gg, gu, gd = tidy(cols, hidden, out, dx, gain_a, gain_m, fin)
    items = (1, seq, width)
    return out.reshape(items), dx.reshape(items), gain_a, gain_m, gq.T, gk.T, gv.T, go, gg, gu, gd


def solution(mesh):
    rows, cols, items = P("mp", None), P(None, "mp"), P(("dp", "mp"), None, None)
    return jax.shard_map(
        functools.partial(per_device, mesh.shape["mp"], mesh.shape["dp"]),
        mesh=mesh,
        in_specs=(items, P("dp"), P(), P(), cols, cols, cols, rows, cols, cols, rows, items),
        out_specs=(items, items, P(), P(), cols, cols, cols, rows, cols, cols, rows),
        check_vma=False,
    )
```

```python
import functools

import jax
import jax.numpy as jnp
import numpy as np
from jax import lax
from jax.experimental import pallas as pl
from jax.experimental.pallas import tpu as pltpu
from jax.sharding import PartitionSpec as P

HEAD = 64
EPS = 1e-05
NEG = -1e30
MESH = pl.DeviceIdType.MESH
f32, bf16 = jnp.float32, jnp.bfloat16
LOOPED = ("A", "F", "B")
SLOTS = (3, 6, 8, 12)
STEPS = ((3, 3, 3), (2, 3, 3), (3, 3, 2))

PLAN = {
    ("P", 0, 0): (("s", 0),),
    ("A", 0, 1): (("s", 1),),
    ("A", 0, 2): (("a", 1, 0, 0), ("a", 1, 1, 0),),
    ("A", 0, 3): (("a", 1, 2, 0),),
    ("A", 1, 0): (("a", 1, 0, 1), ("a", 1, 1, 1), ("a", 2, 0, 0), ("a", 1, 2, 1), ("a", 2, 1, 0), ("a", 2, 2, 0), ("a", 2, 0, 1), ("a", 1, 0, 2), ("a", 3, 0, 0), ("a", 1, 1, 2), ("a", 1, 0, 3), ("a", 2, 1, 1), ("a", 1, 2, 2), ("a", 1, 1, 3), ("a", 3, 1, 0), ("a", 2, 2, 1), ("a", 1, 2, 3),),
    ("A", 1, 1): (("a", 2, 0, 2), ("a", 3, 0, 1), ("a", 3, 2, 0), ("a", 2, 1, 2),),
    ("A", 1, 2): (("a", 2, 0, 3), ("a", 2, 1, 3), ("a", 2, 2, 2), ("a", 3, 1, 1),),
    ("A", 1, 3): (("a", 2, 2, 3), ("a", 3, 2, 1), ("a", 3, 0, 2), ("g", 1, 1, 0),),
    ("A", 2, 0): (("a", 3, 0, 3), ("a", 3, 1, 2), ("s", 2),),
    ("A", 2, 1): (("a", 3, 1, 3), ("g", 1, 2, 0), ("a", 3, 2, 2),),
    ("A", 2, 2): (("a", 3, 2, 3),),
    ("A", 2, 3): (("g", 1, 1, 1), ("g", 1, 3, 0), ("g", 1, 2, 1),),
    ("A", 3, 0): (("g", 2, 1, 0), ("g", 1, 1, 2),),
    ("A", 3, 3): (("g", 1, 3, 1),),
    ("F", 0, 0): (("g", 2, 1, 1), ("g", 2, 2, 0), ("g", 1, 2, 2),),
    ("F", 0, 1): (("g", 1, 2, 3),),
    ("F", 0, 2): (("p", 0),),
    ("F", 0, 3): (("g", 1, 3, 2), ("t", 0, 0), ("g", 2, 2, 1), ("g", 1, 3, 3), ("g", 2, 1, 2),),
    ("F", 0, 4): (("p", 1), ("g", 2, 1, 3), ("g", 2, 3, 0),),
    ("F", 1, 0): (("t", 1, 0),),
    ("F", 1, 2): (("p", 2),),
    ("F", 1, 3): (("t", 0, 1), ("t", 2, 0), ("g", 2, 2, 2),),
    ("F", 1, 4): (("p", 3), ("g", 2, 2, 3),),
    ("F", 2, 0): (("t", 3, 0),),
    ("F", 2, 1): (("g", 2, 3, 1), ("t", 1, 1), ("t", 0, 2),),
    ("F", 2, 2): (("p", 4), ("g", 2, 3, 2),),
    ("F", 2, 4): (("p", 5), ("t", 4, 0), ("t", 2, 1),),
    ("F", 3, 0): (("t", 5, 0), ("t", 1, 2), ("t", 3, 1),),
    ("F", 3, 2): (("p", 6),),
    ("F", 3, 4): (("p", 7), ("t", 2, 2), ("t", 6, 0),),
    ("M", 0, 0): (("t", 7, 0), ("t", 3, 2), ("t", 4, 1),),
    ("B", 0, 0): (("t", 5, 1),),
    ("B", 0, 8): (("t", 6, 1), ("t", 4, 2),),
    ("B", 0, 9): (("p", 8), ("t", 5, 2), ("t", 7, 1), ("t", 6, 2), ("t", 8, 0),),
    ("B", 1, 7): (("t", 7, 2),),
    ("B", 1, 8): (("t", 8, 1),),
    ("B", 1, 9): (("p", 9),),
    ("B", 2, 7): (("t", 8, 2), ("t", 9, 0),),
    ("B", 2, 9): (("p", 10), ("f", 1, 0),),
    ("B", 3, 0): (("t", 9, 1), ("t", 10, 0),),
    ("B", 3, 7): (("p", 11), ("f", 1, 1), ("f", 2, 0), ("t", 9, 2), ("t", 11, 0),),
    ("B", 3, 8): (("p", 12), ("t", 10, 1),),
    ("B", 3, 9): (("p", 13), ("t", 12, 0), ("f", 2, 1), ("t", 11, 1), ("t", 13, 0),),
    ("E", 0, 0): (("f", 1, 2), ("t", 10, 2),),
    ("E", 0, 1): (("n", 0), ("f", 1, 3), ("t", 11, 2), ("n", 1), ("t", 12, 1),),
    ("E", 0, 2): (("t", 13, 1), ("f", 2, 2), ("n", 2), ("t", 12, 2), ("f", 3, 0), ("f", 4, 0), ("f", 2, 3), ("t", 13, 2), ("f", 5, 0), ("n", 3),),
    ("E", 0, 3): (("f", 3, 1), ("f", 4, 1),),
    ("E", 0, 4): (("f", 5, 1), ("n", 4),),
    ("E", 0, 7): (("f", 3, 2), ("f", 4, 2), ("f", 5, 2), ("f", 3, 3), ("f", 4, 3), ("f", 5, 3),),
}


def nn(left, right):
    return lax.dot_general(left, right, (((1,), (0,)), ((), ())), preferred_element_type=f32)


def nt(left, right):
    return lax.dot_general(left, right, (((1,), (1,)), ((), ())), preferred_element_type=f32)


def iota(shape, axis):
    return lax.broadcasted_iota(jnp.int32, shape, axis)


def turned(w, low):
    return jnp.where(low, -pltpu.roll(w, 96, 1), pltpu.roll(w, 32, 1))


def swap(w):
    return pltpu.roll(w, 64, 1)


def order_table(count):
    return [sorted(range(count), key=lambda s: s ^ z) for z in range(count)]


def pick(table, row, column):
    found = 0
    for r, values in enumerate(table):
        for c, value in enumerate(values):
            found = found + jnp.where((row == r) & (column == c), value, 0)
    return found


def kernel(
    mp,
    T,
    len_ref,
    x_ref,
    dy_ref,
    g1_ref,
    g2_ref,
    cos_ref,
    sin_ref,
    wq_ref,
    wk_ref,
    wv_ref,
    wo_ref,
    wg_ref,
    wu_ref,
    wd_ref,
    out_ref,
    dx_ref,
    ga_ref,
    gm_ref,
    fin_ref,
    w,
    n1,
    n2,
    n2t,
    dyb,
    q,
    k,
    v,
    kt,
    ctx,
    outs,
    heads_t,
    lse,
    mask,
    hb,
    turned_rows,
    made,
    acc,
    res,
    dn,
    dk_sum,
    dv_sum,
    gbuf,
    r1,
    r2,
    r3,
    r4,
    total,
    gain_in,
    staged,
    own_sem,
    az_send,
    az_recv,
    ag_send,
    ag_recv,
    z_send,
    z_recv,
    g_send,
    g_recv,
    s_send,
    s_recv,
    h_send,
    h_recv,
    fin_sem,
    f_send,
    f_recv,
    gain_send,
    gain_recv,
    out_sem,
    credit,
):
    seq, width = x_ref.shape[1], x_ref.shape[2]
    half, quarter = width // 2, width // 4
    heads = wq_ref.shape[0] // HEAD
    tall = width // heads
    blocks = [(a, min(a + 256, T)) for a in range(0, T, 256)]
    dp_at, z = lax.axis_index("dp"), lax.axis_index("mp")
    core, bit1, bit2 = dp_at % 2, (dp_at // 2) % 2, (dp_at // 4) % 2
    partner = dp_at + 1 - 2 * core
    flip1, flip2 = dp_at + 2 - 4 * bit1, dp_at + 4 - 8 * bit2
    near = jnp.where(core == 0, flip1, flip2)
    far = jnp.where(core == 0, flip2, flip1)
    near_bit = jnp.where(core == 0, bit1, bit2)
    far_bit = jnp.where(core == 0, bit2, bit1)
    table = order_table(mp)
    units_f, units = 2 * mp, 3 * mp

    def at(start, size):
        return pl.ds(pl.multiple_of(start, 16), size)

    def spans(start, size):
        half_at = start + core * (size // 2)
        quarter_at = half_at + far_bit * (size // 4)
        eighth_at = quarter_at + near_bit * (size // 8)
        return (near, at(eighth_at, size // 8)), (far, at(quarter_at, size // 4)), (partner, at(half_at, size // 2))

    widening = spans(0, width)
    by_head = [spans(h * tall, tall) for h in range(heads)]
    brief = ((near, at(core * half + (bit1 + bit2) % 2 * quarter, quarter)), widening[2])
    direct = (widening[2],)

    def remote(src, dst, send, recv, dp_to, z_to):
        return pltpu.make_async_remote_copy(
            src_ref=src,
            dst_ref=dst,
            send_sem=send,
            recv_sem=recv,
            device_id={"dp": dp_to, "mp": z_to},
            device_id_type=MESH,
        )


    def hops(kind, j):
        return (None, direct, brief, widening)[STEPS[kind][j - 1]]

    def along(kind, j, shard, to):
        part = w.at[kind, shard, hops(kind, j)[0][1]]
        return remote(part, part, z_send.at[kind, j], z_recv.at[kind, j], dp_at, to)

    def across(kind, j, shard, stage):
        to, rows = hops(kind, j)[stage]
        part = w.at[kind, shard, rows]
        return remote(part, part, g_send.at[kind, j, stage], g_recv.at[kind, j, stage], to, z)

    def head_along(j, h, shard, to):
        part = w.at[0, shard, by_head[h][0][1]]
        return remote(part, part, az_send.at[j, h], az_recv.at[j, h], dp_at, to)

    def head_across(j, h, shard, stage):
        to, rows = by_head[h][stage]
        part = w.at[0, shard, rows]
        return remote(part, part, ag_send.at[j, h, stage], ag_recv.at[j, h, stage], to, z)

    def send_own(kind):
        for j in range(1, mp):
            if kind == 0:
                for h in range(heads):
                    head_along(j, h, z, pick(table, z, j)).start()
            else:
                along(kind, j, z, pick(table, z, j)).start()

    def gather_head(j, h, stage):
        shard = pick(table, z, j)
        if stage == 0:
            head_along(j, h, shard, shard).wait_recv()
        else:
            head_across(j, h, shard, stage - 1).wait_recv()
        if stage < 3:
            head_across(j, h, shard, stage).start()

    def gather(kind, j, stage):
        shard = pick(table, z, j)
        if stage == 0:
            along(kind, j, shard, shard).wait_recv()
        else:
            across(kind, j, shard, stage - 1).wait_recv()
        if stage < STEPS[kind][j - 1]:
            across(kind, j, shard, stage).start()

    def gather_drain():
        for j in range(1, mp):
            shard = pick(table, z, j)
            for h in range(heads):
                head_along(j, h, z, shard).wait_send()
                for stage in range(3):
                    head_across(j, h, shard, stage).wait_send()
            for kind in (1, 2):
                along(kind, j, z, shard).wait_send()
                for stage in range(STEPS[kind][j - 1]):
                    across(kind, j, shard, stage).wait_send()


    whole = units - 1

    def unit_of(u):
        return min(u, whole)

    def block_of(u):
        return pl.ds(0, heads) if u < whole else pl.ds(u - whole, 1)

    def shard_of(u):
        return pick(table, z, u // 2) if u < units_f else (z + 1 + u - units_f) % mp

    def kind_of(u):
        return 1 + u % 2 if u < units_f else 0

    stores = (gbuf, r1, r2, r3)
    hops_back = (partner, far, near)
    given = (1 - core, 1 - far_bit, 1 - near_bit)
    kept = (core, far_bit, near_bit)

    def give(u, stage):
        size = tall >> (stage + 1)
        unit, block = unit_of(u), block_of(u)
        return remote(
            stores[stage].at[unit % SLOTS[stage], block, at(given[stage] * size, size)],
            stores[stage + 1].at[unit % SLOTS[stage + 1], block],
            s_send.at[u, stage],
            s_recv.at[u, stage],
            hops_back[stage],
            z,
        )

    def start_give(u, stage):
        if unit_of(u) >= SLOTS[stage + 1] and u <= whole:
            pl.semaphore_wait(credit.at[stage], 1)
        give(u, stage).start()

    def release(u, stage):
        if unit_of(u) + SLOTS[stage + 1] < units:
            pl.semaphore_signal(
                credit.at[stage], inc=1, device_id={"dp": hops_back[stage], "mp": z}, device_id_type=MESH
            )

    def take(u, stage):
        copy = give(u, stage)
        copy.wait_recv()
        copy.wait_send()
        mine, came = stores[stage], stores[stage + 1]
        here, there = unit_of(u) % SLOTS[stage], unit_of(u) % SLOTS[stage + 1]
        size = tall >> (stage + 1)

        def add(block, carry):
            sums = mine[here, block, at(kept[stage] * size, size), :].astype(f32) + came[there, block].astype(f32)
            came[there, block] = sums.astype(bf16)
            return carry

        if u < whole:
            lax.fori_loop(0, heads, add, 0)
        else:
            add(u - whole, 0)
        if stage > 0:
            release(u, stage - 1)
        if stage < 2:
            start_give(u, stage + 1)
        elif own_shard(u):
            r4[kind_of(u), z, block_of(u)] = r3[there, block_of(u)]
        else:
            home(u).start()

    def own_shard(u):
        return u < 2 or u >= whole

    def home(u):
        kind = kind_of(u)
        return remote(r3.at[u % SLOTS[3]], r4.at[kind, z], h_send.at[u], h_recv.at[kind, z], dp_at, shard_of(u))

    def home_drain():
        for u in range(2, whole):
            home(u).wait_send()


    def sum_block(which):
        return (which, pl.ds(0, heads)) if which < 3 else (0, pl.ds(which - 3, 1))

    tall_spans = spans(0, tall)

    def fin_own(which):
        kind, block = sum_block(which)
        return pltpu.make_async_copy(
            total.at[kind, block], fin_ref.at[kind, block, tall_spans[0][1]], fin_sem.at[which]
        )

    def fin_across(which, stage):
        kind, block = sum_block(which)
        to, rows = tall_spans[stage]
        dst = fin_ref.at[kind, block, rows]
        src = total.at[kind, block] if stage == 0 else dst
        return remote(src, dst, f_send.at[which, stage], f_recv.at[which, stage], to, z)

    def finish(which, stage):
        kind, block = sum_block(which)
        if stage == 0:
            if which <= 3:
                for src in range(mp):

                    @pl.when(z != src)
                    def _(src=src):
                        remote(r3.at[0], r4.at[kind, src], h_send.at[0], h_recv.at[kind, src], dp_at, src).wait_recv()

            sums = r4[kind, 0, block].astype(f32)
            for src in range(1, mp):
                sums = sums + r4[kind, src, block].astype(f32)
            total[kind, block] = sums.astype(bf16)
            fin_own(which).start()
        else:
            if stage == 1:
                fin_own(which).wait()
            fin_across(which, stage - 1).wait_recv()
        if stage < 3:
            fin_across(which, stage).start()

    def finish_drain(which):
        for stage in range(3):
            fin_across(which, stage).wait_send()


    def gain_copy(stage):
        to = (partner, far, near)[stage]
        return remote(gain_in.at[0], gain_in.at[1 + stage], gain_send.at[stage], gain_recv.at[stage], to, z)

    def gain_along(i):
        return remote(
            gain_in.at[0], gain_in.at[3 + i], gain_send.at[2 + i], gain_recv.at[2 + i], dp_at, (z + i) % mp
        )

    def gain_step(stage):
        if stage in (1, 2, 3):
            gain_copy(stage - 1).wait()
            gain_in[0] = gain_in[0] + gain_in[stage]
        if stage < 3:
            gain_copy(stage).start()
        elif stage == 3:
            for i in range(1, mp):
                gain_along(i).start()
        else:
            for i in range(1, mp):
                gain_along(i).wait()
            sums = gain_in[0]
            for i in range(1, mp):
                sums = sums + gain_in[3 + i]
            ga_ref[...] = sums[0]
            gm_ref[...] = sums[1]

    move = {"p": lambda u: start_give(u, 0), "s": send_own, "a": gather_head, "g": gather, "t": take, "f": finish, "n": gain_step}

    def place(part, step, i):
        def run(acts):
            for name, *what in acts:
                move[name](*what)

        if isinstance(step, int):
            run(PLAN.get((part, step, i), ()))
            return
        for at_step in range(mp):
            acts = PLAN.get((part, at_step, i))
            if acts is not None:
                pl.when(step == at_step)(functools.partial(run, acts))

    def run_steps(part, body):
        if part in LOOPED:

            def again(step, carry):
                body(step)
                return carry

            lax.fori_loop(0, mp, again, 0)
        else:
            for step in range(mp):
                body(step)


    barrier = pltpu.get_barrier_semaphore()
    for to in (partner, near, far):
        pl.semaphore_signal(barrier, inc=1, device_id={"dp": to, "mp": z}, device_id_type=MESH)
    for i in range(1, mp):
        pl.semaphore_signal(
            barrier, inc=1, device_id={"dp": dp_at, "mp": (z + i) % mp}, device_id_type=MESH
        )
    hidden = wg_ref.shape[1]
    first = width - hidden
    rest = hidden - first
    pieces = [
        (ref.at[pl.ds(HEAD * h, HEAD)], w.at[0, z, pl.ds(tall * h + HEAD * i, HEAD)])
        for h in range(heads)
        for i, ref in enumerate((wq_ref, wk_ref, wv_ref, wo_ref))
    ]
    pieces += [
        (wg_ref, w.at[1, z, :, pl.ds(0, hidden)]),
        (wu_ref.at[:, pl.ds(0, first)], w.at[1, z, :, pl.ds(hidden, first)]),
        (wd_ref, w.at[2, z, pl.ds(0, hidden)]),
    ]
    stripes = width // rest
    stripe = width // stripes
    pieces += [
        (wu_ref.at[pl.ds(j * stripe, stripe), pl.ds(first, rest)], w.at[2, z, pl.ds(hidden, stripe), pl.ds(j * rest, rest)])
        for j in range(stripes)
    ]
    own = [pltpu.make_async_copy(src, dst, own_sem.at[i]) for i, (src, dst) in enumerate(pieces)]
    for copy in own:
        copy.start()

    lane = iota((T, 128), 1)
    lower = lane < 64
    low = (lane % 64) < 32
    length = len_ref[z]
    full = seq // 16 * 16

    def padded(ref):
        tail = jnp.broadcast_to(ref[0, full:seq, :].astype(f32), (T - full, width))
        tail = jnp.where(iota((T - full, width), 0) < seq - full, tail, 0.0).astype(bf16)
        return jnp.concatenate([ref[0, 0:full, :], tail], axis=0)

    def scale_of(rows_in):
        return lax.rsqrt(jnp.mean(rows_in * rows_in, axis=-1, keepdims=True) + EPS)

    def gain(ref):
        return ref[...].reshape(1, width)

    x = padded(x_ref).astype(f32)
    n1[...] = (x * scale_of(x) * gain(g1_ref)).astype(bf16)
    for copy in own[: 4 * heads]:
        copy.wait()
    pl.semaphore_wait(barrier, 3 + mp - 1)
    place("P", 0, 0)
    for copy in own[4 * heads :]:
        copy.wait()

    acc[...] = x
    dyb[...] = jnp.where(iota((T, width), 0) < length, padded(dy_ref).astype(f32), 0.0).astype(bf16)
    key_at, query_at = iota((T, T), 0), iota((T, T), 1)
    mask[...] = jnp.where((key_at <= query_at) & (key_at < length), 0.0, NEG)
    heads_t[...] = jnp.zeros_like(heads_t)
    ctx[:, heads * HEAD :, :] = jnp.zeros((mp, 256 - heads * HEAD, T), bf16)
    outs[...] = jnp.zeros_like(outs)


    def out_rows(s):
        for h in range(heads):
            outs[HEAD * h : HEAD * h + HEAD, :] = w[0, s, tall * h + 3 * HEAD : tall * h + 4 * HEAD, :]

    def attention(step):
        s = pick(table, z, step)
        cos, sin = cos_ref[...], sin_ref[...]
        for h in range(heads):
            place("A", step, h)
            qkv = nt(n1[...], w[0, s, tall * h : tall * h + tall, :])
            qk, vo = qkv[:, 0:128], qkv[:, 128:256]
            qk = qk * cos + turned(qk, low) * sin
            qh = jnp.where(lower, qk * 0.125, 0.0).astype(bf16)
            kh = jnp.where(lower, swap(qk), 0.0).astype(bf16)
            vh = jnp.where(lower, vo, 0.0).astype(bf16)
            q[s, h], k[s, h], v[s, h] = qh, kh, vh
            kt[s, h] = kh.T[0:HEAD]
            vt = vh.T[0:HEAD]
            for a, b in blocks:
                scores = nt(kh[0:b], qh[a:b]) + mask[0:b, a:b]
                peak = jnp.max(scores, axis=0, keepdims=True)
                e = jnp.exp(scores - peak)
                norm = jnp.sum(e, axis=0, keepdims=True)
                c = nn(vt[:, 0:b], e.astype(bf16))
                ctx[s, HEAD * h : HEAD * h + HEAD, a:b] = (c * (1.0 / norm)).astype(bf16)
                lse[s, h : h + 1, a:b] = peak + jnp.log(norm)
        place("A", step, heads)
        out_rows(s)
        acc[...] += nn(ctx[s].T, outs[...])

    run_steps("A", attention)

    x1 = acc[...]
    res[...] = x1
    normed = (x1 * scale_of(x1) * gain(g2_ref)).astype(bf16)
    n2[...] = normed
    n2t[...] = normed.T
    dn[...] = jnp.zeros_like(dn)


    def feed(step):
        place("F", step, 0)
        s = pick(table, z, step)
        w1, w2 = w.at[1, s], w.at[2, s]
        u0, u1 = 2 * step, 2 * step + 1
        gu = nn(n2[...], w1[...])
        late = nn(n2[:, 0:256], w2[512:768, 0:256])
        for j in range(1, 3):
            late = late + nn(n2[:, 256 * j : 256 * j + 256], w2[512:768, 256 * j : 256 * j + 256])
        dh = nt(dyb[...], w2[0:512, :])
        for i in range(2):
            part = slice(256 * i, 256 * i + 256)
            gate = gu[:, part]
            up = gu[:, 512:768] if i == 0 else late
            dhid = dh[:, part]
            sigma = 1.0 / (1.0 + jnp.exp(-gate))
            active = gate * sigma
            hb[step, :, part] = (active * up).astype(bf16)
            made[:, part] = (dhid * up * sigma * (1.0 + gate * (1.0 - sigma))).astype(bf16)
            made[:, 512 + 256 * i : 768 + 256 * i] = (dhid * active).astype(bf16)
        place("F", step, 1)
        gbuf[u0 % SLOTS[0]] = nn(n2t[...], made[:, 0:768]).astype(bf16).reshape(heads, tall, width)
        place("F", step, 2)
        turned_rows[0:512, :] = hb[step].T
        dn[...] += nt(made[:, 0:768], w1[...])
        place("F", step, 3)
        gbuf[u1 % SLOTS[0], 0:2] = nn(turned_rows[0:512, :], dyb[...]).astype(bf16).reshape(2, tall, width)
        for j in range(3):
            part = slice(256 * j, 256 * j + 256)
            gbuf[u1 % SLOTS[0], 2, :, part] = nn(n2t[part, :], made[:, 768:1024]).astype(bf16)
        place("F", step, 4)
        for j in range(3):
            part = slice(256 * j, 256 * j + 256)
            dn[:, part] += nt(made[:, 768:1024], w2[512:768, part])

    run_steps("F", feed)

    place("M", 0, 0)
    x1 = res[...]
    scale = scale_of(x1)
    hat = x1 * scale
    d2 = dn[...]
    gain_in[0] = jnp.zeros_like(gain_in[0])
    gain_in[0, 1:2, :] = jnp.sum(d2 * hat, axis=0, keepdims=True)
    e = d2 * gain(g2_ref)
    dx1 = dyb[...].astype(f32) + scale * (e - hat * jnp.mean(e * hat, axis=-1, keepdims=True))
    res[...] = dx1
    n2[...] = dx1.astype(bf16)
    dn[...] = jnp.zeros_like(dn)


    def back(step):
        slot = (units_f + step) % SLOTS[0]
        cos, sin = cos_ref[...], sin_ref[...]
        s = (z + 1 + step) % mp
        out_rows(s)
        place("B", step, 0)
        dc = nt(n2[...], outs[...])
        dc = [jnp.where(lower, t, 0.0).astype(bf16) for t in (dc[:, 0:128], swap(dc[:, 0:128]), dc[:, 128:256])]
        of_out = nn(ctx[s, 0 : heads * HEAD, :], n2[...]).astype(bf16)
        for h in range(heads):
            gbuf[slot, h, 3 * HEAD : 4 * HEAD, :] = of_out[HEAD * h : HEAD * h + HEAD]
        for h in range(heads):
            place("B", step, 1 + 2 * h)
            qh, dch = q[s, h], dc[h]
            dk_sum[...] = jnp.zeros_like(dk_sum)
            dv_sum[...] = jnp.zeros_like(dv_sum)
            for a, b in blocks:
                scores = nt(k[s, h, 0:b, :], qh[a:b]) + mask[0:b, a:b]
                p = jnp.exp(scores - lse[s, h : h + 1, a:b])
                dprob = nt(v[s, h, 0:b, :], dch[a:b])
                delta = jnp.sum(p * dprob, axis=0, keepdims=True)
                ds = (p * (dprob - delta)).astype(bf16)
                dv_sum[0:b, :] += nn(p.astype(bf16), dch[a:b])
                dk_sum[0:b, :] += nn(ds, qh[a:b])
                heads_t[0:HEAD, a:b] = nn(kt[s, h, :, 0:b], ds)
            d = heads_t[...].T * 0.125 + swap(dk_sum[...])
            made[:, 0:128] = (d * cos - turned(d, low) * sin).astype(bf16)
            made[:, 128:256] = dv_sum[...].astype(bf16)
            turned_rows[0:256, :] = made[:, 0:256].T
            place("B", step, 2 + 2 * h)
            gbuf[slot, h, 0 : 3 * HEAD, :] = nn(turned_rows[0 : 3 * HEAD, :], n1[...]).astype(bf16)
            place("B", step, 7 + h)
            dn[...] += nn(made[:, 0:256], w[0, s, tall * h : tall * h + tall, :])

    run_steps("B", back)


    place("E", 0, 0)
    x = padded(x_ref).astype(f32)
    scale = scale_of(x)
    hat = x * scale
    d1 = dn[...]
    gain_in[0, 0:1, :] = jnp.sum(d1 * hat, axis=0, keepdims=True)
    place("E", 0, 1)
    e = d1 * gain(g1_ref)
    dx = res[...] + scale * (e - hat * jnp.mean(e * hat, axis=-1, keepdims=True))
    staged[:, 0, :] = dx[0:seq]
    out_dx = pltpu.make_async_copy(staged, dx_ref, out_sem.at[0])
    out_dx.start()
    place("E", 0, 2)
    for j in range(mp):
        acc[...] += nn(hb[j], w[2, pick(table, z, j), 0:512, :])
        place("E", 0, 3 + j)
    out_dx.wait()
    staged[:, 0, :] = acc[0:seq, :]
    out_y = pltpu.make_async_copy(staged, out_ref, out_sem.at[1])
    out_y.start()
    place("E", 0, 3 + mp)
    gather_drain()
    home_drain()
    for which in range(1, 3 + heads):
        finish_drain(which)
    out_y.wait()


def rotary(rows):
    position = np.arange(rows).astype(np.float32)
    index = np.arange(HEAD // 2).astype(np.float32)
    freq = (np.float32(10000.0) ** (np.float32(-2.0) * index / np.float32(HEAD))).astype(np.float32)
    angle = position[:, None] * freq[None, :]
    angle = np.concatenate([angle] * 4, axis=-1)
    return np.cos(angle).astype(np.float32), np.sin(angle).astype(np.float32)


def layer(mp, lengths, tokens, cotangent, gain1, gain2, weights):
    _, seq, width = tokens.shape
    T = (seq + 15) // 16 * 16
    cosine, sine = rotary(T)
    vmem, anywhere = pl.BlockSpec(memory_space=pltpu.VMEM), pl.BlockSpec(memory_space=pl.ANY)
    V, DMA = pltpu.VMEM, pltpu.SemaphoreType.DMA
    heads = weights[0].shape[0] // HEAD
    tall = width // heads
    scratch = [
        V((3, mp, width, width), bf16),
        V((T, width), bf16),
        V((T, width), bf16),
        V((width, T), bf16),
        V((T, width), bf16),
        V((mp, heads, T, 128), bf16),
        V((mp, heads, T, 128), bf16),
        V((mp, heads, T, 128), bf16),
        V((mp, heads, HEAD, T), bf16),
        V((mp, 256, T), bf16),
        V((256, width), bf16),
        V((128, T), f32),
        V((mp, 8, T), f32),
        V((T, T), f32),
        V((mp, T, 512), bf16),
        V((512, T), bf16),
        V((T, 1024), bf16),
        V((T, width), f32),
        V((T, width), f32),
        V((T, width), f32),
        V((T, 128), f32),
        V((T, 128), f32),
        V((SLOTS[0], heads, tall, width), bf16),
        V((SLOTS[1], heads, tall // 2, width), bf16),
        V((SLOTS[2], heads, tall // 4, width), bf16),
        V((SLOTS[3], heads, tall // 8, width), bf16),
        V((3, mp, heads, tall // 8, width), bf16),
        V((3, heads, tall // 8, width), bf16),
        V((3 + mp, 8, width), f32),
        V((seq, 1, width), f32),
        DMA((4 * heads + 6,)),
        DMA((mp, heads)),
        DMA((mp, heads)),
        DMA((mp, heads, 3)),
        DMA((mp, heads, 3)),
        DMA((3, mp)),
        DMA((3, mp)),
        DMA((3, mp, 3)),
        DMA((3, mp, 3)),
        DMA((3 * mp - 1 + heads, 3)),
        DMA((3 * mp - 1 + heads, 3)),
        DMA((3 * mp - 1,)),
        DMA((3, mp)),
        DMA((3 + heads,)),
        DMA((3 + heads, 3)),
        DMA((3 + heads, 3)),
        DMA((2 + mp,)),
        DMA((2 + mp,)),
        DMA((2,)),
        pltpu.SemaphoreType.REGULAR((3,)),
    ]
    return pl.pallas_call(
        functools.partial(kernel, mp, T),
        out_shape=(
            jax.ShapeDtypeStruct((seq, 1, width), f32),
            jax.ShapeDtypeStruct((seq, 1, width), f32),
            jax.ShapeDtypeStruct((width,), f32),
            jax.ShapeDtypeStruct((width,), f32),
            jax.ShapeDtypeStruct((3, heads, tall, width), bf16),
        ),
        in_specs=[pl.BlockSpec(memory_space=pltpu.SMEM)] + [vmem] * 6 + [anywhere] * 7,
        out_specs=[anywhere, anywhere, vmem, vmem, anywhere],
        scratch_shapes=scratch,
        compiler_params=pltpu.CompilerParams(
            collective_id=0, has_side_effects=True, vmem_limit_bytes=63 * 2**20
        ),
    )(lengths, tokens, cotangent, gain1, gain2, jnp.asarray(cosine), jnp.asarray(sine), *weights)


def tidy_kernel(
    cols, hidden, out_in, dx_in, ga_in, gm_in, fin, out, dx, ga, gm, gq, gk, gv, go, gg, gu, gd, a, b, c, big, row, sems
):
    seq, width = out.shape[0], out.shape[2]
    first = width - hidden
    rest = hidden - first
    come = [pltpu.make_async_copy(src, row.at[i], sems.at[i]) for i, src in enumerate((out_in, dx_in))]
    go_on = [pltpu.make_async_copy(row.at[i], dst, sems.at[2 + i]) for i, dst in enumerate((out, dx))]
    loads = [pltpu.make_async_copy(fin.at[i], t, sems.at[4 + i]) for i, t in enumerate((a, b, c))]
    for copy in (loads[0], *come, *loads[1:]):
        copy.start()
    ga[...] = ga_in[...]
    gm[...] = gm_in[...]
    stores = []

    def store(src, dst):
        copy = pltpu.make_async_copy(src, dst, sems.at[7 + len(stores)])
        copy.start()
        stores.append(copy)

    loads[0].wait()
    heads = cols // HEAD
    for i, dst in enumerate((gq, gk, gv, go)):
        for h in range(heads):
            at_row, from_row = i * cols + h * HEAD, h * (width // heads) + i * HEAD
            big[0, at_row : at_row + HEAD, :] = a[from_row : from_row + HEAD, :].astype(f32)
        store(big.at[0, pl.ds(i * cols, cols)], dst)
    for first_half, second_half in zip(come, go_on):
        first_half.wait()
        second_half.start()
    loads[1].wait()
    big[1, :, 0:hidden] = b[:, 0:hidden].astype(f32)
    store(big.at[1, :, pl.ds(0, hidden)], gg)
    loads[2].wait()
    big[2, 0:hidden, :] = c[0:hidden, :].astype(f32)
    store(big.at[2, pl.ds(0, hidden)], gd)
    big[3, :, 0:first] = b[:, hidden:].astype(f32)
    tall = width - hidden
    for j in range(width // rest):
        big[3, j * tall : j * tall + tall, first:hidden] = c[hidden:, j * rest : j * rest + rest].astype(f32)
    store(big.at[3, :, pl.ds(0, hidden)], gu)
    for copy in (*go_on, *stores):
        copy.wait()


def tidy(cols, hidden, out, dx, ga, gm, fin):
    seq, _, width = out.shape
    vmem, anywhere = pl.BlockSpec(memory_space=pltpu.VMEM), pl.BlockSpec(memory_space=pl.ANY)
    shapes = [(seq, 1, width)] * 2 + [(width,)] * 2 + [(cols, width)] * 4 + [(width, hidden)] * 2 + [(hidden, width)]
    return pl.pallas_call(
        functools.partial(tidy_kernel, cols, hidden),
        out_shape=tuple(jax.ShapeDtypeStruct(shape, f32) for shape in shapes),
        in_specs=[anywhere, anywhere, vmem, vmem, anywhere],
        out_specs=[anywhere, anywhere, vmem, vmem] + [anywhere] * 7,
        scratch_shapes=[pltpu.VMEM((width, width), fin.dtype)] * 3
        + [
            pltpu.VMEM((4, width, width), f32),
            pltpu.VMEM((2, seq, 1, width), f32),
            pltpu.SemaphoreType.DMA((14,)),
        ],
        compiler_params=pltpu.CompilerParams(vmem_limit_bytes=60 * 2**20),
    )(out, dx, ga, gm, fin)


def per_device(mp, dp, tokens, lengths, gain1, gain2, wq, wk, wv, wo, wg, wu, wd, cotangent):
    _, seq, width = tokens.shape
    weights = (wq.T, wk.T, wv.T, wo, wg, wu, wd)
    out, dx, gain_a, gain_m, fin = layer(mp, lengths, tokens, cotangent, gain1, gain2, weights)
    if dp > 8:
        groups = [[8 * i + j for i in range(dp // 8)] for j in range(8)]
        fin, gain_a, gain_m = lax.psum((fin.astype(f32), gain_a, gain_m), "dp", axis_index_groups=groups)
    cols, hidden = wq.shape[1], wg.shape[1]
    fin = fin.reshape(3, width, width)
    out, dx, gain_a, gain_m, gq, gk, gv, go, gg, gu, gd = tidy(cols, hidden, out, dx, gain_a, gain_m, fin)
    items = (1, seq, width)
    return out.reshape(items), dx.reshape(items), gain_a, gain_m, gq.T, gk.T, gv.T, go, gg, gu, gd


def solution(mesh):
    rows, cols, items = P("mp", None), P(None, "mp"), P(("dp", "mp"), None, None)
    return jax.shard_map(
        functools.partial(per_device, mesh.shape["mp"], mesh.shape["dp"]),
        mesh=mesh,
        in_specs=(items, P("dp"), P(), P(), cols, cols, cols, rows, cols, cols, rows, items),
        out_specs=(items, items, P(), P(), cols, cols, cols, rows, cols, cols, rows),
        check_vma=False,
    )
```
